256 devices in a mesh: key: 8 (over x, core), hid: 32 (over z, y).
Axes of the slice: x: 4, y: 4, z: 8, core: 2. Of those that a mesh axis runs over, the one named last changes fastest.
Arguments:
- queries: bfloat16 [2048, 6144], P(('key', 'hid')), may hold values from -256 to 256
- cache_keys: bfloat16 [6144, 1024], P('key'), may hold values from -8 to 8
- cache_values: bfloat16 [6144, 1024], P('key'), may hold values from -6 to 6
- response_kv: bfloat16 [2048, 2048], P(('key', 'hid')), may hold values from -7 to 7
- segments: int32 [2048], replicated, may hold values from 0 to 3, never falling along the last dimension, each value on 1 to 1024 neighbouring positions
- residual: bfloat16 [2048, 6144], P(('key', 'hid')), may hold values from -6 to 6
- out_weight: bfloat16 [6144, 6144], P('hid', 'key'), may hold values from -1.5 to 1.5
- norm_gain: float32 [6144], replicated, may hold values from 0.5 to 1.5
- up_weight: bfloat16 [6144, 12288], P(None, 'hid'), may hold values from -0.078125 to 0.078125
- down_weight: bfloat16 [12288, 6144], P('hid'), may hold values from -0.0546875 to 0.0546875
Outputs:
- layer_out: bfloat16 [2048, 6144], P(('key', 'hid'))
The draws below stay inside these ranges and needn't reach their ends.
All inputs are finite; a program needn't handle non-finite values.
Results may differ from the reference program's by a relative error of at most 0.025.
Values may be sent and summed in bfloat16 or wider, within the bound.
A program may use at most 128 MiB of HBM per device.

```python
import math
import jax
import jax.numpy as jnp
import numpy as np
from jax import lax

D = 6144
HEADS = 48
KV_HEADS = 8
HEAD = 128
FF_WIN = 12288
GROUP = 6
ROWS = 2048
CTX = 6144


def base_keys(key):
    return jax.random.truncated_normal(key, -6.0, 6.0, (CTX, KV_HEADS * HEAD), jnp.float32)


def draw_cache_keys(key, part):
    keys = base_keys(key)
    return keys.astype(jnp.bfloat16)


def draw_queries(key, part):
    key = jax.random.fold_in(key, 7)
    values = jax.random.truncated_normal(key, -6.0, 6.0, (ROWS, HEADS * HEAD), jnp.float32)
    return values.astype(jnp.bfloat16)


def levels(key, dims, split, least, high):
    factor_of, own = 1.0, jax.random.fold_in(key, 6)
    for position, shards_of in split:
        steps = jnp.exp(jax.random.uniform(jax.random.fold_in(own, position), (shards_of,), jnp.float32, least / len(split), high / len(split)))
        factor_of = factor_of * jnp.repeat(steps, dims[position] // shards_of).reshape([-1 if axis == position else 1 for axis in range(len(dims))])
    return factor_of


def profile(amount, total, limit, slope):
    loads = [(1 << 20) // math.isqrt(standing ** slope) + 1 for standing in range(2, amount + 1)]
    rest, given = total - limit - (amount - 1), [1] * (amount - 1)
    while rest > 0:
        candidates = [i for i in range(amount - 1) if given[i] < limit]
        whole, budget = sum([loads[i] for i in candidates]), rest
        for i in candidates:
            extra = min(limit - given[i], max(1, budget * loads[i] // whole), rest)
            given[i] = given[i] + extra
            rest = rest - extra
    return np.array([limit] + given)


def ragged_sizes(rng, count, total, most, slope):
    if count == 2:
        one = jax.random.randint(rng, (), max(1, total - most), min(most, total - 1) + 1)
        return jnp.stack([one, total - one])
    tallies = jnp.asarray(profile(count, total, most, slope), jnp.int32)
    twos = (count - 1) // 2
    donor, receiver = tallies[1:1 + 2 * twos:2], tallies[2:2 + 2 * twos:2]
    room = jnp.minimum(donor - 1, most - receiver)
    passed = jax.random.randint(jax.random.fold_in(rng, 1), (twos,), 0, 1 << 20) % (room + 1)
    tallies = tallies.at[1:1 + 2 * twos:2].set(donor - passed).at[2:2 + 2 * twos:2].set(receiver + passed)
    return tallies[jax.random.permutation(jax.random.fold_in(rng, 2), count)]


def normal_values(key, shape, spread, limit, shards=(), kind=jnp.bfloat16):
    values = jax.random.normal(key, shape, jnp.float32) * spread
    if len(shards) > 0:
        values = levels(key, shape, shards, -0.22, 0.18) * values
    return jnp.clip(values, min=-limit, max=limit).astype(kind)


def setup_inputs(seed: int = 0) -> dict:
    key_list = jax.random.split(jax.random.key(seed), 11)
    return {
        "queries": draw_queries(jax.random.fold_in(key_list[10], 71), 0),
        "cache_keys": draw_cache_keys(jax.random.fold_in(key_list[10], 71), 0),
        "cache_values": normal_values(key_list[2], (CTX, KV_HEADS * HEAD), 1.0, 6.0, ((0, 8),)),
        "response_kv": normal_values(key_list[3], (ROWS, 2 * KV_HEADS * HEAD), 1.2, 7.0, ((0, 256),)),
        "segments": jnp.searchsorted(jnp.cumsum(ragged_sizes(key_list[4], 4, ROWS, ROWS // 2, 0)), jnp.arange(ROWS), side="right").astype(jnp.int32),
        "residual": normal_values(key_list[5], (ROWS, D), 1.0, 6.0, ((0, 256),)),
        "out_weight": normal_values(key_list[6], (HEADS * HEAD, D), 0.25, 1.5, ((0, 32), (1, 8))),
        "norm_gain": jnp.clip(1.0 + 0.1 * jax.random.normal(key_list[7], (D,), jnp.float32), 0.5, 1.5),
        "up_weight": normal_values(key_list[8], (D, FF_WIN), D ** -0.5, 0.078125, ((1, 32),)),
        "down_weight": normal_values(key_list[9], (FF_WIN, D), FF_WIN ** -0.5, 0.0546875, ((0, 32),)),
    }


def layer_norm(hidden, gain):
    wide = hidden.astype(jnp.float32)
    mean = lax.optimization_barrier(jnp.mean(wide, axis=-1, keepdims=True))
    centred = wide - mean
    var = lax.optimization_barrier(jnp.mean(centred * centred, axis=-1, keepdims=True))
    return (centred * lax.rsqrt(var + 1e-05) * gain.astype(jnp.float32)).astype(jnp.bfloat16)

def reference(queries, cache_keys, cache_values, response_kv, segments, residual, out_weight, norm_gain, up_weight, down_weight):
    width = KV_HEADS * HEAD
    keys = jnp.concatenate([cache_keys, response_kv[:, :width]], 0).astype(jnp.float32).reshape(-1, KV_HEADS, HEAD)
    values = jnp.concatenate([cache_values, response_kv[:, width:]], 0).astype(jnp.float32).reshape(-1, KV_HEADS, HEAD)
    total = keys.shape[0]
    key_rows = jnp.arange(total, dtype=jnp.int32) - CTX
    key_seg = jnp.concatenate([jnp.full((CTX,), -1, jnp.int32), segments.astype(jnp.int32)])
    block = math.gcd(ROWS, 64)
    blocks = ROWS // block
    q_blocks = queries.reshape(blocks, block, KV_HEADS, GROUP, HEAD)
    starts = jnp.arange(blocks, dtype=jnp.int32) * block
    scale = 1.0 / math.sqrt(HEAD)

    def one(item):
        qblock, start = item
        rows = start + jnp.arange(block, dtype=jnp.int32)
        qseg = lax.dynamic_slice_in_dim(segments.astype(jnp.int32), start, block)
        score = jnp.einsum('bgjd,ngd->bgjn', qblock.astype(jnp.float32), keys) * scale
        seen = (key_rows[None, :] < 0) | (key_seg[None, :] == qseg[:, None]) & (key_rows[None, :] <= rows[:, None])
        score = jnp.where(seen[:, None, None, :], score, -jnp.inf)
        top = lax.optimization_barrier(jnp.max(score, axis=-1, keepdims=True))
        weight = jnp.exp(score - top)
        summed = lax.optimization_barrier(jnp.sum(weight, axis=-1, keepdims=True))
        mixed = jnp.einsum('bgjn,ngd->bgjd', weight, values) / summed
        return mixed.reshape(block, HEADS * HEAD).astype(jnp.bfloat16)
    attn = lax.map(one, (q_blocks, starts)).reshape(ROWS, HEADS * HEAD)
    proj = jnp.dot(attn, out_weight, preferred_element_type=jnp.float32)
    mid = (residual.astype(jnp.float32) + proj).astype(jnp.bfloat16)
    normed = layer_norm(mid, norm_gain)
    up = jnp.dot(normed, up_weight, preferred_element_type=jnp.float32)
    active = jnp.square(jnp.maximum(up, 0.0)).astype(jnp.bfloat16)
    down = jnp.dot(active, down_weight, preferred_element_type=jnp.float32)
    return (mid.astype(jnp.float32) + down).astype(jnp.bfloat16)
```

```python
import functools
import math

import jax
import jax.numpy as jnp
from jax import lax
from jax.experimental import pallas as pl
from jax.experimental.pallas import tpu as pltpu
from jax.sharding import PartitionSpec as P

HEADS = 48
KV_HEADS = 8
HEAD = 128
GROUP = 6
D = 6144
MESH = pl.DeviceIdType.MESH
BF = jnp.bfloat16
F32 = jnp.float32

ZI = {0: 0, 1: 1, -1: 2, 2: 3, -2: 4, 3: 5, -3: 6, 4: 7}
YI = {0: 0, 1: 1, -1: 2, 2: 3}
ZGROUPS = (pl.ds(0, 1), pl.ds(1, 2), pl.ds(3, 2), pl.ds(5, 2), pl.ds(7, 1))

A_COLS = 2560
B_COLS = D - A_COLS
CA, A0, A1 = pl.ds(0, A_COLS), pl.ds(0, A_COLS // 2), pl.ds(A_COLS // 2, A_COLS // 2)
CB = pl.ds(A_COLS, B_COLS)
B0, B1 = pl.ds(A_COLS, B_COLS // 2), pl.ds(A_COLS + B_COLS // 2, B_COLS // 2)
LB, L0, L1 = pl.ds(0, B_COLS), pl.ds(0, B_COLS // 2), pl.ds(B_COLS // 2, B_COLS // 2)
N_GATHER = 40
N_REDUCE = 40


class Copies:
    def __init__(self, send_sems, recv_sems):
        self.sems = send_sems, recv_sems
        self.made = []

    def send(self, src, dst, device):
        i = len(self.made)
        copy = pltpu.make_async_remote_copy(
            src_ref=src,
            dst_ref=dst,
            send_sem=self.sems[0].at[i],
            recv_sem=self.sems[1].at[i],
            device_id=device,
            device_id_type=MESH,
        )
        copy.start()
        self.made.append(copy)
        return copy

    def finish(self):
        for copy in self.made:
            copy.wait_send()


def where_am_i():
    key = lax.axis_index("key")
    hid = lax.axis_index("hid")
    return key // 2, key % 2, hid // 4, hid % 4


def device(x, core, z, y):
    return (lax.rem(x, 4) * 2 + core, lax.rem(z, 8) * 4 + lax.rem(y, 4))


def greet(devices):
    barrier = pltpu.get_barrier_semaphore()
    for one in devices:
        pl.semaphore_signal(barrier, inc=1, device_id=one, device_id_type=MESH)
    pl.semaphore_wait(barrier, len(devices))


def add_into(dst, *srcs):
    total = dst[...].astype(F32)
    for src in srcs:
        total = total + src[...].astype(F32)
    dst[...] = total.astype(BF)


def ffn_kernel(
    mid_ref, gain_ref, up_hbm, down_hbm, out_ref,
    up_w, down_w, rows, part, acc, act,
    a_zp, a_zm, a_yp, a_ym, b_yp, b_ym, b_zp, b_zm,
    w_sem, g_send, g_recv, r_send, r_recv,
):
    x, core, z, y = where_am_i()
    zp, zm = device(x, core, z + 1, y), device(x, core, z + 7, y)
    yp, ym = device(x, core, z, y + 1), device(x, core, z, y + 3)
    load_up = pltpu.make_async_copy(up_hbm, up_w, w_sem.at[0])
    load_down = pltpu.make_async_copy(down_hbm, down_w, w_sem.at[1])
    load_up.start()
    load_down.start()

    wide = mid_ref[...].astype(F32)
    mean = jnp.mean(wide, axis=-1, keepdims=True)
    centred = wide - mean
    var = jnp.mean(centred * centred, axis=-1, keepdims=True)
    rows[0, 0] = (centred * lax.rsqrt(var + 1e-05) * gain_ref[...]).astype(BF)
    greet((zp, zm, yp, ym))

    net = Copies(g_send, g_recv)
    every = pl.ds(0, 4)

    def ring_next(i, ys, cols, half0, half1):
        if i == 0:
            return (
                net.send(rows.at[0, ys, :, cols], rows.at[ZI[-1], ys, :, cols], zp),
                net.send(rows.at[0, ys, :, cols], rows.at[ZI[1], ys, :, cols], zm),
            )
        if i < 3:
            return (
                net.send(rows.at[ZI[-i], ys, :, cols], rows.at[ZI[-i - 1], ys, :, cols], zp),
                net.send(rows.at[ZI[i], ys, :, cols], rows.at[ZI[i + 1], ys, :, cols], zm),
            )
        return (
            net.send(rows.at[ZI[-3], ys, :, half0], rows.at[ZI[4], ys, :, half0], zp),
            net.send(rows.at[ZI[3], ys, :, half1], rows.at[ZI[4], ys, :, half1], zm),
        )

    def arrived(copies):
        for copy in copies:
            copy.wait_recv()

    def y_first(zs, cols):
        return (
            net.send(rows.at[zs, 0, :, cols], rows.at[zs, YI[-1], :, cols], yp),
            net.send(rows.at[zs, 0, :, cols], rows.at[zs, YI[1], :, cols], ym),
        )

    def y_second(zs, half0, half1):
        return (
            net.send(rows.at[zs, YI[-1], :, half0], rows.at[zs, YI[2], :, half0], yp),
            net.send(rows.at[zs, YI[1], :, half1], rows.at[zs, YI[2], :, half1], ym),
        )

    own = pl.ds(0, 1)
    ay = y_first(own, CA)
    bz = ring_next(0, 0, CB, B0, B1)
    by = [y_first(ZGROUPS[0], CB)]
    by2 = []
    arrived(ay)
    ay = y_second(own, A0, A1)
    arrived(bz)
    bz = ring_next(1, 0, CB, B0, B1)
    by.append(y_first(ZGROUPS[1], CB))
    arrived(ay)
    az = ring_next(0, every, CA, A0, A1)
    arrived(by[0])
    by2.append(y_second(ZGROUPS[0], B0, B1))
    arrived(bz)
    bz = ring_next(2, 0, CB, B0, B1)
    by.append(y_first(ZGROUPS[2], CB))
    arrived(by[1])
    by2.append(y_second(ZGROUPS[1], B0, B1))
    arrived(az)
    az = ring_next(1, every, CA, A0, A1)
    arrived(bz)
    bz = ring_next(3, 0, CB, B0, B1)
    by.append(y_first(ZGROUPS[3], CB))
    arrived(by[2])
    by2.append(y_second(ZGROUPS[2], B0, B1))
    arrived(az)
    az = ring_next(2, every, CA, A0, A1)
    arrived(bz)
    by.append(y_first(ZGROUPS[4], CB))
    arrived(by[3])
    by2.append(y_second(ZGROUPS[3], B0, B1))
    arrived(az)
    az = ring_next(3, every, CA, A0, A1)
    arrived(by[4])
    by2.append(y_second(ZGROUPS[4], B0, B1))
    arrived(az)
    for pair in by2:
        arrived(pair)

    load_up.wait()
    acc[...] = jnp.zeros_like(acc)

    def up_step(i, _):
        cols = pl.ds(pl.multiple_of(i * 512, 512), 512)
        block = rows[:, :, :, cols].astype(F32).reshape(256, 512).astype(BF)
        acc[...] += jnp.dot(block, up_w[cols, :], preferred_element_type=F32)
        return 0

    lax.fori_loop(0, D // 512, up_step, 0)
    up = jnp.maximum(acc[...], 0.0)
    act[...] = (up * up).astype(BF)
    load_down.wait()

    def down_step(i, _):
        cols = pl.ds(pl.multiple_of(i * 512, 512), 512)
        block = jnp.dot(act[...], down_w[:, cols], preferred_element_type=F32)
        part[:, :, :, cols] = block.reshape(8, 4, 8, 512).astype(BF)
        return 0

    net.finish()
    net = Copies(r_send, r_recv)

    def z_send(d, ys, cols, half0, half1, lcols, lh0, lh1, got_p, got_m, lys):
        if d == 4:
            return (
                net.send(part.at[ZI[4], ys, :, half1], got_p.at[3, lys, :, lh1], zp),
                net.send(part.at[ZI[4], ys, :, half0], got_m.at[3, lys, :, lh0], zm),
            )
        return (
            net.send(part.at[ZI[d], ys, :, cols], got_p.at[d - 1, lys, :, lcols], zp),
            net.send(part.at[ZI[-d], ys, :, cols], got_m.at[d - 1, lys, :, lcols], zm),
        )

    def z_add(copies, d, ys, cols, half0, half1, lcols, lh0, lh1, got_p, got_m, lys):
        arrived(copies)
        if d == 3:
            add_into(part.at[ZI[3], ys, :, half1], got_p.at[3, lys, :, lh1])
            add_into(part.at[ZI[-3], ys, :, half0], got_m.at[3, lys, :, lh0])
        elif d > 0:
            add_into(part.at[ZI[d], ys, :, cols], got_p.at[d, lys, :, lcols])
            add_into(part.at[ZI[-d], ys, :, cols], got_m.at[d, lys, :, lcols])
        else:
            add_into(
                part.at[0, ys, :, cols], got_p.at[0, lys, :, lcols], got_m.at[0, lys, :, lcols]
            )

    def y_send(step, zs, cols, half0, half1, lcols, lh0, lh1, got_p, got_m):
        if step == 0:
            return (
                net.send(part.at[zs, YI[2], :, half1], got_p.at[1, zs, :, lh1], yp),
                net.send(part.at[zs, YI[2], :, half0], got_m.at[1, zs, :, lh0], ym),
            )
        return (
            net.send(part.at[zs, YI[1], :, cols], got_p.at[0, zs, :, lcols], yp),
            net.send(part.at[zs, YI[-1], :, cols], got_m.at[0, zs, :, lcols], ym),
        )

    def y_add(copies, step, zs, cols, half0, half1, lcols, lh0, lh1, got_p, got_m):
        arrived(copies)
        if step == 0:
            add_into(part.at[zs, YI[1], :, half1], got_p.at[1, zs, :, lh1])
            add_into(part.at[zs, YI[-1], :, half0], got_m.at[1, zs, :, lh0])
        else:
            add_into(part.at[zs, 0, :, cols], got_p.at[0, zs, :, lcols], got_m.at[0, zs, :, lcols])

    za = (every, CA, A0, A1, CA, A0, A1, a_zp, a_zm, every)
    zb = (0, CB, B0, B1, LB, L0, L1, b_zp, b_zm, 0)
    yb = (CB, B0, B1, LB, L0, L1, b_yp, b_ym)
    ya = (CA, A0, A1, CA, A0, A1, a_yp, a_ym)

    lax.fori_loop(A_COLS // 512, D // 512, down_step, 0)
    order = [ZGROUPS[i] for i in (4, 3, 2, 1, 0)]
    by = [y_send(0, g, *yb) for g in order]
    lax.fori_loop(0, A_COLS // 512, down_step, 0)
    az = z_send(4, *za)
    y_add(by[0], 0, order[0], *yb)
    by[0] = y_send(1, order[0], *yb)
    y_add(by[1], 0, order[1], *yb)
    by[1] = y_send(1, order[1], *yb)
    z_add(az, 3, *za)
    az = z_send(3, *za)
    y_add(by[2], 0, order[2], *yb)
    by[2] = y_send(1, order[2], *yb)
    y_add(by[0], 1, order[0], *yb)
    bz = z_send(4, *zb)
    y_add(by[3], 0, order[3], *yb)
    by[3] = y_send(1, order[3], *yb)
    z_add(az, 2, *za)
    az = z_send(2, *za)
    y_add(by[4], 0, order[4], *yb)
    by[4] = y_send(1, order[4], *yb)
    y_add(by[1], 1, order[1], *yb)
    z_add(bz, 3, *zb)
    bz = z_send(3, *zb)
    z_add(az, 1, *za)
    az = z_send(1, *za)
    y_add(by[2], 1, order[2], *yb)
    z_add(bz, 2, *zb)
    bz = z_send(2, *zb)
    y_add(by[3], 1, order[3], *yb)
    z_add(az, 0, *za)
    ay = y_send(0, own, *ya)
    z_add(bz, 1, *zb)
    bz = z_send(1, *zb)
    y_add(ay, 0, own, *ya)
    ay = y_send(1, own, *ya)
    y_add(by[4], 1, order[4], *yb)
    arrived(bz)
    out_ref[:, CB] = (
        mid_ref[:, CB].astype(F32)
        + part[0, 0, :, CB].astype(F32)
        + b_zp[0, 0].astype(F32)
        + b_zm[0, 0].astype(F32)
    ).astype(BF)
    arrived(ay)
    out_ref[:, CA] = (
        mid_ref[:, CA].astype(F32)
        + part[0, 0, :, CA].astype(F32)
        + a_yp[0, 0].astype(F32)
        + a_ym[0, 0].astype(F32)
    ).astype(BF)
    net.finish()


def ffn(mid, gain, up_weight, down_weight):
    vmem = pl.BlockSpec(memory_space=pltpu.VMEM)
    hbm = pl.BlockSpec(memory_space=pl.ANY)
    hidden = up_weight.shape[1]
    return pl.pallas_call(
        ffn_kernel,
        name="ffn",
        out_shape=jax.ShapeDtypeStruct(mid.shape, BF),
        in_specs=[vmem, vmem, hbm, hbm],
        out_specs=vmem,
        scratch_shapes=[
            pltpu.VMEM((D, hidden), BF),
            pltpu.VMEM((hidden, D), BF),
            pltpu.VMEM((8, 4, 8, D), BF),
            pltpu.VMEM((8, 4, 8, D), BF),
            pltpu.VMEM((256, hidden), F32),
            pltpu.VMEM((256, hidden), BF),
            pltpu.VMEM((4, 4, 8, A_COLS), BF),
            pltpu.VMEM((4, 4, 8, A_COLS), BF),
            pltpu.VMEM((2, 1, 8, A_COLS), BF),
            pltpu.VMEM((2, 1, 8, A_COLS), BF),
            pltpu.VMEM((2, 8, 8, B_COLS), BF),
            pltpu.VMEM((2, 8, 8, B_COLS), BF),
            pltpu.VMEM((4, 1, 8, B_COLS), BF),
            pltpu.VMEM((4, 1, 8, B_COLS), BF),
            pltpu.SemaphoreType.DMA((2,)),
            pltpu.SemaphoreType.DMA((N_GATHER,)),
            pltpu.SemaphoreType.DMA((N_GATHER,)),
            pltpu.SemaphoreType.DMA((N_REDUCE,)),
            pltpu.SemaphoreType.DMA((N_REDUCE,)),
        ],
        compiler_params=pltpu.CompilerParams(
            collective_id=0, has_side_effects=True, vmem_limit_bytes=48 * 1024 * 1024
        ),
    )(mid, gain.reshape(1, D), up_weight, down_weight)


def combined_all(part, axis, combine):
    gathered = jax.tree.map(lambda a: lax.all_gather(a, axis), part)

    def take(source):
        return jax.tree.map(lambda a: lax.dynamic_index_in_dim(a, source, 0, False), gathered)

    return lax.fori_loop(
        1, lax.axis_size(axis), lambda source, state: combine(state, take(source)), take(0)
    )


def join(first, second):
    top = jnp.maximum(first[0], second[0])
    left = jnp.exp(first[0] - top)
    right = jnp.exp(second[0] - top)
    return (
        top,
        first[1] * left + second[1] * right,
        first[2] * left[..., None] + second[2] * right[..., None],
    )


def on_device(
    queries,
    cache_keys,
    cache_values,
    response_kv,
    segments,
    residual,
    out_weight,
    norm_gain,
    up_weight,
    down_weight,
):
    n_hid = lax.axis_size("hid")
    key_idx = lax.axis_index("key")
    hid_idx = lax.axis_index("hid")
    tok = queries.shape[0]
    width = cache_keys.shape[1]
    ctx_dev = cache_keys.shape[0]
    q_all, wo_full = (
        lax.all_gather(queries, "key", axis=0, tiled=True),
        lax.all_gather(out_weight, "key", axis=1, tiled=True),
    )
    group_kv = lax.all_gather(response_kv, "hid", axis=0, tiled=True)
    group_rows = group_kv.shape[0]
    keys = jnp.concatenate([cache_keys, group_kv[:, :width]], 0).reshape(-1, KV_HEADS, HEAD)
    values = (
        jnp.concatenate([cache_values, group_kv[:, width:]], 0)
        .astype(jnp.float32)
        .reshape(-1, KV_HEADS, HEAD)
    )
    key_rows = jnp.concatenate(
        [
            jnp.full((ctx_dev,), -1, jnp.int32),
            key_idx * group_rows + jnp.arange(group_rows, dtype=jnp.int32),
        ]
    )
    own_seg = lax.dynamic_slice_in_dim(segments, key_idx * group_rows, group_rows)
    key_seg = jnp.concatenate([jnp.full((ctx_dev,), -1, jnp.int32), own_seg])
    count = q_all.shape[0]
    slot = jnp.arange(count, dtype=jnp.int32)
    q_rows = (slot // tok * n_hid + hid_idx) * tok + slot % tok
    q_seg = jnp.take(segments, q_rows)
    scale = 1.0 / math.sqrt(HEAD)
    grouped = q_all.reshape(count, KV_HEADS, GROUP, HEAD)
    score = jnp.einsum("bgjd,ngd->bgjn", grouped, keys, preferred_element_type=jnp.float32) * scale
    seen = (key_rows[None, :] < 0) | (key_seg[None, :] == q_seg[:, None]) & (
        key_rows[None, :] <= q_rows[:, None]
    )
    score = jnp.where(seen[:, None, None, :], score, -jnp.inf)
    top = jnp.max(score, axis=-1)
    weight = jnp.exp(score - top[..., None])
    summed = jnp.sum(weight, axis=-1)
    mixed = jnp.einsum("bgjn,ngd->bgjd", weight, values)
    top = top.reshape(count, HEADS)
    summed = summed.reshape(count, HEADS)
    mixed = mixed.reshape(count, HEADS, HEAD)
    top_all, sum_all, mix_all = combined_all((top, summed, mixed), "key", join)
    own = (
        lax.dynamic_slice_in_dim(top_all, key_idx * tok, tok, 0),
        lax.dynamic_slice_in_dim(sum_all, key_idx * tok, tok, 0),
        lax.dynamic_slice_in_dim(mix_all, key_idx * tok, tok, 0),
    )
    attn = (own[2] / own[1][..., None]).reshape(tok, HEADS * HEAD).astype(jnp.bfloat16)
    attn_cols = lax.all_to_all(attn, "hid", split_axis=1, concat_axis=0, tiled=True)
    block = attn_cols
    proj = lax.psum_scatter(
        jnp.dot(block, wo_full, preferred_element_type=jnp.float32).astype(jnp.bfloat16),
        "hid",
        scatter_dimension=0,
        tiled=True,
    ).astype(jnp.float32)
    mid = (residual.astype(jnp.float32) + proj).astype(jnp.bfloat16)
    return ffn(mid, norm_gain, up_weight, down_weight)


def solution(mesh):
    return jax.shard_map(
        on_device,
        mesh=mesh,
        in_specs=(
            P(("key", "hid"), None),
            P("key", None),
            P("key", None),
            P(("key", "hid"), None),
            P(),
            P(("key", "hid"), None),
            P("hid", "key"),
            P(),
            P(None, "hid"),
            P("hid", None),
        ),
        out_specs=P(("key", "hid"), None),
        check_vma=False,
    )
```

```python
import functools
import math

import jax
import jax.numpy as jnp
from jax import lax
from jax.experimental import pallas as pl
from jax.experimental.pallas import tpu as pltpu
from jax.sharding import PartitionSpec as P

HEADS = 48
KV_HEADS = 8
HEAD = 128
GROUP = 6
D = 6144
MESH = pl.DeviceIdType.MESH
BF = jnp.bfloat16
F32 = jnp.float32

ZI = {0: 0, 1: 1, -1: 2, 2: 3, -2: 4, 3: 5, -3: 6, 4: 7}
YI = {0: 0, 1: 1, -1: 2, 2: 3}
ZGROUPS = (pl.ds(0, 1), pl.ds(1, 2), pl.ds(3, 2), pl.ds(5, 2), pl.ds(7, 1))

A_COLS = 2560
B_COLS = D - A_COLS
CA, A0, A1 = pl.ds(0, A_COLS), pl.ds(0, A_COLS // 2), pl.ds(A_COLS // 2, A_COLS // 2)
CB = pl.ds(A_COLS, B_COLS)
B0, B1 = pl.ds(A_COLS, B_COLS // 2), pl.ds(A_COLS + B_COLS // 2, B_COLS // 2)
LB, L0, L1 = pl.ds(0, B_COLS), pl.ds(0, B_COLS // 2), pl.ds(B_COLS // 2, B_COLS // 2)
N_GATHER = 40
N_REDUCE = 40


class Copies:
    def __init__(self, send_sems, recv_sems):
        self.sems = send_sems, recv_sems
        self.made = []

    def send(self, src, dst, device):
        i = len(self.made)
        copy = pltpu.make_async_remote_copy(
            src_ref=src,
            dst_ref=dst,
            send_sem=self.sems[0].at[i],
            recv_sem=self.sems[1].at[i],
            device_id=device,
            device_id_type=MESH,
        )
        copy.start()
        self.made.append(copy)
        return copy

    def finish(self):
        for copy in self.made:
            copy.wait_send()


def where_am_i():
    key = lax.axis_index("key")
    hid = lax.axis_index("hid")
    return key // 2, key % 2, hid // 4, hid % 4


def device(x, core, z, y):
    return (lax.rem(x, 4) * 2 + core, lax.rem(z, 8) * 4 + lax.rem(y, 4))


def greet(devices):
    barrier = pltpu.get_barrier_semaphore()
    for one in devices:
        pl.semaphore_signal(barrier, inc=1, device_id=one, device_id_type=MESH)
    pl.semaphore_wait(barrier, len(devices))


def add_into(dst, *srcs):
    total = dst[...].astype(F32)
    for src in srcs:
        total = total + src[...].astype(F32)
    dst[...] = total.astype(BF)


def ffn_kernel(
    mid_ref, gain_ref, up_hbm, down_hbm, out_ref,
    up_w, down_w, rows, part, acc, act,
    a_zp, a_zm, a_yp, a_ym, b_yp, b_ym, b_zp, b_zm,
    w_sem, g_send, g_recv, r_send, r_recv,
):
    x, core, z, y = where_am_i()
    zp, zm = device(x, core, z + 1, y), device(x, core, z + 7, y)
    yp, ym = device(x, core, z, y + 1), device(x, core, z, y + 3)
    load_up = pltpu.make_async_copy(up_hbm, up_w, w_sem.at[0])
    load_down = pltpu.make_async_copy(down_hbm, down_w, w_sem.at[1])
    load_up.start()
    load_down.start()

    wide = mid_ref[...].astype(F32)
    mean = jnp.mean(wide, axis=-1, keepdims=True)
    centred = wide - mean
    var = jnp.mean(centred * centred, axis=-1, keepdims=True)
    rows[0, 0] = (centred * lax.rsqrt(var + 1e-05) * gain_ref[...]).astype(BF)
    greet((zp, zm, yp, ym))

    net = Copies(g_send, g_recv)
    every = pl.ds(0, 4)

    def ring_next(i, ys, cols, half0, half1):
        if i == 0:
            return (
                net.send(rows.at[0, ys, :, cols], rows.at[ZI[-1], ys, :, cols], zp),
                net.send(rows.at[0, ys, :, cols], rows.at[ZI[1], ys, :, cols], zm),
            )
        if i < 3:
            return (
                net.send(rows.at[ZI[-i], ys, :, cols], rows.at[ZI[-i - 1], ys, :, cols], zp),
                net.send(rows.at[ZI[i], ys, :, cols], rows.at[ZI[i + 1], ys, :, cols], zm),
            )
        return (
            net.send(rows.at[ZI[-3], ys, :, half0], rows.at[ZI[4], ys, :, half0], zp),
            net.send(rows.at[ZI[3], ys, :, half1], rows.at[ZI[4], ys, :, half1], zm),
        )

    def arrived(copies):
        for copy in copies:
            copy.wait_recv()

    def y_first(zs, cols):
        return (
            net.send(rows.at[zs, 0, :, cols], rows.at[zs, YI[-1], :, cols], yp),
            net.send(rows.at[zs, 0, :, cols], rows.at[zs, YI[1], :, cols], ym),
        )

    def y_second(zs, half0, half1):
        return (
            net.send(rows.at[zs, YI[-1], :, half0], rows.at[zs, YI[2], :, half0], yp),
            net.send(rows.at[zs, YI[1], :, half1], rows.at[zs, YI[2], :, half1], ym),
        )

    own = pl.ds(0, 1)
    ay = y_first(own, CA)
    bz = ring_next(0, 0, CB, B0, B1)
    by = [y_first(ZGROUPS[0], CB)]
    by2 = []
    arrived(ay)
    ay = y_second(own, A0, A1)
    arrived(bz)
    bz = ring_next(1, 0, CB, B0, B1)
    by.append(y_first(ZGROUPS[1], CB))
    arrived(ay)
    az = ring_next(0, every, CA, A0, A1)
    arrived(by[0])
    by2.append(y_second(ZGROUPS[0], B0, B1))
    arrived(bz)
    bz = ring_next(2, 0, CB, B0, B1)
    by.append(y_first(ZGROUPS[2], CB))
    arrived(by[1])
    by2.append(y_second(ZGROUPS[1], B0, B1))
    arrived(az)
    az = ring_next(1, every, CA, A0, A1)
    arrived(bz)
    bz = ring_next(3, 0, CB, B0, B1)
    by.append(y_first(ZGROUPS[3], CB))
    arrived(by[2])
    by2.append(y_second(ZGROUPS[2], B0, B1))
    arrived(az)
    az = ring_next(2, every, CA, A0, A1)
    arrived(bz)
    by.append(y_first(ZGROUPS[4], CB))
    arrived(by[3])
    by2.append(y_second(ZGROUPS[3], B0, B1))
    arrived(az)
    az = ring_next(3, every, CA, A0, A1)
    arrived(by[4])
    by2.append(y_second(ZGROUPS[4], B0, B1))
    arrived(az)
    for pair in by2:
        arrived(pair)

    load_up.wait()
    acc[...] = jnp.zeros_like(acc)

    def up_step(i, _):
        cols = pl.ds(pl.multiple_of(i * 512, 512), 512)
        block = rows[:, :, :, cols].astype(F32).reshape(256, 512).astype(BF)
        acc[...] += jnp.dot(block, up_w[cols, :], preferred_element_type=F32)
        return 0

    lax.fori_loop(0, D // 512, up_step, 0)
    up = jnp.maximum(acc[...], 0.0)
    act[...] = (up * up).astype(BF)
    load_down.wait()

    def down_step(i, _):
        cols = pl.ds(pl.multiple_of(i * 512, 512), 512)
        block = jnp.dot(act[...], down_w[:, cols], preferred_element_type=F32)
        part[:, :, :, cols] = block.reshape(8, 4, 8, 512).astype(BF)
        return 0

    net.finish()
    net = Copies(r_send, r_recv)

    def z_send(d, ys, cols, half0, half1, lcols, lh0, lh1, got_p, got_m, lys):
        if d == 4:
            return (
                net.send(part.at[ZI[4], ys, :, half1], got_p.at[3, lys, :, lh1], zp),
                net.send(part.at[ZI[4], ys, :, half0], got_m.at[3, lys, :, lh0], zm),
            )
        return (
            net.send(part.at[ZI[d], ys, :, cols], got_p.at[d - 1, lys, :, lcols], zp),
            net.send(part.at[ZI[-d], ys, :, cols], got_m.at[d - 1, lys, :, lcols], zm),
        )

    def z_add(copies, d, ys, cols, half0, half1, lcols, lh0, lh1, got_p, got_m, lys):
        arrived(copies)
        if d == 3:
            add_into(part.at[ZI[3], ys, :, half1], got_p.at[3, lys, :, lh1])
            add_into(part.at[ZI[-3], ys, :, half0], got_m.at[3, lys, :, lh0])
        elif d > 0:
            add_into(part.at[ZI[d], ys, :, cols], got_p.at[d, lys, :, lcols])
            add_into(part.at[ZI[-d], ys, :, cols], got_m.at[d, lys, :, lcols])
        else:
            add_into(
                part.at[0, ys, :, cols], got_p.at[0, lys, :, lcols], got_m.at[0, lys, :, lcols]
            )

    def y_send(step, zs, cols, half0, half1, lcols, lh0, lh1, got_p, got_m):
        if step == 0:
            return (
                net.send(part.at[zs, YI[2], :, half1], got_p.at[1, zs, :, lh1], yp),
                net.send(part.at[zs, YI[2], :, half0], got_m.at[1, zs, :, lh0], ym),
            )
        return (
            net.send(part.at[zs, YI[1], :, cols], got_p.at[0, zs, :, lcols], yp),
            net.send(part.at[zs, YI[-1], :, cols], got_m.at[0, zs, :, lcols], ym),
        )

    def y_add(copies, step, zs, cols, half0, half1, lcols, lh0, lh1, got_p, got_m):
        arrived(copies)
        if step == 0:
            add_into(part.at[zs, YI[1], :, half1], got_p.at[1, zs, :, lh1])
            add_into(part.at[zs, YI[-1], :, half0], got_m.at[1, zs, :, lh0])
        else:
            add_into(part.at[zs, 0, :, cols], got_p.at[0, zs, :, lcols], got_m.at[0, zs, :, lcols])

    za = (every, CA, A0, A1, CA, A0, A1, a_zp, a_zm, every)
    zb = (0, CB, B0, B1, LB, L0, L1, b_zp, b_zm, 0)
    yb = (CB, B0, B1, LB, L0, L1, b_yp, b_ym)
    ya = (CA, A0, A1, CA, A0, A1, a_yp, a_ym)

    lax.fori_loop(A_COLS // 512, D // 512, down_step, 0)
    order = [ZGROUPS[i] for i in (4, 3, 2, 1, 0)]
    by = [y_send(0, g, *yb) for g in order]
    lax.fori_loop(0, A_COLS // 512, down_step, 0)
    az = z_send(4, *za)
    y_add(by[0], 0, order[0], *yb)
    by[0] = y_send(1, order[0], *yb)
    y_add(by[1], 0, order[1], *yb)
    by[1] = y_send(1, order[1], *yb)
    z_add(az, 3, *za)
    az = z_send(3, *za)
    y_add(by[2], 0, order[2], *yb)
    by[2] = y_send(1, order[2], *yb)
    y_add(by[0], 1, order[0], *yb)
    bz = z_send(4, *zb)
    y_add(by[3], 0, order[3], *yb)
    by[3] = y_send(1, order[3], *yb)
    z_add(az, 2, *za)
    az = z_send(2, *za)
    y_add(by[4], 0, order[4], *yb)
    by[4] = y_send(1, order[4], *yb)
    y_add(by[1], 1, order[1], *yb)
    z_add(bz, 3, *zb)
    bz = z_send(3, *zb)
    z_add(az, 1, *za)
    az = z_send(1, *za)
    y_add(by[2], 1, order[2], *yb)
    z_add(bz, 2, *zb)
    bz = z_send(2, *zb)
    y_add(by[3], 1, order[3], *yb)
    z_add(az, 0, *za)
    ay = y_send(0, own, *ya)
    z_add(bz, 1, *zb)
    bz = z_send(1, *zb)
    y_add(ay, 0, own, *ya)
    ay = y_send(1, own, *ya)
    y_add(by[4], 1, order[4], *yb)
    arrived(bz)
    out_ref[:, CB] = (
        mid_ref[:, CB].astype(F32)
        + part[0, 0, :, CB].astype(F32)
        + b_zp[0, 0].astype(F32)
        + b_zm[0, 0].astype(F32)
    ).astype(BF)
    arrived(ay)
    out_ref[:, CA] = (
        mid_ref[:, CA].astype(F32)
        + part[0, 0, :, CA].astype(F32)
        + a_yp[0, 0].astype(F32)
        + a_ym[0, 0].astype(F32)
    ).astype(BF)
    net.finish()


def ffn(mid, gain, up_weight, down_weight):
    vmem = pl.BlockSpec(memory_space=pltpu.VMEM)
    hbm = pl.BlockSpec(memory_space=pl.ANY)
    hidden = up_weight.shape[1]
    return pl.pallas_call(
        ffn_kernel,
        name="ffn",
        out_shape=jax.ShapeDtypeStruct(mid.shape, BF),
        in_specs=[vmem, vmem, hbm, hbm],
        out_specs=vmem,
        scratch_shapes=[
            pltpu.VMEM((D, hidden), BF),
            pltpu.VMEM((hidden, D), BF),
            pltpu.VMEM((8, 4, 8, D), BF),
            pltpu.VMEM((8, 4, 8, D), BF),
            pltpu.VMEM((256, hidden), F32),
            pltpu.VMEM((256, hidden), BF),
            pltpu.VMEM((4, 4, 8, A_COLS), BF),
            pltpu.VMEM((4, 4, 8, A_COLS), BF),
            pltpu.VMEM((2, 1, 8, A_COLS), BF),
            pltpu.VMEM((2, 1, 8, A_COLS), BF),
            pltpu.VMEM((2, 8, 8, B_COLS), BF),
            pltpu.VMEM((2, 8, 8, B_COLS), BF),
            pltpu.VMEM((4, 1, 8, B_COLS), BF),
            pltpu.VMEM((4, 1, 8, B_COLS), BF),
            pltpu.SemaphoreType.DMA((2,)),
            pltpu.SemaphoreType.DMA((N_GATHER,)),
            pltpu.SemaphoreType.DMA((N_GATHER,)),
            pltpu.SemaphoreType.DMA((N_REDUCE,)),
            pltpu.SemaphoreType.DMA((N_REDUCE,)),
        ],
        compiler_params=pltpu.CompilerParams(
            collective_id=0, has_side_effects=True, vmem_limit_bytes=48 * 1024 * 1024
        ),
    )(mid, gain.reshape(1, D), up_weight, down_weight)


LOG2_SCALE = math.log2(math.e) / math.sqrt(HEAD)
Q_COLS = GROUP * HEAD
KEYS_OWN = 768
KEYS_CHIP = 2 * KEYS_OWN
RESP = 512
N_CHIP = 1536


def attend_kernel(
    q_ref, ck_hbm, cv_hbm, rkv_ref, seg_ref, res_ref, wo_hbm, mid_ref,
    packed, got, qall, rkv, kbuf, vbuf, wo, obuf, stat, robuf, rstat, attn, part, zp_buf, zm_buf,
    px, local_sem, s_sem, r_sem,
):
    x, core, z, y = where_am_i()
    sib = device(x, 1 - core, z, y)
    zdev = [device(x, core, z + d, y) for d in range(8)]
    xdev = [device(x + d, core, z, y) for d in range(4)]
    ydev = [device(x, core, z, y + d) for d in range(4)]
    head = pl.ds(pl.multiple_of(z * HEAD, HEAD), HEAD)
    wo_rows = pl.ds(pl.multiple_of(y * 192, 64), 192)
    wo_own = pl.ds(pl.multiple_of(core * 768, 128), 768)

    load_k = pltpu.make_async_copy(ck_hbm.at[:, head], kbuf.at[pl.ds(0, KEYS_OWN)], local_sem.at[0])
    load_v = pltpu.make_async_copy(
        cv_hbm.at[:, head], vbuf.at[pl.ds(0, KEYS_OWN), pl.ds(0, HEAD)], local_sem.at[1]
    )
    load_wo = pltpu.make_async_copy(wo_hbm, wo.at[wo_rows, wo_own], local_sem.at[2])
    load_k.start()
    load_v.start()
    load_wo.start()
    for i in range(8):
        packed[i, :, 0:Q_COLS] = q_ref[:, i * Q_COLS : (i + 1) * Q_COLS]
        packed[i, :, Q_COLS : Q_COLS + HEAD] = rkv_ref[:, i * HEAD : (i + 1) * HEAD]
        packed[i, :, Q_COLS + HEAD :] = rkv_ref[:, 1024 + i * HEAD : 1024 + (i + 1) * HEAD]
    greet([*zdev[1:], *xdev[1:], *ydev[1:], sib])
    net = Copies(s_sem, r_sem)

    def arrived(copies):
        for copy in copies:
            copy.wait_recv()

    moves = [
        net.send(packed.at[lax.rem(z + d, 8)], got.at[8 - d], zdev[d]) for d in (4, 3, 5, 2, 6, 1, 7)
    ]
    caches = [
        net.send(ck_hbm.at[:, head], kbuf.at[pl.ds(KEYS_OWN, KEYS_OWN)], sib),
        net.send(cv_hbm.at[:, head], vbuf.at[pl.ds(KEYS_OWN, KEYS_OWN), pl.ds(0, HEAD)], sib),
    ]
    got[0] = packed[z]
    vbuf[:, HEAD:] = jnp.ones((KEYS_CHIP + RESP, HEAD), BF)
    arrived(moves)
    rkv[0, 0] = got[:, :, Q_COLS:]
    kv_moves = [net.send(rkv.at[0, 0], rkv.at[0, 4 - d], ydev[d]) for d in (2, 1, 3)]
    qall[0] = got[:, :, 0:Q_COLS]
    q_moves = [net.send(qall.at[0], qall.at[4 - d], xdev[d]) for d in (1, 3, 2)]

    seg = seg_ref[...]
    bounds = [
        jnp.sum(jnp.where(seg < s, 1, 0), keepdims=True) for s in (1, 2, 3)
    ]
    lanes = lax.broadcasted_iota(jnp.int32, (1, RESP), 1)
    key_row = (
        (2 * x + ((core + lanes // 256) & 1)) * 32
        + ((z + (lanes // 8)) & 7) * 4
        + ((y + (lanes // 64)) & 3)
    ) * 8 + (lanes & 7)
    slots = lax.broadcasted_iota(jnp.int32, (64, 1), 0)

    arrived(kv_moves)
    kv_sib = net.send(rkv.at[0], rkv.at[1], sib)
    load_wo.wait()
    own_wo = wo.at[wo_rows, wo_own]
    wo_moves = [net.send(own_wo, own_wo, ydev[d]) for d in (1, 3)]
    load_k.wait()
    load_v.wait()
    arrived(caches)
    arrived([kv_sib])
    kbuf[pl.ds(KEYS_CHIP, RESP), :] = rkv[:, :, :, :, 0:HEAD].astype(F32).reshape(RESP, HEAD).astype(BF)
    vbuf[pl.ds(KEYS_CHIP, RESP), 0:HEAD] = (
        rkv[:, :, :, :, HEAD:].astype(F32).reshape(RESP, HEAD).astype(BF)
    )

    def attend(i):
        wide = qall[i].astype(F32)
        q = jnp.concatenate(
            [wide[:, :, j * HEAD : (j + 1) * HEAD].reshape(64, HEAD) for j in range(GROUP)], 0
        ).astype(BF)
        q_row = ((2 * ((x + i) & 3) + core) * 32 + ((z + slots // 8) & 7) * 4 + y) * 8 + (slots & 7)
        start = jnp.zeros_like(q_row)
        for bound in bounds:
            start = jnp.maximum(start, jnp.where(q_row >= bound, bound, 0))
        seen = (key_row <= q_row) & (key_row >= start)
        seen = jnp.concatenate([jnp.where(seen, 0.0, -jnp.inf)] * GROUP, 0)
        nt = (((1,), (1,)), ((), ()))
        s1 = lax.dot_general(q, kbuf[0:KEYS_CHIP, :], nt, preferred_element_type=F32)
        s2 = lax.dot_general(q, kbuf[KEYS_CHIP:, :], nt, preferred_element_type=F32) + seen
        top = jnp.maximum(
            jnp.max(s1, axis=-1, keepdims=True), jnp.max(s2, axis=-1, keepdims=True)
        )
        p1 = jnp.exp2((s1 - top) * LOG2_SCALE).astype(BF)
        p2 = jnp.exp2((s2 - top) * LOG2_SCALE).astype(BF)
        mixed = jnp.dot(p1, vbuf[0:KEYS_CHIP, :], preferred_element_type=F32) + jnp.dot(
            p2, vbuf[KEYS_CHIP:, :], preferred_element_type=F32
        )
        lane = lax.broadcasted_iota(jnp.int32, (64, HEAD), 1)
        tops = jnp.zeros((64, HEAD), F32)
        totals = jnp.ones((64, HEAD), F32)
        for j in range(GROUP):
            rows = slice(j * 64, (j + 1) * 64)
            obuf[i, :, :, j * HEAD : (j + 1) * HEAD] = mixed[rows, 0:HEAD].reshape(8, 8, HEAD).astype(BF)
            tops = jnp.where(lane == j, top[rows], tops)
            totals = jnp.where(lane == j, mixed[rows, HEAD:], totals)
        stat[i, 0] = tops
        stat[i, 1] = totals

    o_moves = []

    def give(d):
        attend(d)
        o_moves.append(net.send(obuf.at[d], robuf.at[4 - d], xdev[d]))
        o_moves.append(net.send(stat.at[d], rstat.at[4 - d], xdev[d]))

    arrived([q_moves[2]])
    give(2)
    arrived([q_moves[0]])
    give(3)
    arrived(wo_moves)
    back, ahead = lax.rem(y + 3, 4), lax.rem(y + 1, 4)
    low = wo.at[pl.ds(pl.multiple_of(back * 192, 64), 96), wo_own]
    high = wo.at[pl.ds(pl.multiple_of(ahead * 192 + 96, 32), 96), wo_own]
    wo_moves = [net.send(low, low, ydev[1]), net.send(high, high, ydev[3])]
    arrived([q_moves[1]])
    give(1)
    attend(0)
    arrived(wo_moves)
    wo_cols = wo.at[:, wo_own]
    wo_sib = net.send(wo_cols, wo_cols, sib)
    arrived(o_moves)

    tops = [stat[0, 0]] + [rstat[i, 0] for i in range(1, 4)]
    totals = [stat[0, 1]] + [rstat[i, 1] for i in range(1, 4)]
    top = functools.reduce(jnp.maximum, tops)
    scales = [jnp.exp2((t - top) * LOG2_SCALE) for t in tops]
    total = functools.reduce(jnp.add, [a * b for a, b in zip(scales, totals)])
    scales = [a / total for a in scales]
    for j in range(GROUP):
        cols = slice(j * HEAD, (j + 1) * HEAD)
        mixed = obuf[0, :, :, cols].astype(F32).reshape(64, HEAD) * scales[0][:, j : j + 1]
        for i in range(1, 4):
            mixed = mixed + robuf[i, :, :, cols].astype(F32).reshape(64, HEAD) * scales[i][:, j : j + 1]
        attn[0, :, :, cols] = mixed.reshape(8, 8, HEAD).astype(BF)
    a_moves = [net.send(attn.at[0], attn.at[4 - d], xdev[d]) for d in (2, 1, 3)]
    arrived([wo_sib])
    arrived(a_moves)

    lhs = attn[...].astype(F32).reshape(256, Q_COLS).astype(BF)
    ring = [[], []]

    def z_cols(p):
        base = p * 768
        return pl.ds(base, 768), pl.ds(base, 384), pl.ds(base + 384, 384)

    def z_send(p, d):
        cols, half0, half1 = z_cols(p)
        if d == 4:
            ring[p] = [
                net.send(part.at[4, :, :, half1], zp_buf.at[3, :, :, half1], zdev[1]),
                net.send(part.at[4, :, :, half0], zm_buf.at[3, :, :, half0], zdev[7]),
            ]
        else:
            ring[p] = [
                net.send(part.at[d, :, :, cols], zp_buf.at[d - 1, :, :, cols], zdev[1]),
                net.send(part.at[8 - d, :, :, cols], zm_buf.at[d - 1, :, :, cols], zdev[7]),
            ]

    def z_add(p, d):
        cols, half0, half1 = z_cols(p)
        arrived(ring[p])
        if d == 3:
            add_into(part.at[3, :, :, half1], zp_buf.at[3, :, :, half1])
            add_into(part.at[5, :, :, half0], zm_buf.at[3, :, :, half0])
        elif d > 0:
            add_into(part.at[d, :, :, cols], zp_buf.at[d, :, :, cols])
            add_into(part.at[8 - d, :, :, cols], zm_buf.at[d, :, :, cols])
        else:
            add_into(part.at[0, :, :, cols], zp_buf.at[0, :, :, cols], zm_buf.at[0, :, :, cols])

    for p in range(2):
        cols = slice(p * 768, (p + 1) * 768)
        block = jnp.dot(lhs, wo[:, cols], preferred_element_type=F32).reshape(4, 8, 8, 768)
        for i in range(4):
            part[:, i, :, cols] = block[i].astype(BF)
        z_send(p, 4)
    for d in (3, 2, 1):
        for p in range(2):
            z_add(p, d)
            z_send(p, d)
    p_moves = []
    for p in range(2):
        z_add(p, 0)
        cols = z_cols(p)[0]
        for d in (2, 1, 3):
            p_moves.append(net.send(part.at[0, d, :, cols], px.at[4 - d, :, cols], xdev[d]))
    px[0] = part[0, 0]
    arrived(p_moves)
    for i in range(4):
        cols = pl.ds(pl.multiple_of(((x + i) & 3) * N_CHIP, HEAD), N_CHIP)
        mid_ref[:, cols] = (res_ref[:, cols].astype(F32) + px[i].astype(F32)).astype(BF)
    net.finish()


def attend(queries, cache_keys, cache_values, response_kv, segments, residual, out_weight):
    vmem = pl.BlockSpec(memory_space=pltpu.VMEM)
    hbm = pl.BlockSpec(memory_space=pl.ANY)
    return pl.pallas_call(
        attend_kernel,
        name="attend",
        out_shape=jax.ShapeDtypeStruct(residual.shape, BF),
        in_specs=[vmem, hbm, hbm, vmem, vmem, vmem, hbm],
        out_specs=vmem,
        scratch_shapes=[
            pltpu.VMEM((8, 8, 1024), BF),
            pltpu.VMEM((8, 8, 1024), BF),
            pltpu.VMEM((4, 8, 8, Q_COLS), BF),
            pltpu.VMEM((2, 4, 8, 8, 2 * HEAD), BF),
            pltpu.VMEM((KEYS_CHIP + RESP, HEAD), BF),
            pltpu.VMEM((KEYS_CHIP + RESP, 2 * HEAD), BF),
            pltpu.VMEM((Q_COLS, N_CHIP), BF),
            pltpu.VMEM((4, 8, 8, Q_COLS), BF),
            pltpu.VMEM((4, 2, 64, HEAD), F32),
            pltpu.VMEM((4, 8, 8, Q_COLS), BF),
            pltpu.VMEM((4, 2, 64, HEAD), F32),
            pltpu.VMEM((4, 8, 8, Q_COLS), BF),
            pltpu.VMEM((8, 4, 8, N_CHIP), BF),
            pltpu.VMEM((4, 4, 8, N_CHIP), BF),
            pltpu.VMEM((4, 4, 8, N_CHIP), BF),
            pltpu.VMEM((4, 8, N_CHIP), BF),
            pltpu.SemaphoreType.DMA((3,)),
            pltpu.SemaphoreType.DMA((64,)),
            pltpu.SemaphoreType.DMA((64,)),
        ],
        compiler_params=pltpu.CompilerParams(
            collective_id=1, has_side_effects=True, vmem_limit_bytes=48 * 1024 * 1024
        ),
    )(
        queries, cache_keys, cache_values, response_kv, segments.reshape(16, 128), residual, out_weight
    )


def on_device(
    queries,
    cache_keys,
    cache_values,
    response_kv,
    segments,
    residual,
    out_weight,
    norm_gain,
    up_weight,
    down_weight,
):
    mid = attend(
        queries, cache_keys, cache_values, response_kv, segments, residual, out_weight
    )
    return ffn(mid, norm_gain, up_weight, down_weight)


def solution(mesh):
    return jax.shard_map(
        on_device,
        mesh=mesh,
        in_specs=(
            P(("key", "hid"), None),
            P("key", None),
            P("key", None),
            P(("key", "hid"), None),
            P(),
            P(("key", "hid"), None),
            P("hid", "key"),
            P(),
            P(None, "hid"),
            P("hid", None),
        ),
        out_specs=P(("key", "hid"), None),
        check_vma=False,
    )
```

```python
import functools
import math

import jax
import jax.numpy as jnp
from jax import lax
from jax.experimental import pallas as pl
from jax.experimental.pallas import tpu as pltpu
from jax.sharding import PartitionSpec as P

HEADS = 48
KV_HEADS = 8
HEAD = 128
GROUP = 6
D = 6144
MESH = pl.DeviceIdType.MESH
BF = jnp.bfloat16
F32 = jnp.float32

ZI = {0: 0, 1: 1, -1: 2, 2: 3, -2: 4, 3: 5, -3: 6, 4: 7}
YI = {0: 0, 1: 1, -1: 2, 2: 3}
ZGROUPS = (pl.ds(0, 1), pl.ds(1, 2), pl.ds(3, 2), pl.ds(5, 2), pl.ds(7, 1))

A_COLS = 2560
B_COLS = D - A_COLS
CA, A0, A1 = pl.ds(0, A_COLS), pl.ds(0, A_COLS // 2), pl.ds(A_COLS // 2, A_COLS // 2)
CB = pl.ds(A_COLS, B_COLS)
B0, B1 = pl.ds(A_COLS, B_COLS // 2), pl.ds(A_COLS + B_COLS // 2, B_COLS // 2)
LB, L0, L1 = pl.ds(0, B_COLS), pl.ds(0, B_COLS // 2), pl.ds(B_COLS // 2, B_COLS // 2)
N_GATHER = 40
N_REDUCE = 40


class Copies:
    def __init__(self, send_sems, recv_sems):
        self.sems = send_sems, recv_sems
        self.made = []

    def send(self, src, dst, device):
        i = len(self.made)
        copy = pltpu.make_async_remote_copy(
            src_ref=src,
            dst_ref=dst,
            send_sem=self.sems[0].at[i],
            recv_sem=self.sems[1].at[i],
            device_id=device,
            device_id_type=MESH,
        )
        copy.start()
        self.made.append(copy)
        return copy

    def finish(self):
        for copy in self.made:
            copy.wait_send()


def where_am_i():
    key = lax.axis_index("key")
    hid = lax.axis_index("hid")
    return key // 2, key % 2, hid // 4, hid % 4


def device(x, core, z, y):
    return (lax.rem(x, 4) * 2 + core, lax.rem(z, 8) * 4 + lax.rem(y, 4))


def greet(devices):
    barrier = pltpu.get_barrier_semaphore()
    for one in devices:
        pl.semaphore_signal(barrier, inc=1, device_id=one, device_id_type=MESH)
    pl.semaphore_wait(barrier, len(devices))


def add_into(dst, *srcs):
    total = dst[...].astype(F32)
    for src in srcs:
        total = total + src[...].astype(F32)
    dst[...] = total.astype(BF)


def ffn_phase(
    where, mid_ref, gain_ref, load_up, load_down, out_ref,
    up_w, down_w, rows, part, acc, act,
    a_zp, a_zm, a_yp, a_ym, b_yp, b_ym, b_zp, b_zm,
    g_send, g_recv, r_send, r_recv,
):
    x, core, z, y = where
    zp, zm = device(x, core, z + 1, y), device(x, core, z + 7, y)
    yp, ym = device(x, core, z, y + 1), device(x, core, z, y + 3)

    wide = mid_ref[...].astype(F32)
    mean = jnp.mean(wide, axis=-1, keepdims=True)
    centred = wide - mean
    var = jnp.mean(centred * centred, axis=-1, keepdims=True)
    rows[0, 0] = (centred * lax.rsqrt(var + 1e-05) * gain_ref[...]).astype(BF)

    net = Copies(g_send, g_recv)
    every = pl.ds(0, 4)

    def ring_next(i, ys, cols, half0, half1):
        if i == 0:
            return (
                net.send(rows.at[0, ys, :, cols], rows.at[ZI[-1], ys, :, cols], zp),
                net.send(rows.at[0, ys, :, cols], rows.at[ZI[1], ys, :, cols], zm),
            )
        if i < 3:
            return (
                net.send(rows.at[ZI[-i], ys, :, cols], rows.at[ZI[-i - 1], ys, :, cols], zp),
                net.send(rows.at[ZI[i], ys, :, cols], rows.at[ZI[i + 1], ys, :, cols], zm),
            )
        return (
            net.send(rows.at[ZI[-3], ys, :, half0], rows.at[ZI[4], ys, :, half0], zp),
            net.send(rows.at[ZI[3], ys, :, half1], rows.at[ZI[4], ys, :, half1], zm),
        )

    def arrived(copies):
        for copy in copies:
            copy.wait_recv()

    def y_first(zs, cols):
        return (
            net.send(rows.at[zs, 0, :, cols], rows.at[zs, YI[-1], :, cols], yp),
            net.send(rows.at[zs, 0, :, cols], rows.at[zs, YI[1], :, cols], ym),
        )

    def y_second(zs, half0, half1):
        return (
            net.send(rows.at[zs, YI[-1], :, half0], rows.at[zs, YI[2], :, half0], yp),
            net.send(rows.at[zs, YI[1], :, half1], rows.at[zs, YI[2], :, half1], ym),
        )

    own = pl.ds(0, 1)
    ay = y_first(own, CA)
    bz = ring_next(0, 0, CB, B0, B1)
    by = [y_first(ZGROUPS[0], CB)]
    by2 = []
    arrived(ay)
    ay = y_second(own, A0, A1)
    arrived(bz)
    bz = ring_next(1, 0, CB, B0, B1)
    by.append(y_first(ZGROUPS[1], CB))
    arrived(ay)
    az = ring_next(0, every, CA, A0, A1)
    arrived(by[0])
    by2.append(y_second(ZGROUPS[0], B0, B1))
    arrived(bz)
    bz = ring_next(2, 0, CB, B0, B1)
    by.append(y_first(ZGROUPS[2], CB))
    arrived(by[1])
    by2.append(y_second(ZGROUPS[1], B0, B1))
    arrived(az)
    az = ring_next(1, every, CA, A0, A1)
    arrived(bz)
    bz = ring_next(3, 0, CB, B0, B1)
    by.append(y_first(ZGROUPS[3], CB))
    arrived(by[2])
    by2.append(y_second(ZGROUPS[2], B0, B1))
    arrived(az)
    az = ring_next(2, every, CA, A0, A1)
    arrived(bz)
    by.append(y_first(ZGROUPS[4], CB))
    arrived(by[3])
    by2.append(y_second(ZGROUPS[3], B0, B1))
    arrived(az)
    az = ring_next(3, every, CA, A0, A1)
    arrived(by[4])
    by2.append(y_second(ZGROUPS[4], B0, B1))
    arrived(az)
    for pair in by2:
        arrived(pair)

    load_up.wait()
    acc[...] = jnp.zeros_like(acc)

    def up_step(i, _):
        cols = pl.ds(pl.multiple_of(i * 512, 512), 512)
        block = rows[:, :, :, cols].astype(F32).reshape(256, 512).astype(BF)
        acc[...] += jnp.dot(block, up_w[cols, :], preferred_element_type=F32)
        return 0

    lax.fori_loop(0, D // 512, up_step, 0)
    up = jnp.maximum(acc[...], 0.0)
    act[...] = (up * up).astype(BF)
    load_down.wait()

    def down_step(i, _):
        cols = pl.ds(pl.multiple_of(i * 512, 512), 512)
        block = jnp.dot(act[...], down_w[:, cols], preferred_element_type=F32)
        part[:, :, :, cols] = block.reshape(8, 4, 8, 512).astype(BF)
        return 0

    net.finish()
    net = Copies(r_send, r_recv)

    def z_send(d, ys, cols, half0, half1, lcols, lh0, lh1, got_p, got_m, lys):
        if d == 4:
            return (
                net.send(part.at[ZI[4], ys, :, half1], got_p.at[3, lys, :, lh1], zp),
                net.send(part.at[ZI[4], ys, :, half0], got_m.at[3, lys, :, lh0], zm),
            )
        return (
            net.send(part.at[ZI[d], ys, :, cols], got_p.at[d - 1, lys, :, lcols], zp),
            net.send(part.at[ZI[-d], ys, :, cols], got_m.at[d - 1, lys, :, lcols], zm),
        )

    def z_add(copies, d, ys, cols, half0, half1, lcols, lh0, lh1, got_p, got_m, lys):
        arrived(copies)
        if d == 3:
            add_into(part.at[ZI[3], ys, :, half1], got_p.at[3, lys, :, lh1])
            add_into(part.at[ZI[-3], ys, :, half0], got_m.at[3, lys, :, lh0])
        elif d > 0:
            add_into(part.at[ZI[d], ys, :, cols], got_p.at[d, lys, :, lcols])
            add_into(part.at[ZI[-d], ys, :, cols], got_m.at[d, lys, :, lcols])
        else:
            add_into(
                part.at[0, ys, :, cols], got_p.at[0, lys, :, lcols], got_m.at[0, lys, :, lcols]
            )

    def y_send(step, zs, cols, half0, half1, lcols, lh0, lh1, got_p, got_m):
        if step == 0:
            return (
                net.send(part.at[zs, YI[2], :, half1], got_p.at[1, zs, :, lh1], yp),
                net.send(part.at[zs, YI[2], :, half0], got_m.at[1, zs, :, lh0], ym),
            )
        return (
            net.send(part.at[zs, YI[1], :, cols], got_p.at[0, zs, :, lcols], yp),
            net.send(part.at[zs, YI[-1], :, cols], got_m.at[0, zs, :, lcols], ym),
        )

    def y_add(copies, step, zs, cols, half0, half1, lcols, lh0, lh1, got_p, got_m):
        arrived(copies)
        if step == 0:
            add_into(part.at[zs, YI[1], :, half1], got_p.at[1, zs, :, lh1])
            add_into(part.at[zs, YI[-1], :, half0], got_m.at[1, zs, :, lh0])
        else:
            add_into(part.at[zs, 0, :, cols], got_p.at[0, zs, :, lcols], got_m.at[0, zs, :, lcols])

    za = (every, CA, A0, A1, CA, A0, A1, a_zp, a_zm, every)
    zb = (0, CB, B0, B1, LB, L0, L1, b_zp, b_zm, 0)
    yb = (CB, B0, B1, LB, L0, L1, b_yp, b_ym)
    ya = (CA, A0, A1, CA, A0, A1, a_yp, a_ym)

    lax.fori_loop(A_COLS // 512, D // 512, down_step, 0)
    order = [ZGROUPS[i] for i in (4, 3, 2, 1, 0)]
    by = [y_send(0, g, *yb) for g in order]
    lax.fori_loop(0, A_COLS // 512, down_step, 0)
    az = z_send(4, *za)
    y_add(by[0], 0, order[0], *yb)
    by[0] = y_send(1, order[0], *yb)
    y_add(by[1], 0, order[1], *yb)
    by[1] = y_send(1, order[1], *yb)
    z_add(az, 3, *za)
    az = z_send(3, *za)
    y_add(by[2], 0, order[2], *yb)
    by[2] = y_send(1, order[2], *yb)
    y_add(by[0], 1, order[0], *yb)
    bz = z_send(4, *zb)
    y_add(by[3], 0, order[3], *yb)
    by[3] = y_send(1, order[3], *yb)
    z_add(az, 2, *za)
    az = z_send(2, *za)
    y_add(by[4], 0, order[4], *yb)
    by[4] = y_send(1, order[4], *yb)
    y_add(by[1], 1, order[1], *yb)
    z_add(bz, 3, *zb)
    bz = z_send(3, *zb)
    z_add(az, 1, *za)
    az = z_send(1, *za)
    y_add(by[2], 1, order[2], *yb)
    z_add(bz, 2, *zb)
    bz = z_send(2, *zb)
    y_add(by[3], 1, order[3], *yb)
    z_add(az, 0, *za)
    ay = y_send(0, own, *ya)
    z_add(bz, 1, *zb)
    bz = z_send(1, *zb)
    y_add(ay, 0, own, *ya)
    ay = y_send(1, own, *ya)
    y_add(by[4], 1, order[4], *yb)
    arrived(bz)
    out_ref[:, CB] = (
        mid_ref[:, CB].astype(F32)
        + part[0, 0, :, CB].astype(F32)
        + b_zp[0, 0].astype(F32)
        + b_zm[0, 0].astype(F32)
    ).astype(BF)
    arrived(ay)
    out_ref[:, CA] = (
        mid_ref[:, CA].astype(F32)
        + part[0, 0, :, CA].astype(F32)
        + a_yp[0, 0].astype(F32)
        + a_ym[0, 0].astype(F32)
    ).astype(BF)
    net.finish()


LOG2_SCALE = math.log2(math.e) / math.sqrt(HEAD)
Q_COLS = GROUP * HEAD
KEYS_OWN = 768
KEYS_CHIP = 2 * KEYS_OWN
RESP = 512
N_CHIP = 1536


def layer_kernel(
    q_hbm, ck_hbm, cv_hbm, rkv_hbm, seg_hbm, res_hbm, wo_hbm, gain_hbm, up_hbm, down_hbm, out_ref,
    q_ref, rkv_ref, seg_ref, res_ref, gain_ref, mid_ref, up_w, down_w,
    packed, got, qall, rkv, kbuf, vbuf, wo, obuf, stat, robuf, rstat, attn, part, zp_buf, zm_buf,
    px, local_sem, s_sem, r_sem, *ffn_refs,
):
    x, core, z, y = where_am_i()
    sib = device(x, 1 - core, z, y)
    zdev = [device(x, core, z + d, y) for d in range(8)]
    xdev = [device(x + d, core, z, y) for d in range(4)]
    ydev = [device(x, core, z, y + d) for d in range(4)]
    head = pl.ds(pl.multiple_of(z * HEAD, HEAD), HEAD)
    wo_rows = pl.ds(pl.multiple_of(y * 192, 64), 192)
    wo_own = pl.ds(pl.multiple_of(core * 768, 128), 768)

    loads = [
        pltpu.make_async_copy(src, dst, local_sem.at[3 + i])
        for i, (src, dst) in enumerate(
            (
                (q_hbm, q_ref),
                (rkv_hbm, rkv_ref),
                (seg_hbm, seg_ref),
                (res_hbm, res_ref),
                (gain_hbm, gain_ref),
                (up_hbm, up_w),
                (down_hbm, down_w),
            )
        )
    ]
    load_q, load_rkv, load_seg, load_res, load_gain, load_up, load_down = loads
    load_q.start()
    load_rkv.start()
    load_k = pltpu.make_async_copy(ck_hbm.at[:, head], kbuf.at[pl.ds(0, KEYS_OWN)], local_sem.at[0])
    load_v = pltpu.make_async_copy(
        cv_hbm.at[:, head], vbuf.at[pl.ds(0, KEYS_OWN), pl.ds(0, HEAD)], local_sem.at[1]
    )
    load_wo = pltpu.make_async_copy(wo_hbm, wo.at[wo_rows, wo_own], local_sem.at[2])
    load_k.start()
    load_v.start()
    load_wo.start()
    for load in (load_seg, load_res, load_gain):
        load.start()
    load_q.wait()
    load_rkv.wait()
    for i in range(8):
        packed[i, :, 0:Q_COLS] = q_ref[:, i * Q_COLS : (i + 1) * Q_COLS]
        packed[i, :, Q_COLS : Q_COLS + HEAD] = rkv_ref[:, i * HEAD : (i + 1) * HEAD]
        packed[i, :, Q_COLS + HEAD :] = rkv_ref[:, 1024 + i * HEAD : 1024 + (i + 1) * HEAD]
    greet([*zdev[1:], *xdev[1:], *ydev[1:], sib])
    net = Copies(s_sem, r_sem)

    def arrived(copies):
        for copy in copies:
            copy.wait_recv()

    moves = [
        net.send(packed.at[lax.rem(z + d, 8)], got.at[8 - d], zdev[d]) for d in (4, 3, 5, 2, 6, 1, 7)
    ]
    caches = [
        net.send(ck_hbm.at[:, head], kbuf.at[pl.ds(KEYS_OWN, KEYS_OWN)], sib),
        net.send(cv_hbm.at[:, head], vbuf.at[pl.ds(KEYS_OWN, KEYS_OWN), pl.ds(0, HEAD)], sib),
    ]
    got[0] = packed[z]
    vbuf[:, HEAD:] = jnp.ones((KEYS_CHIP + RESP, HEAD), BF)
    arrived(moves)
    rkv[0, 0] = got[:, :, Q_COLS:]
    kv_moves = [net.send(rkv.at[0, 0], rkv.at[0, 4 - d], ydev[d]) for d in (2, 1, 3)]
    qall[0] = got[:, :, 0:Q_COLS]
    q_moves = [net.send(qall.at[0], qall.at[4 - d], xdev[d]) for d in (1, 3, 2)]

    load_seg.wait()
    seg = seg_ref[...]
    bounds = [
        jnp.sum(jnp.where(seg < s, 1, 0), keepdims=True) for s in (1, 2, 3)
    ]
    lanes = lax.broadcasted_iota(jnp.int32, (1, RESP), 1)
    key_row = (
        (2 * x + ((core + lanes // 256) & 1)) * 32
        + ((z + (lanes // 8)) & 7) * 4
        + ((y + (lanes // 64)) & 3)
    ) * 8 + (lanes & 7)
    slots = lax.broadcasted_iota(jnp.int32, (64, 1), 0)

    load_up.start()
    load_down.start()
    arrived(kv_moves)
    kv_sib = net.send(rkv.at[0], rkv.at[1], sib)
    load_wo.wait()
    own_wo = wo.at[wo_rows, wo_own]
    wo_moves = [net.send(own_wo, own_wo, ydev[d]) for d in (1, 3)]
    load_k.wait()
    load_v.wait()
    arrived(caches)
    arrived([kv_sib])
    kbuf[pl.ds(KEYS_CHIP, RESP), :] = rkv[:, :, :, :, 0:HEAD].astype(F32).reshape(RESP, HEAD).astype(BF)
    vbuf[pl.ds(KEYS_CHIP, RESP), 0:HEAD] = (
        rkv[:, :, :, :, HEAD:].astype(F32).reshape(RESP, HEAD).astype(BF)
    )

    def attend(i):
        wide = qall[i].astype(F32)
        q = jnp.concatenate(
            [wide[:, :, j * HEAD : (j + 1) * HEAD].reshape(64, HEAD) for j in range(GROUP)], 0
        ).astype(BF)
        q_row = ((2 * ((x + i) & 3) + core) * 32 + ((z + slots // 8) & 7) * 4 + y) * 8 + (slots & 7)
        start = jnp.zeros_like(q_row)
        for bound in bounds:
            start = jnp.maximum(start, jnp.where(q_row >= bound, bound, 0))
        seen = (key_row <= q_row) & (key_row >= start)
        seen = jnp.concatenate([jnp.where(seen, 0.0, -jnp.inf)] * GROUP, 0)
        nt = (((1,), (1,)), ((), ()))
        s1 = lax.dot_general(q, kbuf[0:KEYS_CHIP, :], nt, preferred_element_type=F32)
        s2 = lax.dot_general(q, kbuf[KEYS_CHIP:, :], nt, preferred_element_type=F32) + seen
        top = jnp.maximum(
            jnp.max(s1, axis=-1, keepdims=True), jnp.max(s2, axis=-1, keepdims=True)
        )
        p1 = jnp.exp2((s1 - top) * LOG2_SCALE).astype(BF)
        p2 = jnp.exp2((s2 - top) * LOG2_SCALE).astype(BF)
        mixed = jnp.dot(p1, vbuf[0:KEYS_CHIP, :], preferred_element_type=F32) + jnp.dot(
            p2, vbuf[KEYS_CHIP:, :], preferred_element_type=F32
        )
        lane = lax.broadcasted_iota(jnp.int32, (64, HEAD), 1)
        tops = jnp.zeros((64, HEAD), F32)
        totals = jnp.ones((64, HEAD), F32)
        for j in range(GROUP):
            rows = slice(j * 64, (j + 1) * 64)
            obuf[i, :, :, j * HEAD : (j + 1) * HEAD] = mixed[rows, 0:HEAD].reshape(8, 8, HEAD).astype(BF)
            tops = jnp.where(lane == j, top[rows], tops)
            totals = jnp.where(lane == j, mixed[rows, HEAD:], totals)
        stat[i, 0] = tops
        stat[i, 1] = totals

    o_moves = []

    def give(d):
        attend(d)
        o_moves.append(net.send(obuf.at[d], robuf.at[4 - d], xdev[d]))
        o_moves.append(net.send(stat.at[d], rstat.at[4 - d], xdev[d]))

    arrived([q_moves[2]])
    give(2)
    arrived([q_moves[0]])
    give(3)
    arrived(wo_moves)
    back, ahead = lax.rem(y + 3, 4), lax.rem(y + 1, 4)
    low = wo.at[pl.ds(pl.multiple_of(back * 192, 64), 96), wo_own]
    high = wo.at[pl.ds(pl.multiple_of(ahead * 192 + 96, 32), 96), wo_own]
    wo_moves = [net.send(low, low, ydev[1]), net.send(high, high, ydev[3])]
    arrived([q_moves[1]])
    give(1)
    attend(0)
    arrived(wo_moves)
    wo_cols = wo.at[:, wo_own]
    wo_sib = net.send(wo_cols, wo_cols, sib)
    arrived(o_moves)

    tops = [stat[0, 0]] + [rstat[i, 0] for i in range(1, 4)]
    totals = [stat[0, 1]] + [rstat[i, 1] for i in range(1, 4)]
    top = functools.reduce(jnp.maximum, tops)
    scales = [jnp.exp2((t - top) * LOG2_SCALE) for t in tops]
    total = functools.reduce(jnp.add, [a * b for a, b in zip(scales, totals)])
    scales = [a / total for a in scales]
    for j in range(GROUP):
        cols = slice(j * HEAD, (j + 1) * HEAD)
        mixed = obuf[0, :, :, cols].astype(F32).reshape(64, HEAD) * scales[0][:, j : j + 1]
        for i in range(1, 4):
            mixed = mixed + robuf[i, :, :, cols].astype(F32).reshape(64, HEAD) * scales[i][:, j : j + 1]
        attn[0, :, :, cols] = mixed.reshape(8, 8, HEAD).astype(BF)
    a_moves = [net.send(attn.at[0], attn.at[4 - d], xdev[d]) for d in (2, 1, 3)]
    arrived([wo_sib])
    arrived(a_moves)

    lhs = attn[...].astype(F32).reshape(256, Q_COLS).astype(BF)
    ring = [[], []]

    def z_cols(p):
        base = p * 768
        return pl.ds(base, 768), pl.ds(base, 384), pl.ds(base + 384, 384)

    def z_send(p, d):
        cols, half0, half1 = z_cols(p)
        if d == 4:
            ring[p] = [
                net.send(part.at[4, :, :, half1], zp_buf.at[3, :, :, half1], zdev[1]),
                net.send(part.at[4, :, :, half0], zm_buf.at[3, :, :, half0], zdev[7]),
            ]
        else:
            ring[p] = [
                net.send(part.at[d, :, :, cols], zp_buf.at[d - 1, :, :, cols], zdev[1]),
                net.send(part.at[8 - d, :, :, cols], zm_buf.at[d - 1, :, :, cols], zdev[7]),
            ]

    def z_add(p, d):
        cols, half0, half1 = z_cols(p)
        arrived(ring[p])
        if d == 3:
            add_into(part.at[3, :, :, half1], zp_buf.at[3, :, :, half1])
            add_into(part.at[5, :, :, half0], zm_buf.at[3, :, :, half0])
        elif d > 0:
            add_into(part.at[d, :, :, cols], zp_buf.at[d, :, :, cols])
            add_into(part.at[8 - d, :, :, cols], zm_buf.at[d, :, :, cols])
        else:
            add_into(part.at[0, :, :, cols], zp_buf.at[0, :, :, cols], zm_buf.at[0, :, :, cols])

    for p in range(2):
        cols = slice(p * 768, (p + 1) * 768)
        block = jnp.dot(lhs, wo[:, cols], preferred_element_type=F32).reshape(4, 8, 8, 768)
        for i in range(4):
            part[:, i, :, cols] = block[i].astype(BF)
        z_send(p, 4)
    for d in (3, 2, 1):
        for p in range(2):
            z_add(p, d)
            z_send(p, d)
    p_moves = []
    for p in range(2):
        z_add(p, 0)
        cols = z_cols(p)[0]
        for d in (2, 1, 3):
            p_moves.append(net.send(part.at[0, d, :, cols], px.at[4 - d, :, cols], xdev[d]))
    px[0] = part[0, 0]
    load_res.wait()
    load_gain.wait()
    arrived(p_moves)
    for i in range(4):
        cols = pl.ds(pl.multiple_of(((x + i) & 3) * N_CHIP, HEAD), N_CHIP)
        mid_ref[:, cols] = (res_ref[:, cols].astype(F32) + px[i].astype(F32)).astype(BF)
    net.finish()
    ffn_phase(
        (x, core, z, y), mid_ref, gain_ref, load_up, load_down, out_ref, up_w, down_w, *ffn_refs
    )


def on_device(
    queries,
    cache_keys,
    cache_values,
    response_kv,
    segments,
    residual,
    out_weight,
    norm_gain,
    up_weight,
    down_weight,
):
    hbm = pl.BlockSpec(memory_space=pl.ANY)
    hidden = up_weight.shape[1]
    return pl.pallas_call(
        layer_kernel,
        name="layer",
        out_shape=jax.ShapeDtypeStruct(residual.shape, BF),
        in_specs=[hbm] * 10,
        out_specs=pl.BlockSpec(memory_space=pltpu.VMEM),
        scratch_shapes=[
            pltpu.VMEM(queries.shape, BF),
            pltpu.VMEM(response_kv.shape, BF),
            pltpu.VMEM((16, 128), jnp.int32),
            pltpu.VMEM(residual.shape, BF),
            pltpu.VMEM((1, D), F32),
            pltpu.VMEM(residual.shape, BF),
            pltpu.VMEM((D, hidden), BF),
            pltpu.VMEM((hidden, D), BF),
            pltpu.VMEM((8, 8, 1024), BF),
            pltpu.VMEM((8, 8, 1024), BF),
            pltpu.VMEM((4, 8, 8, Q_COLS), BF),
            pltpu.VMEM((2, 4, 8, 8, 2 * HEAD), BF),
            pltpu.VMEM((KEYS_CHIP + RESP, HEAD), BF),
            pltpu.VMEM((KEYS_CHIP + RESP, 2 * HEAD), BF),
            pltpu.VMEM((Q_COLS, N_CHIP), BF),
            pltpu.VMEM((4, 8, 8, Q_COLS), BF),
            pltpu.VMEM((4, 2, 64, HEAD), F32),
            pltpu.VMEM((4, 8, 8, Q_COLS), BF),
            pltpu.VMEM((4, 2, 64, HEAD), F32),
            pltpu.VMEM((4, 8, 8, Q_COLS), BF),
            pltpu.VMEM((8, 4, 8, N_CHIP), BF),
            pltpu.VMEM((4, 4, 8, N_CHIP), BF),
            pltpu.VMEM((4, 4, 8, N_CHIP), BF),
            pltpu.VMEM((4, 8, N_CHIP), BF),
            pltpu.SemaphoreType.DMA((10,)),
            pltpu.SemaphoreType.DMA((64,)),
            pltpu.SemaphoreType.DMA((64,)),
            pltpu.VMEM((8, 4, 8, D), BF),
            pltpu.VMEM((8, 4, 8, D), BF),
            pltpu.VMEM((256, hidden), F32),
            pltpu.VMEM((256, hidden), BF),
            pltpu.VMEM((4, 4, 8, A_COLS), BF),
            pltpu.VMEM((4, 4, 8, A_COLS), BF),
            pltpu.VMEM((2, 1, 8, A_COLS), BF),
            pltpu.VMEM((2, 1, 8, A_COLS), BF),
            pltpu.VMEM((2, 8, 8, B_COLS), BF),
            pltpu.VMEM((2, 8, 8, B_COLS), BF),
            pltpu.VMEM((4, 1, 8, B_COLS), BF),
            pltpu.VMEM((4, 1, 8, B_COLS), BF),
            pltpu.SemaphoreType.DMA((N_GATHER,)),
            pltpu.SemaphoreType.DMA((N_GATHER,)),
            pltpu.SemaphoreType.DMA((N_REDUCE,)),
            pltpu.SemaphoreType.DMA((N_REDUCE,)),
        ],
        compiler_params=pltpu.CompilerParams(
            collective_id=0, has_side_effects=True, vmem_limit_bytes=60 * 1024 * 1024
        ),
    )(
        queries, cache_keys, cache_values, response_kv, segments.reshape(16, 128), residual,
        out_weight, norm_gain.reshape(1, D), up_weight, down_weight,
    )


def solution(mesh):
    return jax.shard_map(
        on_device,
        mesh=mesh,
        in_specs=(
            P(("key", "hid"), None),
            P("key", None),
            P("key", None),
            P(("key", "hid"), None),
            P(),
            P(("key", "hid"), None),
            P("hid", "key"),
            P(),
            P(None, "hid"),
            P("hid", None),
        ),
        out_specs=P(("key", "hid"), None),
        check_vma=False,
    )
```

```python
import functools
import math

import jax
import jax.numpy as jnp
from jax import lax
from jax.experimental import pallas as pl
from jax.experimental.pallas import tpu as pltpu
from jax.sharding import PartitionSpec as P

HEADS = 48
KV_HEADS = 8
HEAD = 128
GROUP = 6
D = 6144
MESH = pl.DeviceIdType.MESH
BF = jnp.bfloat16
F32 = jnp.float32

ZI = {0: 0, 1: 1, -1: 2, 2: 3, -2: 4, 3: 5, -3: 6, 4: 7}
YI = {0: 0, 1: 1, -1: 2, 2: 3}
ZGROUPS = (pl.ds(0, 1), pl.ds(1, 2), pl.ds(3, 2), pl.ds(5, 2), pl.ds(7, 1))

A_COLS = 2560
B_COLS = D - A_COLS
CA, A0, A1 = pl.ds(0, A_COLS), pl.ds(0, A_COLS // 2), pl.ds(A_COLS // 2, A_COLS // 2)
CB = pl.ds(A_COLS, B_COLS)
B0, B1 = pl.ds(A_COLS, B_COLS // 2), pl.ds(A_COLS + B_COLS // 2, B_COLS // 2)
LB, L0, L1 = pl.ds(0, B_COLS), pl.ds(0, B_COLS // 2), pl.ds(B_COLS // 2, B_COLS // 2)
N_GATHER = 56
N_REDUCE = 56


class Copies:
    def __init__(self, send_sems, recv_sems):
        self.sems = send_sems, recv_sems
        self.made = []

    def send(self, src, dst, device):
        i = len(self.made)
        copy = pltpu.make_async_remote_copy(
            src_ref=src,
            dst_ref=dst,
            send_sem=self.sems[0].at[i],
            recv_sem=self.sems[1].at[i],
            device_id=device,
            device_id_type=MESH,
        )
        copy.start()
        self.made.append(copy)
        return copy

    def finish(self):
        for copy in self.made:
            copy.wait_send()


def where_am_i():
    key = lax.axis_index("key")
    hid = lax.axis_index("hid")
    return key // 2, key % 2, hid // 4, hid % 4


def device(x, core, z, y):
    return (lax.rem(x, 4) * 2 + core, lax.rem(z, 8) * 4 + lax.rem(y, 4))


def greet(devices):
    barrier = pltpu.get_barrier_semaphore()
    for one in devices:
        pl.semaphore_signal(barrier, inc=1, device_id=one, device_id_type=MESH)
    return lambda: pl.semaphore_wait(barrier, len(devices))


def add_into(dst, *srcs):
    total = dst[...].astype(F32)
    for src in srcs:
        total = total + src[...].astype(F32)
    dst[...] = total.astype(BF)


GATHER_ORDER = (
    "ay1 bz1 by10 az10 ay2 az11 by11 bz2 by20 az20 az12 az21 by21 bz3 az30 by12 az22 az31 "
    "bz4 az40 by13 az32 by22 az41 by14 az42 up by23 by24"
)
REDUCE_ORDER = (
    "az42 az41 by04 az40 by03 by02 by01 az32 by00 by14 az31 az30 az22 by13 bz4 by12 az21 az20 "
    "az12 by11 bz3 by10 az11 ay0 az10 bz2 ay1 bz1"
)
PIECES = (pl.ds(0, 1), pl.ds(1, 2), pl.ds(3, 1))


def ffn_phase(
    where, mid_ref, gain_ref, load_up, load_down, out_ref,
    up_w, down_w, rows, part, acc, act,
    a_zp, a_zm, a_yp, a_ym, b_yp, b_ym, b_zp, b_zm,
    g_send, g_recv, r_send, r_recv,
):
    x, core, z, y = where
    zp, zm = device(x, core, z + 1, y), device(x, core, z + 7, y)
    yp, ym = device(x, core, z, y + 1), device(x, core, z, y + 3)

    wide = mid_ref[...].astype(F32)
    mean = jnp.mean(wide, axis=-1, keepdims=True)
    centred = wide - mean
    var = jnp.mean(centred * centred, axis=-1, keepdims=True)
    rows[0, 0] = (centred * lax.rsqrt(var + 1e-05) * gain_ref[...]).astype(BF)

    net = Copies(g_send, g_recv)
    flying = {}

    def z_hop(hop, ys, cols, half0, half1):
        if hop == 4:
            return (
                net.send(rows.at[ZI[-3], ys, :, half0], rows.at[ZI[4], ys, :, half0], zp),
                net.send(rows.at[ZI[3], ys, :, half1], rows.at[ZI[4], ys, :, half1], zm),
            )
        return (
            net.send(rows.at[ZI[1 - hop], ys, :, cols], rows.at[ZI[-hop], ys, :, cols], zp),
            net.send(rows.at[ZI[hop - 1], ys, :, cols], rows.at[ZI[hop], ys, :, cols], zm),
        )

    def y_first(zs, cols):
        return (
            net.send(rows.at[zs, 0, :, cols], rows.at[zs, YI[-1], :, cols], yp),
            net.send(rows.at[zs, 0, :, cols], rows.at[zs, YI[1], :, cols], ym),
        )

    def y_second(zs, half0, half1):
        return (
            net.send(rows.at[zs, YI[-1], :, half0], rows.at[zs, YI[2], :, half0], yp),
            net.send(rows.at[zs, YI[1], :, half1], rows.at[zs, YI[2], :, half1], ym),
        )

    def az_hop(hop, piece):
        flying["az%d%d" % (hop, piece)] = z_hop(hop, PIECES[piece], CA, A0, A1)

    def bz_hop(hop):
        flying["bz%d" % hop] = z_hop(hop, 0, CB, B0, B1)

    def up_cols(first, size, fresh):
        cols = pl.ds(first, size)
        block = rows[:, :, :, cols].astype(F32).reshape(256, size).astype(BF)
        product = jnp.dot(block, up_w[cols, :], preferred_element_type=F32)
        if fresh:
            acc[...] = product
        else:
            acc[...] += product

    own = pl.ds(0, 1)
    flying["ay1"] = y_first(own, CA)
    bz_hop(1)
    flying["by10"] = y_first(ZGROUPS[0], CB)
    az_hop(1, 0)
    for name in GATHER_ORDER.split():
        if name == "up":
            load_up.wait()
            for i in range(2):
                up_cols(i * (A_COLS // 2), A_COLS // 2, i == 0)
            continue
        for copy in flying[name]:
            copy.wait_recv()
        kind, step = name[:2], int(name[2])
        if kind == "ay" and step == 1:
            flying["ay2"] = y_second(own, A0, A1)
            az_hop(1, 1)
        elif kind == "ay":
            az_hop(1, 2)
        elif kind == "az" and step < 4:
            az_hop(step + 1, int(name[3]))
        elif kind == "bz":
            if step < 4:
                bz_hop(step + 1)
            flying["by1%d" % step] = y_first(ZGROUPS[step], CB)
        elif kind == "by" and step == 1:
            flying["by2" + name[3]] = y_second(ZGROUPS[int(name[3])], B0, B1)

    for i in range(2):
        up_cols(A_COLS + i * (B_COLS // 2), B_COLS // 2, False)
    up = jnp.maximum(acc[...], 0.0)
    act[...] = (up * up).astype(BF)
    load_down.wait()

    def down_cols(first, size):
        cols = pl.ds(first, size)
        block = jnp.dot(act[...], down_w[:, cols], preferred_element_type=F32)
        part[:, :, :, cols] = block.reshape(8, 4, 8, size).astype(BF)

    net.finish()
    net = Copies(r_send, r_recv)
    flying = {}
    done = set()

    def z_send(d, ys, cols, half0, half1, lcols, lh0, lh1, got_p, got_m, lys):
        if d == 4:
            return (
                net.send(part.at[ZI[4], ys, :, half1], got_p.at[3, lys, :, lh1], zp),
                net.send(part.at[ZI[4], ys, :, half0], got_m.at[3, lys, :, lh0], zm),
            )
        return (
            net.send(part.at[ZI[d], ys, :, cols], got_p.at[d - 1, lys, :, lcols], zp),
            net.send(part.at[ZI[-d], ys, :, cols], got_m.at[d - 1, lys, :, lcols], zm),
        )

    def z_add(d, ys, cols, half0, half1, lcols, lh0, lh1, got_p, got_m, lys):
        if d == 3:
            add_into(part.at[ZI[3], ys, :, half1], got_p.at[3, lys, :, lh1])
            add_into(part.at[ZI[-3], ys, :, half0], got_m.at[3, lys, :, lh0])
        elif d > 0:
            add_into(part.at[ZI[d], ys, :, cols], got_p.at[d, lys, :, lcols])
            add_into(part.at[ZI[-d], ys, :, cols], got_m.at[d, lys, :, lcols])
        else:
            add_into(
                part.at[0, ys, :, cols], got_p.at[0, lys, :, lcols], got_m.at[0, lys, :, lcols]
            )

    def y_send(step, zs, cols, half0, half1, lcols, lh0, lh1, got_p, got_m):
        if step == 0:
            return (
                net.send(part.at[zs, YI[2], :, half1], got_p.at[1, zs, :, lh1], yp),
                net.send(part.at[zs, YI[2], :, half0], got_m.at[1, zs, :, lh0], ym),
            )
        return (
            net.send(part.at[zs, YI[1], :, cols], got_p.at[0, zs, :, lcols], yp),
            net.send(part.at[zs, YI[-1], :, cols], got_m.at[0, zs, :, lcols], ym),
        )

    def y_add(step, zs, cols, half0, half1, lcols, lh0, lh1, got_p, got_m):
        if step == 0:
            add_into(part.at[zs, YI[1], :, half1], got_p.at[1, zs, :, lh1])
            add_into(part.at[zs, YI[-1], :, half0], got_m.at[1, zs, :, lh0])
        else:
            add_into(part.at[zs, 0, :, cols], got_p.at[0, zs, :, lcols], got_m.at[0, zs, :, lcols])

    za = [(p, CA, A0, A1, CA, A0, A1, a_zp, a_zm, p) for p in PIECES]
    zb = (0, CB, B0, B1, LB, L0, L1, b_zp, b_zm, 0)
    yb = (CB, B0, B1, LB, L0, L1, b_yp, b_ym)
    ya = (CA, A0, A1, CA, A0, A1, a_yp, a_ym)

    for i in range(2):
        down_cols(i * (A_COLS // 2), A_COLS // 2)
    for p in (2, 1, 0):
        flying["az4%d" % p] = z_send(4, *za[p])
    for i in range(2):
        down_cols(A_COLS + i * (B_COLS // 2), B_COLS // 2)
    for g in (4, 3, 2, 1, 0):
        flying["by0%d" % g] = y_send(0, ZGROUPS[g], *yb)
    for name in REDUCE_ORDER.split():
        for copy in flying[name]:
            copy.wait_recv()
        done.add(name)
        kind, step = name[:2], int(name[2])
        if kind == "az":
            p = int(name[3])
            z_add(step - 1, *za[p])
            if step > 1:
                flying["az%d%d" % (step - 1, p)] = z_send(step - 1, *za[p])
            elif p == 2:
                flying["ay0"] = y_send(0, own, *ya)
        elif kind == "by" and step == 0:
            y_add(0, ZGROUPS[int(name[3])], *yb)
            flying["by1" + name[3]] = y_send(1, ZGROUPS[int(name[3])], *yb)
        elif kind == "by":
            y_add(1, ZGROUPS[int(name[3])], *yb)
        elif kind == "bz" and step > 1:
            z_add(step - 1, *zb)
        elif kind == "ay" and step == 0:
            y_add(0, own, *ya)
        for d in (4, 3, 2, 1):
            if "bz%d" % d not in flying and "by1%d" % d in done and (d == 4 or "bz%d" % (d + 1) in done):
                flying["bz%d" % d] = z_send(d, *zb)
        if "ay1" not in flying and "ay0" in done and "az11" in done:
            flying["ay1"] = y_send(1, own, *ya)
        if name == "ay1":
            out_ref[:, CA] = (
                mid_ref[:, CA].astype(F32)
                + part[0, 0, :, CA].astype(F32)
                + a_yp[0, 0].astype(F32)
                + a_ym[0, 0].astype(F32)
            ).astype(BF)
        if name == "bz1":
            out_ref[:, CB] = (
                mid_ref[:, CB].astype(F32)
                + part[0, 0, :, CB].astype(F32)
                + b_zp[0, 0].astype(F32)
                + b_zm[0, 0].astype(F32)
            ).astype(BF)
    net.finish()


LOG2_SCALE = math.log2(math.e) / math.sqrt(HEAD)
Q_COLS = GROUP * HEAD
KEYS_OWN = 768
KEYS_CHIP = 2 * KEYS_OWN
RESP = 512
N_CHIP = 1536


def layer_kernel(
    q_hbm, ck_hbm, cv_hbm, rkv_hbm, seg_hbm, res_hbm, wo_hbm, gain_hbm, up_hbm, down_hbm, out_ref,
    q_ref, rkv_ref, seg_ref, res_ref, gain_ref, mid_ref, up_w, down_w,
    packed, got, qcat, osum, qall, rkv, kbuf, vbuf, wo, obuf, stat, robuf, rstat, attn, part, zp_buf, zm_buf,
    px, local_sem, s_sem, r_sem, *ffn_refs,
):
    x, core, z, y = where_am_i()
    sib = device(x, 1 - core, z, y)
    zdev = [device(x, core, z + d, y) for d in range(8)]
    xdev = [device(x + d, core, z, y) for d in range(4)]
    ydev = [device(x, core, z, y + d) for d in range(4)]
    ysib = [device(x, 1 - core, z, y + d) for d in range(4)]
    all_here = greet([*zdev[1:], *xdev[1:], *ydev[1:], *ysib])
    head = pl.ds(pl.multiple_of(z * HEAD, HEAD), HEAD)
    wo_rows = pl.ds(pl.multiple_of(y * 192, 64), 192)
    wo_own = pl.ds(pl.multiple_of(core * 768, 128), 768)

    loads = [
        pltpu.make_async_copy(src, dst, local_sem.at[3 + i])
        for i, (src, dst) in enumerate(
            (
                (q_hbm, q_ref),
                (rkv_hbm, rkv_ref),
                (seg_hbm, seg_ref),
                (res_hbm, res_ref),
                (gain_hbm, gain_ref),
                (up_hbm, up_w),
                (down_hbm, down_w),
            )
        )
    ]
    load_q, load_rkv, load_seg, load_res, load_gain, load_up, load_down = loads
    load_q.start()
    load_rkv.start()
    load_k = pltpu.make_async_copy(ck_hbm.at[:, head], kbuf.at[pl.ds(0, KEYS_OWN)], local_sem.at[0])
    load_v = pltpu.make_async_copy(
        cv_hbm.at[:, head], vbuf.at[pl.ds(0, KEYS_OWN), pl.ds(0, HEAD)], local_sem.at[1]
    )
    load_wo = pltpu.make_async_copy(wo_hbm, wo.at[wo_rows, wo_own], local_sem.at[2])
    load_k.start()
    load_v.start()
    load_wo.start()
    for load in (load_seg, load_res, load_gain):
        load.start()
    load_q.wait()
    load_rkv.wait()
    for i in range(8):
        packed[i, :, 0:Q_COLS] = q_ref[:, i * Q_COLS : (i + 1) * Q_COLS]
        packed[i, :, Q_COLS : Q_COLS + HEAD] = rkv_ref[:, i * HEAD : (i + 1) * HEAD]
        packed[i, :, Q_COLS + HEAD :] = rkv_ref[:, 1024 + i * HEAD : 1024 + (i + 1) * HEAD]
    all_here()
    net = Copies(s_sem, r_sem)

    def arrived(copies):
        for copy in copies:
            copy.wait_recv()

    moves = [
        net.send(packed.at[lax.rem(z + d, 8)], got.at[8 - d], zdev[d]) for d in (4, 3, 5, 2, 6, 1, 7)
    ]
    caches = [
        net.send(ck_hbm.at[:, head], kbuf.at[pl.ds(KEYS_OWN, KEYS_OWN)], sib),
        net.send(cv_hbm.at[:, head], vbuf.at[pl.ds(KEYS_OWN, KEYS_OWN), pl.ds(0, HEAD)], sib),
    ]
    got[0] = packed[z]
    vbuf[:, HEAD:] = jnp.ones((KEYS_CHIP + RESP, HEAD), BF)
    arrived(moves)
    rkv[0, 0] = got[:, :, Q_COLS:]
    kv_moves = [net.send(rkv.at[0, 0], rkv.at[0, 4 - d], ydev[d]) for d in (2, 1, 3)]
    kv_moves += [net.send(rkv.at[0, 0], rkv.at[1, (4 - d) % 4], ysib[d]) for d in (2, 1, 3, 0)]
    qall[0] = got[:, :, 0:Q_COLS]
    q_moves = [net.send(qall.at[0], qall.at[4 - d], xdev[d]) for d in (1, 3, 2)]

    load_seg.wait()
    seg = seg_ref[...]
    bounds = [
        jnp.sum(jnp.where(seg < s, 1, 0), keepdims=True) for s in (1, 2, 3)
    ]
    lanes = lax.broadcasted_iota(jnp.int32, (1, RESP), 1)
    key_row = (
        (2 * x + ((core + lanes // 256) & 1)) * 32
        + ((z + (lanes // 8)) & 7) * 4
        + ((y + (lanes // 64)) & 3)
    ) * 8 + (lanes & 7)
    slots = lax.broadcasted_iota(jnp.int32, (64, 1), 0)

    load_up.start()
    load_down.start()
    nt = (((1,), (1,)), ((), ()))
    lane = lax.broadcasted_iota(jnp.int32, (64, HEAD), 1)
    wide_lane = lax.broadcasted_iota(jnp.int32, (GROUP * 64, HEAD), 1)

    def attend_cache(i):
        wide = qall[i].astype(F32)
        q = jnp.concatenate(
            [wide[:, :, j * HEAD : (j + 1) * HEAD].reshape(64, HEAD) for j in range(GROUP)], 0
        ).astype(BF)
        qcat[i] = q
        score = lax.dot_general(q, kbuf[0:KEYS_CHIP, :], nt, preferred_element_type=F32)
        top = jnp.max(score, axis=-1, keepdims=True)
        weight = jnp.exp2((score - top) * LOG2_SCALE).astype(BF)
        mixed = jnp.dot(weight, vbuf[0:KEYS_CHIP, :], preferred_element_type=F32)
        osum[i, :, 0:HEAD] = mixed[:, 0:HEAD]
        osum[i, :, HEAD:] = jnp.where(wide_lane < 64, mixed[:, HEAD:], top)

    def attend_response(i):
        q_row = ((2 * ((x + i) & 3) + core) * 32 + ((z + slots // 8) & 7) * 4 + y) * 8 + (slots & 7)
        start = jnp.zeros_like(q_row)
        for bound in bounds:
            start = jnp.maximum(start, jnp.where(q_row >= bound, bound, 0))
        seen = (key_row <= q_row) & (key_row >= start)
        seen = jnp.concatenate([jnp.where(seen, 0.0, -jnp.inf)] * GROUP, 0)
        score = lax.dot_general(qcat[i], kbuf[KEYS_CHIP:, :], nt, preferred_element_type=F32) + seen
        first_top = osum[i, :, 2 * HEAD - 1 : 2 * HEAD]
        top = jnp.maximum(first_top, jnp.max(score, axis=-1, keepdims=True))
        weight = jnp.exp2((score - top) * LOG2_SCALE).astype(BF)
        mixed = osum[i] * jnp.exp2((first_top - top) * LOG2_SCALE) + jnp.dot(
            weight, vbuf[KEYS_CHIP:, :], preferred_element_type=F32
        )
        tops = jnp.zeros((64, HEAD), F32)
        totals = jnp.ones((64, HEAD), F32)
        for j in range(GROUP):
            rows = slice(j * 64, (j + 1) * 64)
            obuf[i, :, :, j * HEAD : (j + 1) * HEAD] = mixed[rows, 0:HEAD].reshape(8, 8, HEAD).astype(BF)
            tops = jnp.where(lane == j, top[rows], tops)
            totals = jnp.where(lane == j, mixed[rows, HEAD:], totals)
        stat[i, 0] = tops
        stat[i, 1] = totals

    o_moves = []

    def give(d):
        attend_response(d)
        o_moves.append(net.send(obuf.at[d], robuf.at[4 - d], xdev[d]))
        o_moves.append(net.send(stat.at[d], rstat.at[4 - d], xdev[d]))

    load_k.wait()
    load_v.wait()
    arrived(caches)
    attend_cache(0)
    load_wo.wait()
    own_wo = wo.at[wo_rows, wo_own]
    wo_moves = [net.send(own_wo, own_wo, ydev[d]) for d in (1, 3)]
    arrived([q_moves[0]])
    attend_cache(3)
    arrived([q_moves[1]])
    attend_cache(1)
    arrived([q_moves[2]])
    attend_cache(2)
    arrived(kv_moves)
    kbuf[pl.ds(KEYS_CHIP, RESP), :] = rkv[:, :, :, :, 0:HEAD].astype(F32).reshape(RESP, HEAD).astype(BF)
    vbuf[pl.ds(KEYS_CHIP, RESP), 0:HEAD] = (
        rkv[:, :, :, :, HEAD:].astype(F32).reshape(RESP, HEAD).astype(BF)
    )
    give(2)
    give(3)
    give(1)
    arrived(wo_moves)
    back, ahead = lax.rem(y + 3, 4), lax.rem(y + 1, 4)
    low = wo.at[pl.ds(pl.multiple_of(back * 192, 64), 96), wo_own]
    high = wo.at[pl.ds(pl.multiple_of(ahead * 192 + 96, 32), 96), wo_own]
    wo_moves = [net.send(low, low, ydev[1]), net.send(high, high, ydev[3])]
    attend_response(0)
    arrived(wo_moves)
    wo_cols = wo.at[:, wo_own]
    wo_sib = net.send(wo_cols, wo_cols, sib)
    arrived(o_moves)

    tops = [stat[0, 0]] + [rstat[i, 0] for i in range(1, 4)]
    totals = [stat[0, 1]] + [rstat[i, 1] for i in range(1, 4)]
    top = functools.reduce(jnp.maximum, tops)
    scales = [jnp.exp2((t - top) * LOG2_SCALE) for t in tops]
    total = functools.reduce(jnp.add, [a * b for a, b in zip(scales, totals)])
    scales = [a / total for a in scales]
    for j in range(GROUP):
        cols = slice(j * HEAD, (j + 1) * HEAD)
        mixed = obuf[0, :, :, cols].astype(F32).reshape(64, HEAD) * scales[0][:, j : j + 1]
        for i in range(1, 4):
            mixed = mixed + robuf[i, :, :, cols].astype(F32).reshape(64, HEAD) * scales[i][:, j : j + 1]
        attn[0, :, :, cols] = mixed.reshape(8, 8, HEAD).astype(BF)
    a_moves = [net.send(attn.at[0], attn.at[4 - d], xdev[d]) for d in (2, 1, 3)]
    arrived([wo_sib])
    arrived(a_moves)

    lhs = attn[...].astype(F32).reshape(256, Q_COLS).astype(BF)
    ring = [[], []]

    def z_cols(p):
        base = p * 768
        return pl.ds(base, 768), pl.ds(base, 384), pl.ds(base + 384, 384)

    def z_send(p, d):
        cols, half0, half1 = z_cols(p)
        if d == 4:
            ring[p] = [
                net.send(part.at[4, :, :, half1], zp_buf.at[3, :, :, half1], zdev[1]),
                net.send(part.at[4, :, :, half0], zm_buf.at[3, :, :, half0], zdev[7]),
            ]
        else:
            ring[p] = [
                net.send(part.at[d, :, :, cols], zp_buf.at[d - 1, :, :, cols], zdev[1]),
                net.send(part.at[8 - d, :, :, cols], zm_buf.at[d - 1, :, :, cols], zdev[7]),
            ]

    def z_add(p, d):
        cols, half0, half1 = z_cols(p)
        arrived(ring[p])
        if d == 3:
            add_into(part.at[3, :, :, half1], zp_buf.at[3, :, :, half1])
            add_into(part.at[5, :, :, half0], zm_buf.at[3, :, :, half0])
        elif d > 0:
            add_into(part.at[d, :, :, cols], zp_buf.at[d, :, :, cols])
            add_into(part.at[8 - d, :, :, cols], zm_buf.at[d, :, :, cols])
        else:
            add_into(part.at[0, :, :, cols], zp_buf.at[0, :, :, cols], zm_buf.at[0, :, :, cols])

    for p in range(2):
        cols = slice(p * 768, (p + 1) * 768)
        block = jnp.dot(lhs, wo[:, cols], preferred_element_type=F32).reshape(4, 8, 8, 768)
        for i in range(4):
            part[:, i, :, cols] = block[i].astype(BF)
        z_send(p, 4)
    for d in (3, 2, 1):
        for p in range(2):
            z_add(p, d)
            z_send(p, d)
    p_moves = []
    for p in range(2):
        z_add(p, 0)
        cols = z_cols(p)[0]
        for d in (2, 1, 3):
            p_moves.append(net.send(part.at[0, d, :, cols], px.at[4 - d, :, cols], xdev[d]))
    px[0] = part[0, 0]
    load_res.wait()
    load_gain.wait()
    arrived(p_moves)
    for i in range(4):
        cols = pl.ds(pl.multiple_of(((x + i) & 3) * N_CHIP, HEAD), N_CHIP)
        mid_ref[:, cols] = (res_ref[:, cols].astype(F32) + px[i].astype(F32)).astype(BF)
    net.finish()
    ffn_phase(
        (x, core, z, y), mid_ref, gain_ref, load_up, load_down, out_ref, up_w, down_w, *ffn_refs
    )


def on_device(
    queries,
    cache_keys,
    cache_values,
    response_kv,
    segments,
    residual,
    out_weight,
    norm_gain,
    up_weight,
    down_weight,
):
    hbm = pl.BlockSpec(memory_space=pl.ANY)
    hidden = up_weight.shape[1]
    return pl.pallas_call(
        layer_kernel,
        name="layer",
        out_shape=jax.ShapeDtypeStruct(residual.shape, BF),
        in_specs=[hbm] * 10,
        out_specs=pl.BlockSpec(memory_space=pltpu.VMEM),
        scratch_shapes=[
            pltpu.VMEM(queries.shape, BF),
            pltpu.VMEM(response_kv.shape, BF),
            pltpu.VMEM((16, 128), jnp.int32),
            pltpu.VMEM(residual.shape, BF),
            pltpu.VMEM((1, D), F32),
            pltpu.VMEM(residual.shape, BF),
            pltpu.VMEM((D, hidden), BF),
            pltpu.VMEM((hidden, D), BF),
            pltpu.VMEM((8, 8, 1024), BF),
            pltpu.VMEM((8, 8, 1024), BF),
            pltpu.VMEM((4, GROUP * 64, HEAD), BF),
            pltpu.VMEM((4, GROUP * 64, 2 * HEAD), F32),
            pltpu.VMEM((4, 8, 8, Q_COLS), BF),
            pltpu.VMEM((2, 4, 8, 8, 2 * HEAD), BF),
            pltpu.VMEM((KEYS_CHIP + RESP, HEAD), BF),
            pltpu.VMEM((KEYS_CHIP + RESP, 2 * HEAD), BF),
            pltpu.VMEM((Q_COLS, N_CHIP), BF),
            pltpu.VMEM((4, 8, 8, Q_COLS), BF),
            pltpu.VMEM((4, 2, 64, HEAD), F32),
            pltpu.VMEM((4, 8, 8, Q_COLS), BF),
            pltpu.VMEM((4, 2, 64, HEAD), F32),
            pltpu.VMEM((4, 8, 8, Q_COLS), BF),
            pltpu.VMEM((8, 4, 8, N_CHIP), BF),
            pltpu.VMEM((4, 4, 8, N_CHIP), BF),
            pltpu.VMEM((4, 4, 8, N_CHIP), BF),
            pltpu.VMEM((4, 8, N_CHIP), BF),
            pltpu.SemaphoreType.DMA((10,)),
            pltpu.SemaphoreType.DMA((64,)),
            pltpu.SemaphoreType.DMA((64,)),
            pltpu.VMEM((8, 4, 8, D), BF),
            pltpu.VMEM((8, 4, 8, D), BF),
            pltpu.VMEM((256, hidden), F32),
            pltpu.VMEM((256, hidden), BF),
            pltpu.VMEM((4, 4, 8, A_COLS), BF),
            pltpu.VMEM((4, 4, 8, A_COLS), BF),
            pltpu.VMEM((2, 1, 8, A_COLS), BF),
            pltpu.VMEM((2, 1, 8, A_COLS), BF),
            pltpu.VMEM((2, 8, 8, B_COLS), BF),
            pltpu.VMEM((2, 8, 8, B_COLS), BF),
            pltpu.VMEM((4, 1, 8, B_COLS), BF),
            pltpu.VMEM((4, 1, 8, B_COLS), BF),
            pltpu.SemaphoreType.DMA((N_GATHER,)),
            pltpu.SemaphoreType.DMA((N_GATHER,)),
            pltpu.SemaphoreType.DMA((N_REDUCE,)),
            pltpu.SemaphoreType.DMA((N_REDUCE,)),
        ],
        compiler_params=pltpu.CompilerParams(
            collective_id=0, has_side_effects=True, vmem_limit_bytes=60 * 1024 * 1024
        ),
    )(
        queries, cache_keys, cache_values, response_kv, segments.reshape(16, 128), residual,
        out_weight, norm_gain.reshape(1, D), up_weight, down_weight,
    )


def solution(mesh):
    return jax.shard_map(
        on_device,
        mesh=mesh,
        in_specs=(
            P(("key", "hid"), None),
            P("key", None),
            P("key", None),
            P(("key", "hid"), None),
            P(),
            P(("key", "hid"), None),
            P("hid", "key"),
            P(),
            P(None, "hid"),
            P("hid", None),
        ),
        out_specs=P(("key", "hid"), None),
        check_vma=False,
    )
```

```python
import functools
import math

import jax
import jax.numpy as jnp
from jax import lax
from jax.experimental import pallas as pl
from jax.experimental.pallas import tpu as pltpu
from jax.sharding import PartitionSpec as P

HEADS = 48
KV_HEADS = 8
HEAD = 128
GROUP = 6
D = 6144
MESH = pl.DeviceIdType.MESH
BF = jnp.bfloat16
F32 = jnp.float32

ZI = {0: 0, 1: 1, -1: 2, 2: 3, -2: 4, 3: 5, -3: 6, 4: 7}
YI = {0: 0, 1: 1, -1: 2, 2: 3}
ZGROUPS = (pl.ds(0, 1), pl.ds(1, 2), pl.ds(3, 2), pl.ds(5, 2), pl.ds(7, 1))

A_COLS = 2560
B_COLS = D - A_COLS
CA, A0, A1 = pl.ds(0, A_COLS), pl.ds(0, A_COLS // 2), pl.ds(A_COLS // 2, A_COLS // 2)
CB = pl.ds(A_COLS, B_COLS)
B0, B1 = pl.ds(A_COLS, B_COLS // 2), pl.ds(A_COLS + B_COLS // 2, B_COLS // 2)
LB, L0, L1 = pl.ds(0, B_COLS), pl.ds(0, B_COLS // 2), pl.ds(B_COLS // 2, B_COLS // 2)
N_GATHER = 56
N_REDUCE = 56


class Copies:
    def __init__(self, send_sems, recv_sems):
        self.sems = send_sems, recv_sems
        self.made = []

    def send(self, src, dst, device):
        i = len(self.made)
        copy = pltpu.make_async_remote_copy(
            src_ref=src,
            dst_ref=dst,
            send_sem=self.sems[0].at[i],
            recv_sem=self.sems[1].at[i],
            device_id=device,
            device_id_type=MESH,
        )
        copy.start()
        self.made.append(copy)
        return copy

    def finish(self):
        for copy in self.made:
            copy.wait_send()


def where_am_i():
    key = lax.axis_index("key")
    hid = lax.axis_index("hid")
    return key // 2, key % 2, hid // 4, hid % 4


def device(x, core, z, y):
    return (lax.rem(x, 4) * 2 + core, lax.rem(z, 8) * 4 + lax.rem(y, 4))


def greet(devices):
    barrier = pltpu.get_barrier_semaphore()
    for one in devices:
        pl.semaphore_signal(barrier, inc=1, device_id=one, device_id_type=MESH)
    return lambda: pl.semaphore_wait(barrier, len(devices))


def add_into(dst, *srcs):
    total = dst[...].astype(F32)
    for src in srcs:
        total = total + src[...].astype(F32)
    dst[...] = total.astype(BF)


GATHER_ORDER = (
    "ay1", "bz1", "by10", "az10", "ay2", "az11", "by11", "bz2", "by20", "az20", "az12", "az21",
    "by21", "bz3", "az30", "by12", "az22", "az31", "bz4", "az40", "by13", "az32", "by22", "az41",
    "by14", "az42", "up", "upb", "by23", "by24",
)
REDUCE_ORDER = (
    "az42", "az41", "by04", "az40", "by03", "by02", "by01", "az32", "by00", "by14", "az31", "az30",
    "az22", "by13", "bz4", "by12", "az21", "az20", "az12", "by11", "bz3", "by10", "az11", "ay0",
    "az10", "bz2", "ay1", "bz1",
)
PIECES = (pl.ds(0, 1), pl.ds(1, 2), pl.ds(3, 1))


def ffn_phase(
    where, mid_ref, gain_ref, load_up, load_down, out_ref,
    up_w, down_w, rows, part, acc, act,
    a_zp, a_zm, a_yp, a_ym, b_yp, b_ym, b_zp, b_zm,
    g_send, g_recv, r_send, r_recv,
):
    x, core, z, y = where
    zp, zm = device(x, core, z + 1, y), device(x, core, z + 7, y)
    yp, ym = device(x, core, z, y + 1), device(x, core, z, y + 3)

    wide = mid_ref[...].astype(F32)
    mean = jnp.mean(wide, axis=-1, keepdims=True)
    centred = wide - mean
    var = jnp.mean(centred * centred, axis=-1, keepdims=True)
    rows[0, 0] = (centred * lax.rsqrt(var + 1e-05) * gain_ref[...]).astype(BF)

    net = Copies(g_send, g_recv)
    flying = {}

    def z_hop(hop, ys, cols, half0, half1):
        if hop == 4:
            return (
                net.send(rows.at[ZI[-3], ys, :, half0], rows.at[ZI[4], ys, :, half0], zp),
                net.send(rows.at[ZI[3], ys, :, half1], rows.at[ZI[4], ys, :, half1], zm),
            )
        return (
            net.send(rows.at[ZI[1 - hop], ys, :, cols], rows.at[ZI[-hop], ys, :, cols], zp),
            net.send(rows.at[ZI[hop - 1], ys, :, cols], rows.at[ZI[hop], ys, :, cols], zm),
        )

    def y_first(zs, cols):
        return (
            net.send(rows.at[zs, 0, :, cols], rows.at[zs, YI[-1], :, cols], yp),
            net.send(rows.at[zs, 0, :, cols], rows.at[zs, YI[1], :, cols], ym),
        )

    def y_second(zs, half0, half1):
        return (
            net.send(rows.at[zs, YI[-1], :, half0], rows.at[zs, YI[2], :, half0], yp),
            net.send(rows.at[zs, YI[1], :, half1], rows.at[zs, YI[2], :, half1], ym),
        )

    def az_hop(hop, piece):
        flying["az%d%d" % (hop, piece)] = z_hop(hop, PIECES[piece], CA, A0, A1)

    def bz_hop(hop):
        flying["bz%d" % hop] = z_hop(hop, 0, CB, B0, B1)

    def up_cols(first, size, fresh, low=0, high=8):
        cols = pl.ds(first, size)
        count = (high - low) * 32
        block = rows[low:high, :, :, cols].astype(F32).reshape(count, size).astype(BF)
        product = jnp.dot(block, up_w[cols, :], preferred_element_type=F32)
        if fresh:
            acc[low * 32 : high * 32] = product
        else:
            acc[low * 32 : high * 32] += product

    own = pl.ds(0, 1)
    flying["ay1"] = y_first(own, CA)
    bz_hop(1)
    flying["by10"] = y_first(ZGROUPS[0], CB)
    az_hop(1, 0)
    for name in GATHER_ORDER:
        if name == "up":
            load_up.wait()
            for i in range(2):
                up_cols(i * (A_COLS // 2), A_COLS // 2, i == 0)
            continue
        if name == "upb":
            for i in range(2):
                up_cols(A_COLS + i * (B_COLS // 2), B_COLS // 2, False, 0, 5)
            continue
        for copy in flying[name]:
            copy.wait_recv()
        kind, step = name[:2], int(name[2])
        if kind == "ay" and step == 1:
            flying["ay2"] = y_second(own, A0, A1)
            az_hop(1, 1)
        elif kind == "ay":
            az_hop(1, 2)
        elif kind == "az" and step < 4:
            az_hop(step + 1, int(name[3]))
        elif kind == "bz":
            if step < 4:
                bz_hop(step + 1)
            flying["by1%d" % step] = y_first(ZGROUPS[step], CB)
        elif kind == "by" and step == 1:
            flying["by2" + name[3]] = y_second(ZGROUPS[int(name[3])], B0, B1)

    for i in range(2):
        up_cols(A_COLS + i * (B_COLS // 2), B_COLS // 2, False, 5, 8)
    up = jnp.maximum(acc[...], 0.0)
    act[...] = (up * up).astype(BF)
    load_down.wait()

    def down_cols(first, size):
        cols = pl.ds(first, size)
        block = jnp.dot(act[...], down_w[:, cols], preferred_element_type=F32)
        part[:, :, :, cols] = block.reshape(8, 4, 8, size).astype(BF)

    net.finish()
    net = Copies(r_send, r_recv)
    flying = {}
    done = set()

    def z_send(d, ys, cols, half0, half1, lcols, lh0, lh1, got_p, got_m, lys):
        if d == 4:
            return (
                net.send(part.at[ZI[4], ys, :, half1], got_p.at[3, lys, :, lh1], zp),
                net.send(part.at[ZI[4], ys, :, half0], got_m.at[3, lys, :, lh0], zm),
            )
        return (
            net.send(part.at[ZI[d], ys, :, cols], got_p.at[d - 1, lys, :, lcols], zp),
            net.send(part.at[ZI[-d], ys, :, cols], got_m.at[d - 1, lys, :, lcols], zm),
        )

    def z_add(d, ys, cols, half0, half1, lcols, lh0, lh1, got_p, got_m, lys):
        if d == 3:
            add_into(part.at[ZI[3], ys, :, half1], got_p.at[3, lys, :, lh1])
            add_into(part.at[ZI[-3], ys, :, half0], got_m.at[3, lys, :, lh0])
        elif d > 0:
            add_into(part.at[ZI[d], ys, :, cols], got_p.at[d, lys, :, lcols])
            add_into(part.at[ZI[-d], ys, :, cols], got_m.at[d, lys, :, lcols])
        else:
            add_into(
                part.at[0, ys, :, cols], got_p.at[0, lys, :, lcols], got_m.at[0, lys, :, lcols]
            )

    def y_send(step, zs, cols, half0, half1, lcols, lh0, lh1, got_p, got_m):
        if step == 0:
            return (
                net.send(part.at[zs, YI[2], :, half1], got_p.at[1, zs, :, lh1], yp),
                net.send(part.at[zs, YI[2], :, half0], got_m.at[1, zs, :, lh0], ym),
            )
        return (
            net.send(part.at[zs, YI[1], :, cols], got_p.at[0, zs, :, lcols], yp),
            net.send(part.at[zs, YI[-1], :, cols], got_m.at[0, zs, :, lcols], ym),
        )

    def y_add(step, zs, cols, half0, half1, lcols, lh0, lh1, got_p, got_m):
        if step == 0:
            add_into(part.at[zs, YI[1], :, half1], got_p.at[1, zs, :, lh1])
            add_into(part.at[zs, YI[-1], :, half0], got_m.at[1, zs, :, lh0])
        else:
            add_into(part.at[zs, 0, :, cols], got_p.at[0, zs, :, lcols], got_m.at[0, zs, :, lcols])

    za = [(p, CA, A0, A1, CA, A0, A1, a_zp, a_zm, p) for p in PIECES]
    zb = (0, CB, B0, B1, LB, L0, L1, b_zp, b_zm, 0)
    yb = (CB, B0, B1, LB, L0, L1, b_yp, b_ym)
    ya = (CA, A0, A1, CA, A0, A1, a_yp, a_ym)

    for i in range(2):
        down_cols(i * (A_COLS // 2), A_COLS // 2)
    for p in (2, 1, 0):
        flying["az4%d" % p] = z_send(4, *za[p])
    for i in range(2):
        down_cols(A_COLS + i * (B_COLS // 2), B_COLS // 2)
    for g in (4, 3, 2, 1, 0):
        flying["by0%d" % g] = y_send(0, ZGROUPS[g], *yb)
    for name in REDUCE_ORDER:
        for copy in flying[name]:
            copy.wait_recv()
        done.add(name)
        kind, step = name[:2], int(name[2])
        if kind == "az":
            p = int(name[3])
            z_add(step - 1, *za[p])
            if step > 1:
                flying["az%d%d" % (step - 1, p)] = z_send(step - 1, *za[p])
            elif p == 2:
                flying["ay0"] = y_send(0, own, *ya)
        elif kind == "by" and step == 0:
            y_add(0, ZGROUPS[int(name[3])], *yb)
            flying["by1" + name[3]] = y_send(1, ZGROUPS[int(name[3])], *yb)
        elif kind == "by":
            y_add(1, ZGROUPS[int(name[3])], *yb)
        elif kind == "bz" and step > 1:
            z_add(step - 1, *zb)
        elif kind == "ay" and step == 0:
            y_add(0, own, *ya)
        for d in (4, 3, 2, 1):
            if "bz%d" % d not in flying and "by1%d" % d in done and (d == 4 or "bz%d" % (d + 1) in done):
                flying["bz%d" % d] = z_send(d, *zb)
        if "ay1" not in flying and "ay0" in done and "az11" in done:
            flying["ay1"] = y_send(1, own, *ya)
        if name == "ay1":
            out_ref[:, CA] = (
                mid_ref[:, CA].astype(F32)
                + part[0, 0, :, CA].astype(F32)
                + a_yp[0, 0].astype(F32)
                + a_ym[0, 0].astype(F32)
            ).astype(BF)
        if name == "bz1":
            out_ref[:, CB] = (
                mid_ref[:, CB].astype(F32)
                + part[0, 0, :, CB].astype(F32)
                + b_zp[0, 0].astype(F32)
                + b_zm[0, 0].astype(F32)
            ).astype(BF)
    net.finish()


LOG2_SCALE = math.log2(math.e) / math.sqrt(HEAD)
Q_COLS = GROUP * HEAD
KEYS_OWN = 768
KEYS_CHIP = 2 * KEYS_OWN
RESP = 512
N_CHIP = 1536


def layer_kernel(
    q_hbm, ck_hbm, cv_hbm, rkv_hbm, seg_hbm, res_hbm, wo_hbm, gain_hbm, up_hbm, down_hbm, out_ref,
    q_ref, rkv_ref, seg_ref, res_ref, gain_ref, mid_ref, up_w, down_w,
    packed, got, qcat, osum, qall, rkv, kbuf, vbuf, wo, obuf, stat, robuf, rstat, attn, part, zp_buf, zm_buf,
    px, local_sem, s_sem, r_sem, *ffn_refs,
):
    x, core, z, y = where_am_i()
    sib = device(x, 1 - core, z, y)
    zdev = [device(x, core, z + d, y) for d in range(8)]
    xdev = [device(x + d, core, z, y) for d in range(4)]
    ydev = [device(x, core, z, y + d) for d in range(4)]
    ysib = [device(x, 1 - core, z, y + d) for d in range(4)]
    all_here = greet([*zdev[1:], *xdev[1:], *ydev[1:], *ysib])
    head = pl.ds(pl.multiple_of(z * HEAD, HEAD), HEAD)
    wo_rows = pl.ds(pl.multiple_of(y * 192, 64), 192)
    wo_own = pl.ds(pl.multiple_of(core * 768, 128), 768)

    loads = [
        pltpu.make_async_copy(src, dst, local_sem.at[3 + i])
        for i, (src, dst) in enumerate(
            (
                (q_hbm, q_ref),
                (rkv_hbm, rkv_ref),
                (seg_hbm, seg_ref),
                (res_hbm, res_ref),
                (gain_hbm, gain_ref),
                (up_hbm, up_w),
                (down_hbm, down_w),
            )
        )
    ]
    load_q, load_rkv, load_seg, load_res, load_gain, load_up, load_down = loads
    load_q.start()
    load_rkv.start()
    load_k = pltpu.make_async_copy(ck_hbm.at[:, head], kbuf.at[pl.ds(0, KEYS_OWN)], local_sem.at[0])
    load_v = pltpu.make_async_copy(
        cv_hbm.at[:, head], vbuf.at[pl.ds(0, KEYS_OWN), pl.ds(0, HEAD)], local_sem.at[1]
    )
    load_wo = pltpu.make_async_copy(wo_hbm, wo.at[wo_rows, wo_own], local_sem.at[2])
    load_k.start()
    load_v.start()
    load_wo.start()
    for load in (load_seg, load_res, load_gain):
        load.start()
    load_q.wait()
    load_rkv.wait()
    for i in range(8):
        packed[i, :, 0:Q_COLS] = q_ref[:, i * Q_COLS : (i + 1) * Q_COLS]
        packed[i, :, Q_COLS : Q_COLS + HEAD] = rkv_ref[:, i * HEAD : (i + 1) * HEAD]
        packed[i, :, Q_COLS + HEAD :] = rkv_ref[:, 1024 + i * HEAD : 1024 + (i + 1) * HEAD]
    all_here()
    net = Copies(s_sem, r_sem)

    def arrived(copies):
        for copy in copies:
            copy.wait_recv()

    moves = [
        net.send(packed.at[lax.rem(z + d, 8)], got.at[8 - d], zdev[d]) for d in (4, 3, 5, 2, 6, 1, 7)
    ]
    caches = [
        net.send(ck_hbm.at[:, head], kbuf.at[pl.ds(KEYS_OWN, KEYS_OWN)], sib),
        net.send(cv_hbm.at[:, head], vbuf.at[pl.ds(KEYS_OWN, KEYS_OWN), pl.ds(0, HEAD)], sib),
    ]
    got[0] = packed[z]
    vbuf[:, HEAD:] = jnp.ones((KEYS_CHIP + RESP, HEAD), BF)
    arrived(moves)
    rkv[0, 0] = got[:, :, Q_COLS:]
    kv_moves = [net.send(rkv.at[0, 0], rkv.at[0, 4 - d], ydev[d]) for d in (2, 1, 3)]
    kv_moves += [net.send(rkv.at[0, 0], rkv.at[1, (4 - d) % 4], ysib[d]) for d in (2, 1, 3, 0)]
    qall[0] = got[:, :, 0:Q_COLS]
    q_moves = [net.send(qall.at[0], qall.at[4 - d], xdev[d]) for d in (1, 3, 2)]

    load_seg.wait()
    seg = seg_ref[...]
    bounds = [
        jnp.sum(jnp.where(seg < s, 1, 0), keepdims=True) for s in (1, 2, 3)
    ]
    lanes = lax.broadcasted_iota(jnp.int32, (1, RESP), 1)
    key_row = (
        (2 * x + ((core + lanes // 256) & 1)) * 32
        + ((z + (lanes // 8)) & 7) * 4
        + ((y + (lanes // 64)) & 3)
    ) * 8 + (lanes & 7)
    slots = lax.broadcasted_iota(jnp.int32, (64, 1), 0)

    load_up.start()
    load_down.start()
    nt = (((1,), (1,)), ((), ()))
    lane = lax.broadcasted_iota(jnp.int32, (64, HEAD), 1)
    wide_lane = lax.broadcasted_iota(jnp.int32, (GROUP * 64, HEAD), 1)

    def attend_cache(i):
        wide = qall[i].astype(F32)
        q = jnp.concatenate(
            [wide[:, :, j * HEAD : (j + 1) * HEAD].reshape(64, HEAD) for j in range(GROUP)], 0
        ).astype(BF)
        qcat[i] = q
        score = lax.dot_general(q, kbuf[0:KEYS_CHIP, :], nt, preferred_element_type=F32)
        top = jnp.max(score, axis=-1, keepdims=True)
        weight = jnp.exp2((score - top) * LOG2_SCALE).astype(BF)
        mixed = jnp.dot(weight, vbuf[0:KEYS_CHIP, :], preferred_element_type=F32)
        osum[i, :, 0:HEAD] = mixed[:, 0:HEAD]
        osum[i, :, HEAD:] = jnp.where(wide_lane < 64, mixed[:, HEAD:], top)

    def attend_response(i):
        q_row = ((2 * ((x + i) & 3) + core) * 32 + ((z + slots // 8) & 7) * 4 + y) * 8 + (slots & 7)
        start = jnp.zeros_like(q_row)
        for bound in bounds:
            start = jnp.maximum(start, jnp.where(q_row >= bound, bound, 0))
        seen = (key_row <= q_row) & (key_row >= start)
        seen = jnp.concatenate([jnp.where(seen, 0.0, -jnp.inf)] * GROUP, 0)
        score = lax.dot_general(qcat[i], kbuf[KEYS_CHIP:, :], nt, preferred_element_type=F32) + seen
        first_top = osum[i, :, 2 * HEAD - 1 : 2 * HEAD]
        top = jnp.maximum(first_top, jnp.max(score, axis=-1, keepdims=True))
        weight = jnp.exp2((score - top) * LOG2_SCALE).astype(BF)
        mixed = osum[i] * jnp.exp2((first_top - top) * LOG2_SCALE) + jnp.dot(
            weight, vbuf[KEYS_CHIP:, :], preferred_element_type=F32
        )
        both = jnp.ones((64, HEAD), F32)
        for j in range(GROUP):
            rows = slice(j * 64, (j + 1) * 64)
            obuf[i, :, :, j * HEAD : (j + 1) * HEAD] = mixed[rows, 0:HEAD].reshape(8, 8, HEAD).astype(BF)
            both = jnp.where((lane & 31) == j, top[rows], both)
            both = jnp.where((lane & 31) == 8 + j, mixed[rows, HEAD : HEAD + 1], both)
        for g in range(4):
            quarter = both[g * 16 : (g + 1) * 16]
            packed_stat = quarter if g == 0 else jnp.where(lane[0:16] >= 32 * g, quarter, packed_stat)
        stat[i] = packed_stat

    o_moves = []

    def give(d):
        attend_response(d)
        o_moves.append(net.send(obuf.at[d], robuf.at[4 - d], xdev[d]))
        o_moves.append(net.send(stat.at[d], rstat.at[4 - d], xdev[d]))

    load_k.wait()
    load_v.wait()
    arrived(caches)
    attend_cache(0)
    load_wo.wait()
    own_wo = wo.at[wo_rows, wo_own]
    wo_moves = [net.send(own_wo, own_wo, ydev[d]) for d in (1, 3)]
    arrived([q_moves[2]])
    attend_cache(2)
    arrived(kv_moves)
    kbuf[pl.ds(KEYS_CHIP, RESP), :] = rkv[:, :, :, :, 0:HEAD].astype(F32).reshape(RESP, HEAD).astype(BF)
    vbuf[pl.ds(KEYS_CHIP, RESP), 0:HEAD] = (
        rkv[:, :, :, :, HEAD:].astype(F32).reshape(RESP, HEAD).astype(BF)
    )
    give(2)
    arrived([q_moves[0]])
    attend_cache(3)
    give(3)
    arrived([q_moves[1]])
    attend_cache(1)
    give(1)
    arrived(wo_moves)
    back, ahead = lax.rem(y + 3, 4), lax.rem(y + 1, 4)
    low = wo.at[pl.ds(pl.multiple_of(back * 192, 64), 96), wo_own]
    high = wo.at[pl.ds(pl.multiple_of(ahead * 192 + 96, 32), 96), wo_own]
    wo_moves = [net.send(low, low, ydev[1]), net.send(high, high, ydev[3])]
    attend_response(0)
    arrived(wo_moves)
    wo_cols = wo.at[:, wo_own]
    wo_sib = net.send(wo_cols, wo_cols, sib)
    arrived(o_moves)

    def unpacked(tile, shift):
        parts = [(tile, (HEAD - 32 * g - shift) % HEAD) for g in range(4)]
        return jnp.concatenate([pltpu.roll(t, by, 1) if by else t for t, by in parts], 0)

    tiles = [stat[0]] + [rstat[i] for i in range(1, 4)]
    tops = [unpacked(t, 0) for t in tiles]
    totals = [unpacked(t, 8) for t in tiles]
    top = functools.reduce(jnp.maximum, tops)
    scales = [jnp.exp2((t - top) * LOG2_SCALE) for t in tops]
    total = functools.reduce(jnp.add, [a * b for a, b in zip(scales, totals)])
    scales = [a / total for a in scales]
    for j in range(GROUP):
        cols = slice(j * HEAD, (j + 1) * HEAD)
        mixed = obuf[0, :, :, cols].astype(F32).reshape(64, HEAD) * scales[0][:, j : j + 1]
        for i in range(1, 4):
            mixed = mixed + robuf[i, :, :, cols].astype(F32).reshape(64, HEAD) * scales[i][:, j : j + 1]
        attn[0, :, :, cols] = mixed.reshape(8, 8, HEAD).astype(BF)
    a_moves = [net.send(attn.at[0], attn.at[4 - d], xdev[d]) for d in (2, 1, 3)]
    arrived([wo_sib])
    ring = {}

    far0, far1 = slice(0, 768), slice(768, N_CHIP)

    def project(*slots):
        count = 64 * len(slots)
        lhs = jnp.concatenate([attn[i].astype(F32).reshape(64, Q_COLS) for i in slots], 0).astype(BF)
        for p in range(2):
            cols = slice(p * 768, (p + 1) * 768)
            block = jnp.dot(lhs, wo[:, cols], preferred_element_type=F32)
            for k, i in enumerate(slots):
                part[:, i, :, cols] = block[k * 64 : (k + 1) * 64].reshape(8, 8, 768).astype(BF)
        for i in slots:
            ring[i] = [
                net.send(part.at[4, i, :, far1], zp_buf.at[3, i, :, far1], zdev[2]),
                net.send(part.at[4, i, :, far0], zm_buf.at[3, i, :, far0], zdev[6]),
                net.send(part.at[3, i], zp_buf.at[1, i], zdev[1]),
                net.send(part.at[5, i], zm_buf.at[1, i], zdev[7]),
            ]

    def relay(i):
        arrived(ring[i])
        add_into(part.at[2, i], zp_buf.at[1, i])
        add_into(part.at[2, i, :, far1], zp_buf.at[3, i, :, far1])
        add_into(part.at[6, i], zm_buf.at[1, i])
        add_into(part.at[6, i, :, far0], zm_buf.at[3, i, :, far0])
        ring[i] = [
            net.send(part.at[2, i], zp_buf.at[2, i], zdev[2]),
            net.send(part.at[6, i], zm_buf.at[2, i], zdev[6]),
            net.send(part.at[1, i], zp_buf.at[0, i], zdev[1]),
            net.send(part.at[7, i], zm_buf.at[0, i], zdev[7]),
        ]

    p_moves = []

    def settle(i):
        arrived(ring[i])
        add_into(
            part.at[0, i], zp_buf.at[0, i], zm_buf.at[0, i], zp_buf.at[2, i], zm_buf.at[2, i]
        )
        if i > 0:
            p_moves.append(net.send(part.at[0, i], px.at[4 - i], xdev[i]))

    project(0)
    arrived([a_moves[1], a_moves[2]])
    project(1, 3)
    relay(0)
    arrived([a_moves[0]])
    project(2)
    relay(1)
    relay(3)
    relay(2)
    settle(0)
    settle(1)
    settle(3)
    settle(2)
    px[0] = part[0, 0]
    load_res.wait()
    load_gain.wait()
    arrived(p_moves)
    for i in range(4):
        cols = pl.ds(pl.multiple_of(((x + i) & 3) * N_CHIP, HEAD), N_CHIP)
        mid_ref[:, cols] = (res_ref[:, cols].astype(F32) + px[i].astype(F32)).astype(BF)
    net.finish()
    ffn_phase(
        (x, core, z, y), mid_ref, gain_ref, load_up, load_down, out_ref, up_w, down_w, *ffn_refs
    )


def on_device(
    queries,
    cache_keys,
    cache_values,
    response_kv,
    segments,
    residual,
    out_weight,
    norm_gain,
    up_weight,
    down_weight,
):
    hbm = pl.BlockSpec(memory_space=pl.ANY)
    hidden = up_weight.shape[1]
    return pl.pallas_call(
        layer_kernel,
        name="layer",
        out_shape=jax.ShapeDtypeStruct(residual.shape, BF),
        in_specs=[hbm] * 10,
        out_specs=pl.BlockSpec(memory_space=pltpu.VMEM),
        scratch_shapes=[
            pltpu.VMEM(queries.shape, BF),
            pltpu.VMEM(response_kv.shape, BF),
            pltpu.VMEM((16, 128), jnp.int32),
            pltpu.VMEM(residual.shape, BF),
            pltpu.VMEM((1, D), F32),
            pltpu.VMEM(residual.shape, BF),
            pltpu.VMEM((D, hidden), BF),
            pltpu.VMEM((hidden, D), BF),
            pltpu.VMEM((8, 8, 1024), BF),
            pltpu.VMEM((8, 8, 1024), BF),
            pltpu.VMEM((4, GROUP * 64, HEAD), BF),
            pltpu.VMEM((4, GROUP * 64, 2 * HEAD), F32),
            pltpu.VMEM((4, 8, 8, Q_COLS), BF),
            pltpu.VMEM((2, 4, 8, 8, 2 * HEAD), BF),
            pltpu.VMEM((KEYS_CHIP + RESP, HEAD), BF),
            pltpu.VMEM((KEYS_CHIP + RESP, 2 * HEAD), BF),
            pltpu.VMEM((Q_COLS, N_CHIP), BF),
            pltpu.VMEM((4, 8, 8, Q_COLS), BF),
            pltpu.VMEM((4, 16, HEAD), F32),
            pltpu.VMEM((4, 8, 8, Q_COLS), BF),
            pltpu.VMEM((4, 16, HEAD), F32),
            pltpu.VMEM((4, 8, 8, Q_COLS), BF),
            pltpu.VMEM((8, 4, 8, N_CHIP), BF),
            pltpu.VMEM((4, 4, 8, N_CHIP), BF),
            pltpu.VMEM((4, 4, 8, N_CHIP), BF),
            pltpu.VMEM((4, 8, N_CHIP), BF),
            pltpu.SemaphoreType.DMA((10,)),
            pltpu.SemaphoreType.DMA((72,)),
            pltpu.SemaphoreType.DMA((72,)),
            pltpu.VMEM((8, 4, 8, D), BF),
            pltpu.VMEM((8, 4, 8, D), BF),
            pltpu.VMEM((256, hidden), F32),
            pltpu.VMEM((256, hidden), BF),
            pltpu.VMEM((4, 4, 8, A_COLS), BF),
            pltpu.VMEM((4, 4, 8, A_COLS), BF),
            pltpu.VMEM((2, 1, 8, A_COLS), BF),
            pltpu.VMEM((2, 1, 8, A_COLS), BF),
            pltpu.VMEM((2, 8, 8, B_COLS), BF),
            pltpu.VMEM((2, 8, 8, B_COLS), BF),
            pltpu.VMEM((4, 1, 8, B_COLS), BF),
            pltpu.VMEM((4, 1, 8, B_COLS), BF),
            pltpu.SemaphoreType.DMA((N_GATHER,)),
            pltpu.SemaphoreType.DMA((N_GATHER,)),
            pltpu.SemaphoreType.DMA((N_REDUCE,)),
            pltpu.SemaphoreType.DMA((N_REDUCE,)),
        ],
        compiler_params=pltpu.CompilerParams(
            collective_id=0, has_side_effects=True, vmem_limit_bytes=60 * 1024 * 1024
        ),
    )(
        queries, cache_keys, cache_values, response_kv, segments.reshape(16, 128), residual,
        out_weight, norm_gain.reshape(1, D), up_weight, down_weight,
    )


def solution(mesh):
    return jax.shard_map(
        on_device,
        mesh=mesh,
        in_specs=(
            P(("key", "hid"), None),
            P("key", None),
            P("key", None),
            P(("key", "hid"), None),
            P(),
            P(("key", "hid"), None),
            P("hid", "key"),
            P(),
            P(None, "hid"),
            P("hid", None),
        ),
        out_specs=P(("key", "hid"), None),
        check_vma=False,
    )
```

```python
import functools
import math

import jax
import jax.numpy as jnp
from jax import lax
from jax.experimental import pallas as pl
from jax.experimental.pallas import tpu as pltpu
from jax.sharding import PartitionSpec as P

HEADS = 48
KV_HEADS = 8
HEAD = 128
GROUP = 6
D = 6144
MESH = pl.DeviceIdType.MESH
BF = jnp.bfloat16
F32 = jnp.float32

ZI = {0: 0, 1: 1, -1: 2, 2: 3, -2: 4, 3: 5, -3: 6, 4: 7}
YI = {0: 0, 1: 1, -1: 2, 2: 3}
ZGROUPS = (pl.ds(0, 1), pl.ds(1, 2), pl.ds(3, 2), pl.ds(5, 2), pl.ds(7, 1))

A_COLS = 2304
B_COLS = D - A_COLS
CA, A0, A1 = pl.ds(0, A_COLS), pl.ds(0, A_COLS // 2), pl.ds(A_COLS // 2, A_COLS // 2)
CB = pl.ds(A_COLS, B_COLS)
B0, B1 = pl.ds(A_COLS, B_COLS // 2), pl.ds(A_COLS + B_COLS // 2, B_COLS // 2)
LB, L0, L1 = pl.ds(0, B_COLS), pl.ds(0, B_COLS // 2), pl.ds(B_COLS // 2, B_COLS // 2)
N_GATHER = 56
N_REDUCE = 56


class Copies:
    def __init__(self, send_sems, recv_sems):
        self.sems = send_sems, recv_sems
        self.made = []

    def send(self, src, dst, device):
        i = len(self.made)
        copy = pltpu.make_async_remote_copy(
            src_ref=src,
            dst_ref=dst,
            send_sem=self.sems[0].at[i],
            recv_sem=self.sems[1].at[i],
            device_id=device,
            device_id_type=MESH,
        )
        copy.start()
        self.made.append(copy)
        return copy

    def finish(self):
        for copy in self.made:
            copy.wait_send()


def where_am_i():
    key = lax.axis_index("key")
    hid = lax.axis_index("hid")
    return key // 2, key % 2, hid // 4, hid % 4


def device(x, core, z, y):
    return (lax.rem(x, 4) * 2 + core, lax.rem(z, 8) * 4 + lax.rem(y, 4))


def greet(devices):
    barrier = pltpu.get_barrier_semaphore()
    for one in devices:
        pl.semaphore_signal(barrier, inc=1, device_id=one, device_id_type=MESH)
    return lambda: pl.semaphore_wait(barrier, len(devices))


def add_into(dst, *srcs):
    total = dst[...].astype(F32)
    for src in srcs:
        total = total + src[...].astype(F32)
    dst[...] = total.astype(BF)


GATHER_ORDER = (
    "ay1", "bz1", "by10", "ay2", "bz2", "az10", "az11", "by11", "az12", "by20", "bz3", "by12",
    "bz4", "az20", "by21", "az21", "az22", "by13", "az30", "by22", "az31", "by14", "az32", "up",
    "az40", "by23", "az41", "by24", "az42",
)
REDUCE_ORDER = (
    "az42", "by04", "az41", "az40", "by03", "by02", "az32", "by01", "az31", "by00", "az30", "by14",
    "az22", "by13", "az21", "az20", "by12", "bz4", "az12", "bz3", "by11", "az11", "by10", "az10",
    "ay0", "bz2", "ay1", "bz1",
)
BZ_NEEDS = {4: ("by14",), 3: ("by13",), 2: ("by12", "bz3", "bz4"), 1: ("by11",)}
PIECES = (pl.ds(0, 1), pl.ds(1, 2), pl.ds(3, 1))


def ffn_phase(
    where, mid_ref, gain_ref, load_up, load_down, out_ref,
    up_w, down_w, rows, part, acc, act,
    a_zp, a_zm, a_yp, a_ym, b_yp, b_ym, b_zp, b_zm,
    g_send, g_recv, r_send, r_recv,
):
    x, core, z, y = where
    zp, zm = device(x, core, z + 1, y), device(x, core, z + 7, y)
    yp, ym = device(x, core, z, y + 1), device(x, core, z, y + 3)
    zp2, zm2 = device(x, core, z + 2, y), device(x, core, z + 6, y)

    wide = mid_ref[...].astype(F32)
    mean = jnp.mean(wide, axis=-1, keepdims=True)
    centred = wide - mean
    var = jnp.mean(centred * centred, axis=-1, keepdims=True)
    rows[0, 0] = (centred * lax.rsqrt(var + 1e-05) * gain_ref[...]).astype(BF)

    net = Copies(g_send, g_recv)
    flying = {}

    def z_hop(hop, ys, cols, half0, half1):
        if hop == 4:
            return (
                net.send(rows.at[ZI[-3], ys, :, half0], rows.at[ZI[4], ys, :, half0], zp),
                net.send(rows.at[ZI[3], ys, :, half1], rows.at[ZI[4], ys, :, half1], zm),
            )
        return (
            net.send(rows.at[ZI[1 - hop], ys, :, cols], rows.at[ZI[-hop], ys, :, cols], zp),
            net.send(rows.at[ZI[hop - 1], ys, :, cols], rows.at[ZI[hop], ys, :, cols], zm),
        )

    def y_first(zs, cols):
        return (
            net.send(rows.at[zs, 0, :, cols], rows.at[zs, YI[-1], :, cols], yp),
            net.send(rows.at[zs, 0, :, cols], rows.at[zs, YI[1], :, cols], ym),
        )

    def y_second(zs, half0, half1):
        return (
            net.send(rows.at[zs, YI[-1], :, half0], rows.at[zs, YI[2], :, half0], yp),
            net.send(rows.at[zs, YI[1], :, half1], rows.at[zs, YI[2], :, half1], ym),
        )

    def az_hop(hop, piece):
        flying["az%d%d" % (hop, piece)] = z_hop(hop, PIECES[piece], CA, A0, A1)

    def bz_hop(hop):
        if hop == 1:
            pair = z_hop(1, 0, CB, B0, B1)
        elif hop == 2:
            pair = (
                net.send(rows.at[0, 0, :, CB], rows.at[ZI[-2], 0, :, CB], zp2),
                net.send(rows.at[0, 0, :, CB], rows.at[ZI[2], 0, :, CB], zm2),
            )
        elif hop == 3:
            pair = z_hop(3, 0, CB, B0, B1)
        else:
            pair = (
                net.send(rows.at[ZI[-2], 0, :, B0], rows.at[ZI[4], 0, :, B0], zp2),
                net.send(rows.at[ZI[2], 0, :, B1], rows.at[ZI[4], 0, :, B1], zm2),
            )
        flying["bz%d" % hop] = pair

    def up_cols(first, size, fresh, low, high):
        cols = pl.ds(first, size)
        count = (high - low) * 32
        block = rows[low:high, :, :, cols].astype(F32).reshape(count, size).astype(BF)
        product = jnp.dot(block, up_w[cols, :], preferred_element_type=F32)
        if fresh:
            acc[low * 32 : high * 32] = product
        else:
            acc[low * 32 : high * 32] += product

    def up_rows(low, high):
        for i in range(2):
            up_cols(i * (A_COLS // 2), A_COLS // 2, i == 0, low, high)
        for i in range(2):
            up_cols(A_COLS + i * (B_COLS // 2), B_COLS // 2, False, low, high)

    own = pl.ds(0, 1)
    flying["ay1"] = y_first(own, CA)
    bz_hop(1)
    bz_hop(2)
    flying["by10"] = y_first(ZGROUPS[0], CB)
    az_hop(1, 0)
    for name in GATHER_ORDER:
        if name == "up":
            load_up.wait()
            up_rows(0, 5)
            continue
        for copy in flying[name]:
            copy.wait_recv()
        kind, step = name[:2], int(name[2])
        if kind == "ay" and step == 1:
            flying["ay2"] = y_second(own, A0, A1)
            az_hop(1, 1)
        elif kind == "ay":
            az_hop(1, 2)
        elif kind == "az" and step < 4:
            az_hop(step + 1, int(name[3]))
        elif kind == "bz":
            if step == 2:
                bz_hop(3)
                bz_hop(4)
            flying["by1%d" % step] = y_first(ZGROUPS[step], CB)
        elif kind == "by" and step == 1:
            flying["by2" + name[3]] = y_second(ZGROUPS[int(name[3])], B0, B1)

    up_rows(5, 8)
    up = jnp.maximum(acc[...], 0.0)
    act[...] = (up * up).astype(BF)
    load_down.wait()

    def down_cols(first, size):
        cols = pl.ds(first, size)
        block = jnp.dot(act[...], down_w[:, cols], preferred_element_type=F32)
        part[:, :, :, cols] = block.reshape(8, 4, 8, size).astype(BF)

    net.finish()
    net = Copies(r_send, r_recv)
    flying = {}
    done = set()

    def z_send(d, ys, cols, half0, half1, lcols, lh0, lh1, got_p, got_m, lys):
        if d == 4:
            return (
                net.send(part.at[ZI[4], ys, :, half1], got_p.at[3, lys, :, lh1], zp),
                net.send(part.at[ZI[4], ys, :, half0], got_m.at[3, lys, :, lh0], zm),
            )
        return (
            net.send(part.at[ZI[d], ys, :, cols], got_p.at[d - 1, lys, :, lcols], zp),
            net.send(part.at[ZI[-d], ys, :, cols], got_m.at[d - 1, lys, :, lcols], zm),
        )

    def z_add(d, ys, cols, half0, half1, lcols, lh0, lh1, got_p, got_m, lys):
        if d == 3:
            add_into(part.at[ZI[3], ys, :, half1], got_p.at[3, lys, :, lh1])
            add_into(part.at[ZI[-3], ys, :, half0], got_m.at[3, lys, :, lh0])
        elif d > 0:
            add_into(part.at[ZI[d], ys, :, cols], got_p.at[d, lys, :, lcols])
            add_into(part.at[ZI[-d], ys, :, cols], got_m.at[d, lys, :, lcols])
        else:
            add_into(
                part.at[0, ys, :, cols], got_p.at[0, lys, :, lcols], got_m.at[0, lys, :, lcols]
            )

    def y_send(step, zs, cols, half0, half1, lcols, lh0, lh1, got_p, got_m):
        if step == 0:
            return (
                net.send(part.at[zs, YI[2], :, half1], got_p.at[1, zs, :, lh1], yp),
                net.send(part.at[zs, YI[2], :, half0], got_m.at[1, zs, :, lh0], ym),
            )
        return (
            net.send(part.at[zs, YI[1], :, cols], got_p.at[0, zs, :, lcols], yp),
            net.send(part.at[zs, YI[-1], :, cols], got_m.at[0, zs, :, lcols], ym),
        )

    def y_add(step, zs, cols, half0, half1, lcols, lh0, lh1, got_p, got_m):
        if step == 0:
            add_into(part.at[zs, YI[1], :, half1], got_p.at[1, zs, :, lh1])
            add_into(part.at[zs, YI[-1], :, half0], got_m.at[1, zs, :, lh0])
        else:
            add_into(part.at[zs, 0, :, cols], got_p.at[0, zs, :, lcols], got_m.at[0, zs, :, lcols])

    za = [(p, CA, A0, A1, CA, A0, A1, a_zp, a_zm, p) for p in PIECES]

    def bz_send(d):
        slot, ahead, behind = {1: (0, zp, zm), 2: (2, zp2, zm2), 3: (1, zp, zm), 4: (3, zp2, zm2)}[d]
        if d == 4:
            return (
                net.send(part.at[ZI[4], 0, :, B1], b_zp.at[slot, 0, :, L1], ahead),
                net.send(part.at[ZI[4], 0, :, B0], b_zm.at[slot, 0, :, L0], behind),
            )
        return (
            net.send(part.at[ZI[d], 0, :, CB], b_zp.at[slot, 0], ahead),
            net.send(part.at[ZI[-d], 0, :, CB], b_zm.at[slot, 0], behind),
        )

    def bz_add(d):
        if d == 4:
            add_into(part.at[ZI[2], 0, :, B1], b_zp.at[3, 0, :, L1])
            add_into(part.at[ZI[-2], 0, :, B0], b_zm.at[3, 0, :, L0])
        elif d == 3:
            add_into(part.at[ZI[2], 0, :, CB], b_zp.at[1, 0])
            add_into(part.at[ZI[-2], 0, :, CB], b_zm.at[1, 0])

    yb = (CB, B0, B1, LB, L0, L1, b_yp, b_ym)
    ya = (CA, A0, A1, CA, A0, A1, a_yp, a_ym)

    for i in range(2):
        down_cols(i * (A_COLS // 2), A_COLS // 2)
    for p in (2, 1, 0):
        flying["az4%d" % p] = z_send(4, *za[p])
    for i in range(2):
        down_cols(A_COLS + i * (B_COLS // 2), B_COLS // 2)
    for g in (4, 3, 2, 1, 0):
        flying["by0%d" % g] = y_send(0, ZGROUPS[g], *yb)
    for name in REDUCE_ORDER:
        for copy in flying[name]:
            copy.wait_recv()
        done.add(name)
        kind, step = name[:2], int(name[2])
        if kind == "az":
            p = int(name[3])
            z_add(step - 1, *za[p])
            if step > 1:
                flying["az%d%d" % (step - 1, p)] = z_send(step - 1, *za[p])
            elif p == 2:
                flying["ay0"] = y_send(0, own, *ya)
        elif kind == "by" and step == 0:
            y_add(0, ZGROUPS[int(name[3])], *yb)
            flying["by1" + name[3]] = y_send(1, ZGROUPS[int(name[3])], *yb)
        elif kind == "by":
            y_add(1, ZGROUPS[int(name[3])], *yb)
        elif kind == "bz":
            bz_add(step)
        elif kind == "ay" and step == 0:
            y_add(0, own, *ya)
        for d, needs in BZ_NEEDS.items():
            if "bz%d" % d not in flying and done.issuperset(needs):
                flying["bz%d" % d] = bz_send(d)
        if "ay1" not in flying and "ay0" in done and "az11" in done:
            flying["ay1"] = y_send(1, own, *ya)
        if name == "ay1":
            out_ref[:, CA] = (
                mid_ref[:, CA].astype(F32)
                + part[0, 0, :, CA].astype(F32)
                + a_yp[0, 0].astype(F32)
                + a_ym[0, 0].astype(F32)
            ).astype(BF)
        if name == "bz1":
            out_ref[:, CB] = (
                mid_ref[:, CB].astype(F32)
                + part[0, 0, :, CB].astype(F32)
                + b_zp[0, 0].astype(F32)
                + b_zm[0, 0].astype(F32)
                + b_zp[2, 0].astype(F32)
                + b_zm[2, 0].astype(F32)
            ).astype(BF)
    net.finish()


LOG2_SCALE = math.log2(math.e) / math.sqrt(HEAD)
Q_COLS = GROUP * HEAD
KEYS_OWN = 768
KEYS_CHIP = 2 * KEYS_OWN
RESP = 512
N_CHIP = 1536


def layer_kernel(
    q_hbm, ck_hbm, cv_hbm, rkv_hbm, seg_hbm, res_hbm, wo_hbm, gain_hbm, up_hbm, down_hbm, out_ref,
    q_ref, rkv_ref, seg_ref, res_ref, gain_ref, mid_ref, up_w, down_w,
    packed, got, qcat, osum, qall, rkv, kbuf, vbuf, wo, obuf, stat, robuf, rstat, attn, part, zp_buf, zm_buf,
    px, local_sem, s_sem, r_sem, *ffn_refs,
):
    x, core, z, y = where_am_i()
    sib = device(x, 1 - core, z, y)
    zdev = [device(x, core, z + d, y) for d in range(8)]
    xdev = [device(x + d, core, z, y) for d in range(4)]
    ydev = [device(x, core, z, y + d) for d in range(4)]
    ysib = [device(x, 1 - core, z, y + d) for d in range(4)]
    all_here = greet([*zdev[1:], *xdev[1:], *ydev[1:], *ysib])
    head = pl.ds(pl.multiple_of(z * HEAD, HEAD), HEAD)
    wo_rows = pl.ds(pl.multiple_of(y * 192, 64), 192)
    wo_own = pl.ds(pl.multiple_of(core * 768, 128), 768)

    loads = [
        pltpu.make_async_copy(src, dst, local_sem.at[3 + i])
        for i, (src, dst) in enumerate(
            (
                (q_hbm, q_ref),
                (rkv_hbm, rkv_ref),
                (seg_hbm, seg_ref),
                (res_hbm, res_ref),
                (gain_hbm, gain_ref),
                (up_hbm, up_w),
                (down_hbm, down_w),
            )
        )
    ]
    load_q, load_rkv, load_seg, load_res, load_gain, load_up, load_down = loads
    load_q.start()
    load_rkv.start()
    load_k = pltpu.make_async_copy(ck_hbm.at[:, head], kbuf.at[pl.ds(0, KEYS_OWN)], local_sem.at[0])
    load_v = pltpu.make_async_copy(
        cv_hbm.at[:, head], vbuf.at[pl.ds(0, KEYS_OWN), pl.ds(0, HEAD)], local_sem.at[1]
    )
    load_wo = pltpu.make_async_copy(wo_hbm, wo.at[wo_rows, wo_own], local_sem.at[2])
    load_k.start()
    load_v.start()
    load_wo.start()
    for load in (load_seg, load_res, load_gain):
        load.start()
    load_q.wait()
    load_rkv.wait()
    for i in range(8):
        packed[i, :, 0:Q_COLS] = q_ref[:, i * Q_COLS : (i + 1) * Q_COLS]
        packed[i, :, Q_COLS : Q_COLS + HEAD] = rkv_ref[:, i * HEAD : (i + 1) * HEAD]
        packed[i, :, Q_COLS + HEAD :] = rkv_ref[:, 1024 + i * HEAD : 1024 + (i + 1) * HEAD]
    all_here()
    net = Copies(s_sem, r_sem)

    def arrived(copies):
        for copy in copies:
            copy.wait_recv()

    moves = [
        net.send(packed.at[lax.rem(z + d, 8)], got.at[8 - d], zdev[d]) for d in (4, 3, 5, 2, 6, 1, 7)
    ]
    caches = [
        net.send(ck_hbm.at[:, head], kbuf.at[pl.ds(KEYS_OWN, KEYS_OWN)], sib),
        net.send(cv_hbm.at[:, head], vbuf.at[pl.ds(KEYS_OWN, KEYS_OWN), pl.ds(0, HEAD)], sib),
    ]
    got[0] = packed[z]
    vbuf[:, HEAD:] = jnp.ones((KEYS_CHIP + RESP, HEAD), BF)
    arrived(moves)
    rkv[0, 0] = got[:, :, Q_COLS:]
    kv_moves = [net.send(rkv.at[0, 0], rkv.at[0, 4 - d], ydev[d]) for d in (2, 1, 3)]
    kv_moves += [net.send(rkv.at[0, 0], rkv.at[1, (4 - d) % 4], ysib[d]) for d in (2, 1, 3, 0)]
    qall[0] = got[:, :, 0:Q_COLS]
    q_moves = [net.send(qall.at[0], qall.at[4 - d], xdev[d]) for d in (1, 3, 2)]

    load_seg.wait()
    seg = seg_ref[...]
    bounds = [
        jnp.sum(jnp.where(seg < s, 1, 0), keepdims=True) for s in (1, 2, 3)
    ]
    lanes = lax.broadcasted_iota(jnp.int32, (1, RESP), 1)
    key_row = (
        (2 * x + ((core + lanes // 256) & 1)) * 32
        + ((z + (lanes // 8)) & 7) * 4
        + ((y + (lanes // 64)) & 3)
    ) * 8 + (lanes & 7)
    slots = lax.broadcasted_iota(jnp.int32, (64, 1), 0)

    load_up.start()
    load_down.start()
    nt = (((1,), (1,)), ((), ()))
    lane = lax.broadcasted_iota(jnp.int32, (64, HEAD), 1)
    wide_lane = lax.broadcasted_iota(jnp.int32, (GROUP * 64, HEAD), 1)

    def attend_cache(i):
        wide = qall[i].astype(F32)
        q = jnp.concatenate(
            [wide[:, :, j * HEAD : (j + 1) * HEAD].reshape(64, HEAD) for j in range(GROUP)], 0
        ).astype(BF)
        qcat[i] = q
        score = lax.dot_general(q, kbuf[0:KEYS_CHIP, :], nt, preferred_element_type=F32)
        top = jnp.max(score, axis=-1, keepdims=True)
        weight = jnp.exp2((score - top) * LOG2_SCALE).astype(BF)
        mixed = jnp.dot(weight, vbuf[0:KEYS_CHIP, :], preferred_element_type=F32)
        osum[i, :, 0:HEAD] = mixed[:, 0:HEAD]
        osum[i, :, HEAD:] = jnp.where(wide_lane < 64, mixed[:, HEAD:], top)

    def attend_response(i):
        q_row = ((2 * ((x + i) & 3) + core) * 32 + ((z + slots // 8) & 7) * 4 + y) * 8 + (slots & 7)
        start = jnp.zeros_like(q_row)
        for bound in bounds:
            start = jnp.maximum(start, jnp.where(q_row >= bound, bound, 0))
        seen = (key_row <= q_row) & (key_row >= start)
        seen = jnp.concatenate([jnp.where(seen, 0.0, -jnp.inf)] * GROUP, 0)
        score = lax.dot_general(qcat[i], kbuf[KEYS_CHIP:, :], nt, preferred_element_type=F32) + seen
        first_top = osum[i, :, 2 * HEAD - 1 : 2 * HEAD]
        top = jnp.maximum(first_top, jnp.max(score, axis=-1, keepdims=True))
        weight = jnp.exp2((score - top) * LOG2_SCALE).astype(BF)
        mixed = osum[i] * jnp.exp2((first_top - top) * LOG2_SCALE) + jnp.dot(
            weight, vbuf[KEYS_CHIP:, :], preferred_element_type=F32
        )
        both = jnp.ones((64, HEAD), F32)
        for j in range(GROUP):
            rows = slice(j * 64, (j + 1) * 64)
            obuf[i, :, :, j * HEAD : (j + 1) * HEAD] = mixed[rows, 0:HEAD].reshape(8, 8, HEAD).astype(BF)
            both = jnp.where((lane & 31) == j, top[rows], both)
            both = jnp.where((lane & 31) == 8 + j, mixed[rows, HEAD : HEAD + 1], both)
        for g in range(4):
            quarter = both[g * 16 : (g + 1) * 16]
            packed_stat = quarter if g == 0 else jnp.where(lane[0:16] >= 32 * g, quarter, packed_stat)
        stat[i] = packed_stat

    o_moves = []

    def give(d):
        attend_response(d)
        o_moves.append(net.send(obuf.at[d], robuf.at[4 - d], xdev[d]))
        o_moves.append(net.send(stat.at[d], rstat.at[4 - d], xdev[d]))

    load_k.wait()
    load_v.wait()
    arrived(caches)
    attend_cache(0)
    load_wo.wait()
    own_wo = wo.at[wo_rows, wo_own]
    wo_moves = [net.send(own_wo, own_wo, ydev[d]) for d in (1, 3)]
    arrived([q_moves[2]])
    attend_cache(2)
    arrived(kv_moves)
    kbuf[pl.ds(KEYS_CHIP, RESP), :] = rkv[:, :, :, :, 0:HEAD].astype(F32).reshape(RESP, HEAD).astype(BF)
    vbuf[pl.ds(KEYS_CHIP, RESP), 0:HEAD] = (
        rkv[:, :, :, :, HEAD:].astype(F32).reshape(RESP, HEAD).astype(BF)
    )
    give(2)
    arrived([q_moves[0]])
    attend_cache(3)
    give(3)
    arrived([q_moves[1]])
    attend_cache(1)
    give(1)
    arrived(wo_moves)
    back, ahead = lax.rem(y + 3, 4), lax.rem(y + 1, 4)
    low = wo.at[pl.ds(pl.multiple_of(back * 192, 64), 96), wo_own]
    high = wo.at[pl.ds(pl.multiple_of(ahead * 192 + 96, 32), 96), wo_own]
    wo_moves = [net.send(low, low, ydev[1]), net.send(high, high, ydev[3])]
    attend_response(0)
    arrived(wo_moves)
    wo_cols = wo.at[:, wo_own]
    wo_sib = net.send(wo_cols, wo_cols, sib)
    arrived(o_moves)

    def unpacked(tile, shift):
        parts = [(tile, (HEAD - 32 * g - shift) % HEAD) for g in range(4)]
        return jnp.concatenate([pltpu.roll(t, by, 1) if by else t for t, by in parts], 0)

    tiles = [stat[0]] + [rstat[i] for i in range(1, 4)]
    tops = [unpacked(t, 0) for t in tiles]
    totals = [unpacked(t, 8) for t in tiles]
    top = functools.reduce(jnp.maximum, tops)
    scales = [jnp.exp2((t - top) * LOG2_SCALE) for t in tops]
    total = functools.reduce(jnp.add, [a * b for a, b in zip(scales, totals)])
    scales = [a / total for a in scales]
    for j in range(GROUP):
        cols = slice(j * HEAD, (j + 1) * HEAD)
        mixed = obuf[0, :, :, cols].astype(F32).reshape(64, HEAD) * scales[0][:, j : j + 1]
        for i in range(1, 4):
            mixed = mixed + robuf[i, :, :, cols].astype(F32).reshape(64, HEAD) * scales[i][:, j : j + 1]
        attn[0, :, :, cols] = mixed.reshape(8, 8, HEAD).astype(BF)
    a_moves = [net.send(attn.at[0], attn.at[4 - d], xdev[d]) for d in (2, 1, 3)]
    arrived([wo_sib])
    ring = {}

    far0, far1 = slice(0, 768), slice(768, N_CHIP)

    def project(*slots):
        count = 64 * len(slots)
        lhs = jnp.concatenate([attn[i].astype(F32).reshape(64, Q_COLS) for i in slots], 0).astype(BF)
        for p in range(2):
            cols = slice(p * 768, (p + 1) * 768)
            block = jnp.dot(lhs, wo[:, cols], preferred_element_type=F32)
            for k, i in enumerate(slots):
                part[:, i, :, cols] = block[k * 64 : (k + 1) * 64].reshape(8, 8, 768).astype(BF)
        for i in slots:
            ring[i] = [
                net.send(part.at[4, i, :, far1], zp_buf.at[3, i, :, far1], zdev[2]),
                net.send(part.at[4, i, :, far0], zm_buf.at[3, i, :, far0], zdev[6]),
                net.send(part.at[3, i], zp_buf.at[1, i], zdev[1]),
                net.send(part.at[5, i], zm_buf.at[1, i], zdev[7]),
            ]

    def relay(i):
        arrived(ring[i])
        add_into(part.at[2, i], zp_buf.at[1, i])
        add_into(part.at[2, i, :, far1], zp_buf.at[3, i, :, far1])
        add_into(part.at[6, i], zm_buf.at[1, i])
        add_into(part.at[6, i, :, far0], zm_buf.at[3, i, :, far0])
        ring[i] = [
            net.send(part.at[2, i], zp_buf.at[2, i], zdev[2]),
            net.send(part.at[6, i], zm_buf.at[2, i], zdev[6]),
            net.send(part.at[1, i], zp_buf.at[0, i], zdev[1]),
            net.send(part.at[7, i], zm_buf.at[0, i], zdev[7]),
        ]

    p_moves = []

    def settle(i):
        arrived(ring[i])
        add_into(
            part.at[0, i], zp_buf.at[0, i], zm_buf.at[0, i], zp_buf.at[2, i], zm_buf.at[2, i]
        )
        if i > 0:
            p_moves.append(net.send(part.at[0, i], px.at[4 - i], xdev[i]))

    project(0)
    arrived([a_moves[1], a_moves[2]])
    project(1, 3)
    relay(0)
    arrived([a_moves[0]])
    project(2)
    relay(1)
    relay(3)
    relay(2)
    settle(0)
    settle(1)
    settle(3)
    settle(2)
    px[0] = part[0, 0]
    load_res.wait()
    load_gain.wait()
    arrived(p_moves)
    for i in range(4):
        cols = pl.ds(pl.multiple_of(((x + i) & 3) * N_CHIP, HEAD), N_CHIP)
        mid_ref[:, cols] = (res_ref[:, cols].astype(F32) + px[i].astype(F32)).astype(BF)
    net.finish()
    ffn_phase(
        (x, core, z, y), mid_ref, gain_ref, load_up, load_down, out_ref, up_w, down_w, *ffn_refs
    )


def on_device(
    queries,
    cache_keys,
    cache_values,
    response_kv,
    segments,
    residual,
    out_weight,
    norm_gain,
    up_weight,
    down_weight,
):
    hbm = pl.BlockSpec(memory_space=pl.ANY)
    hidden = up_weight.shape[1]
    return pl.pallas_call(
        layer_kernel,
        name="layer",
        out_shape=jax.ShapeDtypeStruct(residual.shape, BF),
        in_specs=[hbm] * 10,
        out_specs=pl.BlockSpec(memory_space=pltpu.VMEM),
        scratch_shapes=[
            pltpu.VMEM(queries.shape, BF),
            pltpu.VMEM(response_kv.shape, BF),
            pltpu.VMEM((16, 128), jnp.int32),
            pltpu.VMEM(residual.shape, BF),
            pltpu.VMEM((1, D), F32),
            pltpu.VMEM(residual.shape, BF),
            pltpu.VMEM((D, hidden), BF),
            pltpu.VMEM((hidden, D), BF),
            pltpu.VMEM((8, 8, 1024), BF),
            pltpu.VMEM((8, 8, 1024), BF),
            pltpu.VMEM((4, GROUP * 64, HEAD), BF),
            pltpu.VMEM((4, GROUP * 64, 2 * HEAD), F32),
            pltpu.VMEM((4, 8, 8, Q_COLS), BF),
            pltpu.VMEM((2, 4, 8, 8, 2 * HEAD), BF),
            pltpu.VMEM((KEYS_CHIP + RESP, HEAD), BF),
            pltpu.VMEM((KEYS_CHIP + RESP, 2 * HEAD), BF),
            pltpu.VMEM((Q_COLS, N_CHIP), BF),
            pltpu.VMEM((4, 8, 8, Q_COLS), BF),
            pltpu.VMEM((4, 16, HEAD), F32),
            pltpu.VMEM((4, 8, 8, Q_COLS), BF),
            pltpu.VMEM((4, 16, HEAD), F32),
            pltpu.VMEM((4, 8, 8, Q_COLS), BF),
            pltpu.VMEM((8, 4, 8, N_CHIP), BF),
            pltpu.VMEM((4, 4, 8, N_CHIP), BF),
            pltpu.VMEM((4, 4, 8, N_CHIP), BF),
            pltpu.VMEM((4, 8, N_CHIP), BF),
            pltpu.SemaphoreType.DMA((10,)),
            pltpu.SemaphoreType.DMA((72,)),
            pltpu.SemaphoreType.DMA((72,)),
            pltpu.VMEM((8, 4, 8, D), BF),
            pltpu.VMEM((8, 4, 8, D), BF),
            pltpu.VMEM((256, hidden), F32),
            pltpu.VMEM((256, hidden), BF),
            pltpu.VMEM((4, 4, 8, A_COLS), BF),
            pltpu.VMEM((4, 4, 8, A_COLS), BF),
            pltpu.VMEM((2, 1, 8, A_COLS), BF),
            pltpu.VMEM((2, 1, 8, A_COLS), BF),
            pltpu.VMEM((2, 8, 8, B_COLS), BF),
            pltpu.VMEM((2, 8, 8, B_COLS), BF),
            pltpu.VMEM((4, 1, 8, B_COLS), BF),
            pltpu.VMEM((4, 1, 8, B_COLS), BF),
            pltpu.SemaphoreType.DMA((N_GATHER,)),
            pltpu.SemaphoreType.DMA((N_GATHER,)),
            pltpu.SemaphoreType.DMA((N_REDUCE,)),
            pltpu.SemaphoreType.DMA((N_REDUCE,)),
        ],
        compiler_params=pltpu.CompilerParams(
            collective_id=0, has_side_effects=True, vmem_limit_bytes=60 * 1024 * 1024
        ),
    )(
        queries, cache_keys, cache_values, response_kv, segments.reshape(16, 128), residual,
        out_weight, norm_gain.reshape(1, D), up_weight, down_weight,
    )


def solution(mesh):
    return jax.shard_map(
        on_device,
        mesh=mesh,
        in_specs=(
            P(("key", "hid"), None),
            P("key", None),
            P("key", None),
            P(("key", "hid"), None),
            P(),
            P(("key", "hid"), None),
            P("hid", "key"),
            P(),
            P(None, "hid"),
            P("hid", None),
        ),
        out_specs=P(("key", "hid"), None),
        check_vma=False,
    )
```

```python
import functools
import math

import jax
import jax.numpy as jnp
from jax import lax
from jax.experimental import pallas as pl
from jax.experimental.pallas import tpu as pltpu
from jax.sharding import PartitionSpec as P

HEADS = 48
KV_HEADS = 8
HEAD = 128
GROUP = 6
D = 6144
MESH = pl.DeviceIdType.MESH
BF = jnp.bfloat16
F32 = jnp.float32

ZI = {0: 0, 1: 1, -1: 2, 2: 3, -2: 4, 3: 5, -3: 6, 4: 7}
YI = {0: 0, 1: 1, -1: 2, 2: 3}
ZGROUPS = (pl.ds(0, 1), pl.ds(1, 2), pl.ds(3, 2), pl.ds(5, 2), pl.ds(7, 1))

A_COLS = 2304
B_COLS = D - A_COLS
CA, A0, A1 = pl.ds(0, A_COLS), pl.ds(0, A_COLS // 2), pl.ds(A_COLS // 2, A_COLS // 2)
CB = pl.ds(A_COLS, B_COLS)
B0, B1 = pl.ds(A_COLS, B_COLS // 2), pl.ds(A_COLS + B_COLS // 2, B_COLS // 2)
LB, L0, L1 = pl.ds(0, B_COLS), pl.ds(0, B_COLS // 2), pl.ds(B_COLS // 2, B_COLS // 2)
N_GATHER = 56
N_REDUCE = 56


class Copies:
    def __init__(self, send_sems, recv_sems):
        self.sems = send_sems, recv_sems
        self.made = []
        self.finished = 0

    def send(self, src, dst, device):
        i = len(self.made)
        copy = pltpu.make_async_remote_copy(
            src_ref=src,
            dst_ref=dst,
            send_sem=self.sems[0].at[i],
            recv_sem=self.sems[1].at[i],
            device_id=device,
            device_id_type=MESH,
        )
        copy.start()
        self.made.append(copy)
        return copy

    def finish(self, but=0):
        last = len(self.made) - but
        for copy in self.made[self.finished : last]:
            copy.wait_send()
        self.finished = max(self.finished, last)


def where_am_i():
    key = lax.axis_index("key")
    hid = lax.axis_index("hid")
    return key // 2, key % 2, hid // 4, hid % 4


def device(x, core, z, y):
    return (lax.rem(x, 4) * 2 + core, lax.rem(z, 8) * 4 + lax.rem(y, 4))


def greet(devices):
    barrier = pltpu.get_barrier_semaphore()
    for one in devices:
        pl.semaphore_signal(barrier, inc=1, device_id=one, device_id_type=MESH)
    return lambda: pl.semaphore_wait(barrier, len(devices))


def add_into(dst, *srcs):
    total = dst[...].astype(F32)
    for src in srcs:
        total = total + src[...].astype(F32)
    dst[...] = total.astype(BF)


GATHER_ORDER = (
    "ay1", "bz1", "by10", "ay2", "bz2", "az10", "az11", "by11", "az12", "by20", "bz3", "by12",
    "bz4", "az20", "by21", "az21", "az22", "by13", "az30", "by22", "az31", "by14", "az32", "up",
    "az40", "by23", "az41", "by24", "az42",
)
REDUCE_ORDER = (
    "az42", "by04", "az41", "az40", "by03", "by02", "az32", "by01", "az31", "by00", "az30", "by14",
    "az22", "by13", "az21", "az20", "by12", "bz4", "az12", "bz3", "by11", "az11", "by10", "az10",
    "ay0", "bz2", "ay1", "bz1",
)
BZ_NEEDS = {4: ("by14",), 3: ("by13",), 2: ("by12", "bz3", "bz4"), 1: ("by11",)}
PIECES = (pl.ds(0, 1), pl.ds(1, 2), pl.ds(3, 1))


def ffn_phase(
    where, before, mid_ref, gain_ref, load_up, load_down, out_ref,
    up_w, down_w, rows, part, acc, act,
    a_zp, a_zm, a_yp, a_ym, b_yp, b_ym, b_zp, b_zm,
    g_send, g_recv, r_send, r_recv,
):
    x, core, z, y = where
    zp, zm = device(x, core, z + 1, y), device(x, core, z + 7, y)
    yp, ym = device(x, core, z, y + 1), device(x, core, z, y + 3)
    zp2, zm2 = device(x, core, z + 2, y), device(x, core, z + 6, y)

    wide = mid_ref[...].astype(F32)
    mean = jnp.mean(wide, axis=-1, keepdims=True)
    centred = wide - mean
    var = jnp.mean(centred * centred, axis=-1, keepdims=True)
    rows[0, 0] = (centred * lax.rsqrt(var + 1e-05) * gain_ref[...]).astype(BF)

    net = Copies(g_send, g_recv)
    flying = {}

    def z_hop(hop, ys, cols, half0, half1):
        if hop == 4:
            return (
                net.send(rows.at[ZI[-3], ys, :, half0], rows.at[ZI[4], ys, :, half0], zp),
                net.send(rows.at[ZI[3], ys, :, half1], rows.at[ZI[4], ys, :, half1], zm),
            )
        return (
            net.send(rows.at[ZI[1 - hop], ys, :, cols], rows.at[ZI[-hop], ys, :, cols], zp),
            net.send(rows.at[ZI[hop - 1], ys, :, cols], rows.at[ZI[hop], ys, :, cols], zm),
        )

    def y_first(zs, cols):
        return (
            net.send(rows.at[zs, 0, :, cols], rows.at[zs, YI[-1], :, cols], yp),
            net.send(rows.at[zs, 0, :, cols], rows.at[zs, YI[1], :, cols], ym),
        )

    def y_second(zs, half0, half1):
        return (
            net.send(rows.at[zs, YI[-1], :, half0], rows.at[zs, YI[2], :, half0], yp),
            net.send(rows.at[zs, YI[1], :, half1], rows.at[zs, YI[2], :, half1], ym),
        )

    def az_hop(hop, piece):
        flying["az%d%d" % (hop, piece)] = z_hop(hop, PIECES[piece], CA, A0, A1)

    def bz_hop(hop):
        if hop == 1:
            pair = z_hop(1, 0, CB, B0, B1)
        elif hop == 2:
            pair = (
                net.send(rows.at[0, 0, :, CB], rows.at[ZI[-2], 0, :, CB], zp2),
                net.send(rows.at[0, 0, :, CB], rows.at[ZI[2], 0, :, CB], zm2),
            )
        elif hop == 3:
            pair = z_hop(3, 0, CB, B0, B1)
        else:
            pair = (
                net.send(rows.at[ZI[-2], 0, :, B0], rows.at[ZI[4], 0, :, B0], zp2),
                net.send(rows.at[ZI[2], 0, :, B1], rows.at[ZI[4], 0, :, B1], zm2),
            )
        flying["bz%d" % hop] = pair

    def up_cols(first, size, fresh, low, high):
        cols = pl.ds(first, size)
        count = (high - low) * 32
        block = rows[low:high, :, :, cols].astype(F32).reshape(count, size).astype(BF)
        product = jnp.dot(block, up_w[cols, :], preferred_element_type=F32)
        if fresh:
            acc[low * 32 : high * 32] = product
        else:
            acc[low * 32 : high * 32] += product

    def up_rows(low, high):
        for i in range(2):
            up_cols(i * (A_COLS // 2), A_COLS // 2, i == 0, low, high)
        for i in range(2):
            up_cols(A_COLS + i * (B_COLS // 2), B_COLS // 2, False, low, high)

    own = pl.ds(0, 1)
    flying["ay1"] = y_first(own, CA)
    bz_hop(1)
    bz_hop(2)
    flying["by10"] = y_first(ZGROUPS[0], CB)
    az_hop(1, 0)
    before.finish()
    for name in GATHER_ORDER:
        if name == "up":
            load_up.wait()
            up_rows(0, 5)
            continue
        for copy in flying[name]:
            copy.wait_recv()
        kind, step = name[:2], int(name[2])
        if kind == "ay" and step == 1:
            flying["ay2"] = y_second(own, A0, A1)
            az_hop(1, 1)
        elif kind == "ay":
            az_hop(1, 2)
        elif kind == "az" and step < 4:
            az_hop(step + 1, int(name[3]))
        elif kind == "bz":
            if step == 2:
                bz_hop(3)
                bz_hop(4)
            flying["by1%d" % step] = y_first(ZGROUPS[step], CB)
        elif kind == "by" and step == 1:
            flying["by2" + name[3]] = y_second(ZGROUPS[int(name[3])], B0, B1)

    up_rows(5, 8)
    up = jnp.maximum(acc[...], 0.0)
    act[...] = (up * up).astype(BF)
    load_down.wait()

    def down_cols(first, size):
        cols = pl.ds(first, size)
        block = jnp.dot(act[...], down_w[:, cols], preferred_element_type=F32)
        part[:, :, :, cols] = block.reshape(8, 4, 8, size).astype(BF)

    gather = net
    net = Copies(r_send, r_recv)
    flying = {}
    done = set()

    def z_send(d, ys, cols, half0, half1, lcols, lh0, lh1, got_p, got_m, lys):
        if d == 4:
            return (
                net.send(part.at[ZI[4], ys, :, half1], got_p.at[3, lys, :, lh1], zp),
                net.send(part.at[ZI[4], ys, :, half0], got_m.at[3, lys, :, lh0], zm),
            )
        return (
            net.send(part.at[ZI[d], ys, :, cols], got_p.at[d - 1, lys, :, lcols], zp),
            net.send(part.at[ZI[-d], ys, :, cols], got_m.at[d - 1, lys, :, lcols], zm),
        )

    def z_add(d, ys, cols, half0, half1, lcols, lh0, lh1, got_p, got_m, lys):
        if d == 3:
            add_into(part.at[ZI[3], ys, :, half1], got_p.at[3, lys, :, lh1])
            add_into(part.at[ZI[-3], ys, :, half0], got_m.at[3, lys, :, lh0])
        elif d > 0:
            add_into(part.at[ZI[d], ys, :, cols], got_p.at[d, lys, :, lcols])
            add_into(part.at[ZI[-d], ys, :, cols], got_m.at[d, lys, :, lcols])
        else:
            add_into(
                part.at[0, ys, :, cols], got_p.at[0, lys, :, lcols], got_m.at[0, lys, :, lcols]
            )

    def y_send(step, zs, cols, half0, half1, lcols, lh0, lh1, got_p, got_m):
        if step == 0:
            return (
                net.send(part.at[zs, YI[2], :, half1], got_p.at[1, zs, :, lh1], yp),
                net.send(part.at[zs, YI[2], :, half0], got_m.at[1, zs, :, lh0], ym),
            )
        return (
            net.send(part.at[zs, YI[1], :, cols], got_p.at[0, zs, :, lcols], yp),
            net.send(part.at[zs, YI[-1], :, cols], got_m.at[0, zs, :, lcols], ym),
        )

    def y_add(step, zs, cols, half0, half1, lcols, lh0, lh1, got_p, got_m):
        if step == 0:
            add_into(part.at[zs, YI[1], :, half1], got_p.at[1, zs, :, lh1])
            add_into(part.at[zs, YI[-1], :, half0], got_m.at[1, zs, :, lh0])
        else:
            add_into(part.at[zs, 0, :, cols], got_p.at[0, zs, :, lcols], got_m.at[0, zs, :, lcols])

    za = [(p, CA, A0, A1, CA, A0, A1, a_zp, a_zm, p) for p in PIECES]

    def bz_send(d):
        slot, ahead, behind = {1: (0, zp, zm), 2: (2, zp2, zm2), 3: (1, zp, zm), 4: (3, zp2, zm2)}[d]
        if d == 4:
            return (
                net.send(part.at[ZI[4], 0, :, B1], b_zp.at[slot, 0, :, L1], ahead),
                net.send(part.at[ZI[4], 0, :, B0], b_zm.at[slot, 0, :, L0], behind),
            )
        return (
            net.send(part.at[ZI[d], 0, :, CB], b_zp.at[slot, 0], ahead),
            net.send(part.at[ZI[-d], 0, :, CB], b_zm.at[slot, 0], behind),
        )

    def bz_add(d):
        if d == 4:
            add_into(part.at[ZI[2], 0, :, B1], b_zp.at[3, 0, :, L1])
            add_into(part.at[ZI[-2], 0, :, B0], b_zm.at[3, 0, :, L0])
        elif d == 3:
            add_into(part.at[ZI[2], 0, :, CB], b_zp.at[1, 0])
            add_into(part.at[ZI[-2], 0, :, CB], b_zm.at[1, 0])

    yb = (CB, B0, B1, LB, L0, L1, b_yp, b_ym)
    ya = (CA, A0, A1, CA, A0, A1, a_yp, a_ym)

    for i in range(2):
        down_cols(i * (A_COLS // 2), A_COLS // 2)
    for p in (2, 1, 0):
        flying["az4%d" % p] = z_send(4, *za[p])
    for i in range(2):
        down_cols(A_COLS + i * (B_COLS // 2), B_COLS // 2)
    for g in (4, 3, 2, 1, 0):
        flying["by0%d" % g] = y_send(0, ZGROUPS[g], *yb)
    gather.finish()
    for name in REDUCE_ORDER:
        for copy in flying[name]:
            copy.wait_recv()
        done.add(name)
        kind, step = name[:2], int(name[2])
        if kind == "az":
            p = int(name[3])
            z_add(step - 1, *za[p])
            if step > 1:
                flying["az%d%d" % (step - 1, p)] = z_send(step - 1, *za[p])
            elif p == 2:
                flying["ay0"] = y_send(0, own, *ya)
        elif kind == "by" and step == 0:
            y_add(0, ZGROUPS[int(name[3])], *yb)
            flying["by1" + name[3]] = y_send(1, ZGROUPS[int(name[3])], *yb)
        elif kind == "by":
            y_add(1, ZGROUPS[int(name[3])], *yb)
        elif kind == "bz":
            bz_add(step)
        elif kind == "ay" and step == 0:
            y_add(0, own, *ya)
        for d, needs in BZ_NEEDS.items():
            if "bz%d" % d not in flying and done.issuperset(needs):
                flying["bz%d" % d] = bz_send(d)
        if name in ("by14", "by12", "az10"):
            net.finish(16)
        if "ay1" not in flying and "ay0" in done and "az11" in done:
            flying["ay1"] = y_send(1, own, *ya)
        if name == "ay1":
            out_ref[:, CA] = (
                mid_ref[:, CA].astype(F32)
                + part[0, 0, :, CA].astype(F32)
                + a_yp[0, 0].astype(F32)
                + a_ym[0, 0].astype(F32)
            ).astype(BF)
        if name == "bz1":
            out_ref[:, CB] = (
                mid_ref[:, CB].astype(F32)
                + part[0, 0, :, CB].astype(F32)
                + b_zp[0, 0].astype(F32)
                + b_zm[0, 0].astype(F32)
                + b_zp[2, 0].astype(F32)
                + b_zm[2, 0].astype(F32)
            ).astype(BF)
    net.finish()


LOG2_SCALE = math.log2(math.e) / math.sqrt(HEAD)
Q_COLS = GROUP * HEAD
KEYS_OWN = 768
KEYS_CHIP = 2 * KEYS_OWN
RESP = 512
N_CHIP = 1536


def layer_kernel(
    q_hbm, ck_hbm, cv_hbm, rkv_hbm, seg_hbm, res_hbm, wo_hbm, gain_hbm, up_hbm, down_hbm, out_ref,
    q_ref, rkv_ref, seg_ref, res_ref, gain_ref, mid_ref, up_w, down_w,
    packed, got, qcat, osum, qall, rkv, kbuf, vbuf, wo, obuf, stat, robuf, rstat, attn, part, zp_buf, zm_buf,
    px, local_sem, s_sem, r_sem, *ffn_refs,
):
    x, core, z, y = where_am_i()
    sib = device(x, 1 - core, z, y)
    zdev = [device(x, core, z + d, y) for d in range(8)]
    xdev = [device(x + d, core, z, y) for d in range(4)]
    ydev = [device(x, core, z, y + d) for d in range(4)]
    ysib = [device(x, 1 - core, z, y + d) for d in range(4)]
    all_here = greet([*zdev[1:], *xdev[1:], *ydev[1:], *ysib])
    head = pl.ds(pl.multiple_of(z * HEAD, HEAD), HEAD)
    wo_rows = pl.ds(pl.multiple_of(y * 192, 64), 192)
    wo_own = pl.ds(pl.multiple_of(core * 768, 128), 768)

    loads = [
        pltpu.make_async_copy(src, dst, local_sem.at[3 + i])
        for i, (src, dst) in enumerate(
            (
                (q_hbm, q_ref),
                (rkv_hbm, rkv_ref),
                (seg_hbm, seg_ref),
                (res_hbm, res_ref),
                (gain_hbm, gain_ref),
                (up_hbm, up_w),
                (down_hbm, down_w),
            )
        )
    ]
    load_q, load_rkv, load_seg, load_res, load_gain, load_up, load_down = loads
    load_q.start()
    load_rkv.start()
    load_k = pltpu.make_async_copy(ck_hbm.at[:, head], kbuf.at[pl.ds(0, KEYS_OWN)], local_sem.at[0])
    load_v = pltpu.make_async_copy(
        cv_hbm.at[:, head], vbuf.at[pl.ds(0, KEYS_OWN), pl.ds(0, HEAD)], local_sem.at[1]
    )
    load_wo = pltpu.make_async_copy(wo_hbm, wo.at[wo_rows, wo_own], local_sem.at[2])
    load_k.start()
    load_v.start()
    load_wo.start()
    for load in (load_seg, load_res, load_gain):
        load.start()
    load_q.wait()
    load_rkv.wait()
    for i in range(8):
        packed[i, :, 0:Q_COLS] = q_ref[:, i * Q_COLS : (i + 1) * Q_COLS]
        packed[i, :, Q_COLS : Q_COLS + HEAD] = rkv_ref[:, i * HEAD : (i + 1) * HEAD]
        packed[i, :, Q_COLS + HEAD :] = rkv_ref[:, 1024 + i * HEAD : 1024 + (i + 1) * HEAD]
    all_here()
    net = Copies(s_sem, r_sem)

    def arrived(copies):
        for copy in copies:
            copy.wait_recv()

    moves = [
        net.send(packed.at[lax.rem(z + d, 8)], got.at[8 - d], zdev[d]) for d in (4, 3, 5, 2, 6, 1, 7)
    ]
    caches = [
        net.send(ck_hbm.at[:, head], kbuf.at[pl.ds(KEYS_OWN, KEYS_OWN)], sib),
        net.send(cv_hbm.at[:, head], vbuf.at[pl.ds(KEYS_OWN, KEYS_OWN), pl.ds(0, HEAD)], sib),
    ]
    got[0] = packed[z]
    vbuf[:, HEAD:] = jnp.ones((KEYS_CHIP + RESP, HEAD), BF)
    arrived(moves)
    rkv[0, 0] = got[:, :, Q_COLS:]
    kv_moves = [net.send(rkv.at[0, 0], rkv.at[0, 4 - d], ydev[d]) for d in (2, 1, 3)]
    kv_moves += [net.send(rkv.at[0, 0], rkv.at[1, (4 - d) % 4], ysib[d]) for d in (2, 1, 3, 0)]
    qall[0] = got[:, :, 0:Q_COLS]
    q_moves = [net.send(qall.at[0], qall.at[4 - d], xdev[d]) for d in (1, 3, 2)]

    load_seg.wait()
    seg = seg_ref[...]
    bounds = [
        jnp.sum(jnp.where(seg < s, 1, 0), keepdims=True) for s in (1, 2, 3)
    ]
    lanes = lax.broadcasted_iota(jnp.int32, (1, RESP), 1)
    key_row = (
        (2 * x + ((core + lanes // 256) & 1)) * 32
        + ((z + (lanes // 8)) & 7) * 4
        + ((y + (lanes // 64)) & 3)
    ) * 8 + (lanes & 7)
    slots = lax.broadcasted_iota(jnp.int32, (64, 1), 0)

    load_up.start()
    load_down.start()
    nt = (((1,), (1,)), ((), ()))
    lane = lax.broadcasted_iota(jnp.int32, (64, HEAD), 1)
    wide_lane = lax.broadcasted_iota(jnp.int32, (GROUP * 64, HEAD), 1)

    def attend_cache(i):
        wide = qall[i].astype(F32)
        q = jnp.concatenate(
            [wide[:, :, j * HEAD : (j + 1) * HEAD].reshape(64, HEAD) for j in range(GROUP)], 0
        ).astype(BF)
        qcat[i] = q
        score = lax.dot_general(q, kbuf[0:KEYS_CHIP, :], nt, preferred_element_type=F32)
        top = jnp.max(score, axis=-1, keepdims=True)
        weight = jnp.exp2((score - top) * LOG2_SCALE).astype(BF)
        mixed = jnp.dot(weight, vbuf[0:KEYS_CHIP, :], preferred_element_type=F32)
        osum[i, :, 0:HEAD] = mixed[:, 0:HEAD]
        osum[i, :, HEAD:] = jnp.where(wide_lane < 64, mixed[:, HEAD:], top)

    def attend_response(i):
        q_row = ((2 * ((x + i) & 3) + core) * 32 + ((z + slots // 8) & 7) * 4 + y) * 8 + (slots & 7)
        start = jnp.zeros_like(q_row)
        for bound in bounds:
            start = jnp.maximum(start, jnp.where(q_row >= bound, bound, 0))
        seen = (key_row <= q_row) & (key_row >= start)
        seen = jnp.concatenate([jnp.where(seen, 0.0, -jnp.inf)] * GROUP, 0)
        score = lax.dot_general(qcat[i], kbuf[KEYS_CHIP:, :], nt, preferred_element_type=F32) + seen
        first_top = osum[i, :, 2 * HEAD - 1 : 2 * HEAD]
        top = jnp.maximum(first_top, jnp.max(score, axis=-1, keepdims=True))
        weight = jnp.exp2((score - top) * LOG2_SCALE).astype(BF)
        mixed = osum[i] * jnp.exp2((first_top - top) * LOG2_SCALE) + jnp.dot(
            weight, vbuf[KEYS_CHIP:, :], preferred_element_type=F32
        )
        both = jnp.ones((64, HEAD), F32)
        for j in range(GROUP):
            rows = slice(j * 64, (j + 1) * 64)
            obuf[i, :, :, j * HEAD : (j + 1) * HEAD] = mixed[rows, 0:HEAD].reshape(8, 8, HEAD).astype(BF)
            both = jnp.where((lane & 31) == j, top[rows], both)
            both = jnp.where((lane & 31) == 8 + j, mixed[rows, HEAD : HEAD + 1], both)
        for g in range(4):
            quarter = both[g * 16 : (g + 1) * 16]
            packed_stat = quarter if g == 0 else jnp.where(lane[0:16] >= 32 * g, quarter, packed_stat)
        stat[i] = packed_stat

    o_moves = []

    def give(d):
        attend_response(d)
        o_moves.append(net.send(obuf.at[d], robuf.at[4 - d], xdev[d]))
        o_moves.append(net.send(stat.at[d], rstat.at[4 - d], xdev[d]))

    load_k.wait()
    load_v.wait()
    arrived(caches)
    attend_cache(0)
    load_wo.wait()
    own_wo = wo.at[wo_rows, wo_own]
    wo_moves = [net.send(own_wo, own_wo, ydev[d]) for d in (1, 3)]
    arrived([q_moves[2]])
    attend_cache(2)
    arrived(kv_moves)
    kbuf[pl.ds(KEYS_CHIP, RESP), :] = rkv[:, :, :, :, 0:HEAD].astype(F32).reshape(RESP, HEAD).astype(BF)
    vbuf[pl.ds(KEYS_CHIP, RESP), 0:HEAD] = (
        rkv[:, :, :, :, HEAD:].astype(F32).reshape(RESP, HEAD).astype(BF)
    )
    give(2)
    arrived([q_moves[0]])
    attend_cache(3)
    give(3)
    arrived([q_moves[1]])
    attend_cache(1)
    give(1)
    arrived(wo_moves)
    back, ahead = lax.rem(y + 3, 4), lax.rem(y + 1, 4)
    low = wo.at[pl.ds(pl.multiple_of(back * 192, 64), 96), wo_own]
    high = wo.at[pl.ds(pl.multiple_of(ahead * 192 + 96, 32), 96), wo_own]
    wo_moves = [net.send(low, low, ydev[1]), net.send(high, high, ydev[3])]
    attend_response(0)
    arrived(wo_moves)
    wo_cols = wo.at[:, wo_own]
    wo_sib = net.send(wo_cols, wo_cols, sib)
    arrived(o_moves)

    def unpacked(tile, shift):
        parts = [(tile, (HEAD - 32 * g - shift) % HEAD) for g in range(4)]
        return jnp.concatenate([pltpu.roll(t, by, 1) if by else t for t, by in parts], 0)

    tiles = [stat[0]] + [rstat[i] for i in range(1, 4)]
    tops = [unpacked(t, 0) for t in tiles]
    totals = [unpacked(t, 8) for t in tiles]
    top = functools.reduce(jnp.maximum, tops)
    scales = [jnp.exp2((t - top) * LOG2_SCALE) for t in tops]
    total = functools.reduce(jnp.add, [a * b for a, b in zip(scales, totals)])
    scales = [a / total for a in scales]
    for j in range(GROUP):
        cols = slice(j * HEAD, (j + 1) * HEAD)
        mixed = obuf[0, :, :, cols].astype(F32).reshape(64, HEAD) * scales[0][:, j : j + 1]
        for i in range(1, 4):
            mixed = mixed + robuf[i, :, :, cols].astype(F32).reshape(64, HEAD) * scales[i][:, j : j + 1]
        attn[0, :, :, cols] = mixed.reshape(8, 8, HEAD).astype(BF)
    a_moves = [net.send(attn.at[0], attn.at[4 - d], xdev[d]) for d in (2, 1, 3)]
    arrived([wo_sib])
    ring = {}

    far0, far1 = slice(0, 768), slice(768, N_CHIP)

    def project(*slots):
        count = 64 * len(slots)
        lhs = jnp.concatenate([attn[i].astype(F32).reshape(64, Q_COLS) for i in slots], 0).astype(BF)
        for p in range(2):
            cols = slice(p * 768, (p + 1) * 768)
            block = jnp.dot(lhs, wo[:, cols], preferred_element_type=F32)
            for k, i in enumerate(slots):
                part[:, i, :, cols] = block[k * 64 : (k + 1) * 64].reshape(8, 8, 768).astype(BF)
        for i in slots:
            ring[i] = [
                net.send(part.at[4, i, :, far1], zp_buf.at[3, i, :, far1], zdev[2]),
                net.send(part.at[4, i, :, far0], zm_buf.at[3, i, :, far0], zdev[6]),
                net.send(part.at[3, i], zp_buf.at[1, i], zdev[1]),
                net.send(part.at[5, i], zm_buf.at[1, i], zdev[7]),
            ]

    def relay(i):
        arrived(ring[i])
        add_into(part.at[2, i], zp_buf.at[1, i])
        add_into(part.at[2, i, :, far1], zp_buf.at[3, i, :, far1])
        add_into(part.at[6, i], zm_buf.at[1, i])
        add_into(part.at[6, i, :, far0], zm_buf.at[3, i, :, far0])
        ring[i] = [
            net.send(part.at[2, i], zp_buf.at[2, i], zdev[2]),
            net.send(part.at[6, i], zm_buf.at[2, i], zdev[6]),
            net.send(part.at[1, i], zp_buf.at[0, i], zdev[1]),
            net.send(part.at[7, i], zm_buf.at[0, i], zdev[7]),
        ]

    p_moves = []

    def settle(i):
        arrived(ring[i])
        add_into(
            part.at[0, i], zp_buf.at[0, i], zm_buf.at[0, i], zp_buf.at[2, i], zm_buf.at[2, i]
        )
        if i > 0:
            p_moves.append(net.send(part.at[0, i], px.at[4 - i], xdev[i]))

    project(0)
    arrived([a_moves[1], a_moves[2]])
    project(1, 3)
    relay(0)
    arrived([a_moves[0]])
    project(2)
    relay(1)
    relay(3)
    relay(2)
    settle(0)
    settle(1)
    settle(3)
    settle(2)
    px[0] = part[0, 0]
    load_res.wait()
    load_gain.wait()
    arrived(p_moves)
    for i in range(4):
        cols = pl.ds(pl.multiple_of(((x + i) & 3) * N_CHIP, HEAD), N_CHIP)
        mid_ref[:, cols] = (res_ref[:, cols].astype(F32) + px[i].astype(F32)).astype(BF)
    ffn_phase(
        (x, core, z, y), net, mid_ref, gain_ref, load_up, load_down, out_ref, up_w, down_w, *ffn_refs
    )


def on_device(
    queries,
    cache_keys,
    cache_values,
    response_kv,
    segments,
    residual,
    out_weight,
    norm_gain,
    up_weight,
    down_weight,
):
    hbm = pl.BlockSpec(memory_space=pl.ANY)
    hidden = up_weight.shape[1]
    return pl.pallas_call(
        layer_kernel,
        name="layer",
        out_shape=jax.ShapeDtypeStruct(residual.shape, BF),
        in_specs=[hbm] * 10,
        out_specs=pl.BlockSpec(memory_space=pltpu.VMEM),
        scratch_shapes=[
            pltpu.VMEM(queries.shape, BF),
            pltpu.VMEM(response_kv.shape, BF),
            pltpu.VMEM((16, 128), jnp.int32),
            pltpu.VMEM(residual.shape, BF),
            pltpu.VMEM((1, D), F32),
            pltpu.VMEM(residual.shape, BF),
            pltpu.VMEM((D, hidden), BF),
            pltpu.VMEM((hidden, D), BF),
            pltpu.VMEM((8, 8, 1024), BF),
            pltpu.VMEM((8, 8, 1024), BF),
            pltpu.VMEM((4, GROUP * 64, HEAD), BF),
            pltpu.VMEM((4, GROUP * 64, 2 * HEAD), F32),
            pltpu.VMEM((4, 8, 8, Q_COLS), BF),
            pltpu.VMEM((2, 4, 8, 8, 2 * HEAD), BF),
            pltpu.VMEM((KEYS_CHIP + RESP, HEAD), BF),
            pltpu.VMEM((KEYS_CHIP + RESP, 2 * HEAD), BF),
            pltpu.VMEM((Q_COLS, N_CHIP), BF),
            pltpu.VMEM((4, 8, 8, Q_COLS), BF),
            pltpu.VMEM((4, 16, HEAD), F32),
            pltpu.VMEM((4, 8, 8, Q_COLS), BF),
            pltpu.VMEM((4, 16, HEAD), F32),
            pltpu.VMEM((4, 8, 8, Q_COLS), BF),
            pltpu.VMEM((8, 4, 8, N_CHIP), BF),
            pltpu.VMEM((4, 4, 8, N_CHIP), BF),
            pltpu.VMEM((4, 4, 8, N_CHIP), BF),
            pltpu.VMEM((4, 8, N_CHIP), BF),
            pltpu.SemaphoreType.DMA((10,)),
            pltpu.SemaphoreType.DMA((72,)),
            pltpu.SemaphoreType.DMA((72,)),
            pltpu.VMEM((8, 4, 8, D), BF),
            pltpu.VMEM((8, 4, 8, D), BF),
            pltpu.VMEM((256, hidden), F32),
            pltpu.VMEM((256, hidden), BF),
            pltpu.VMEM((4, 4, 8, A_COLS), BF),
            pltpu.VMEM((4, 4, 8, A_COLS), BF),
            pltpu.VMEM((2, 1, 8, A_COLS), BF),
            pltpu.VMEM((2, 1, 8, A_COLS), BF),
            pltpu.VMEM((2, 8, 8, B_COLS), BF),
            pltpu.VMEM((2, 8, 8, B_COLS), BF),
            pltpu.VMEM((4, 1, 8, B_COLS), BF),
            pltpu.VMEM((4, 1, 8, B_COLS), BF),
            pltpu.SemaphoreType.DMA((N_GATHER,)),
            pltpu.SemaphoreType.DMA((N_GATHER,)),
            pltpu.SemaphoreType.DMA((N_REDUCE,)),
            pltpu.SemaphoreType.DMA((N_REDUCE,)),
        ],
        compiler_params=pltpu.CompilerParams(
            collective_id=0, has_side_effects=True, vmem_limit_bytes=60 * 1024 * 1024
        ),
    )(
        queries, cache_keys, cache_values, response_kv, segments.reshape(16, 128), residual,
        out_weight, norm_gain.reshape(1, D), up_weight, down_weight,
    )


def solution(mesh):
    return jax.shard_map(
        on_device,
        mesh=mesh,
        in_specs=(
            P(("key", "hid"), None),
            P("key", None),
            P("key", None),
            P(("key", "hid"), None),
            P(),
            P(("key", "hid"), None),
            P("hid", "key"),
            P(),
            P(None, "hid"),
            P("hid", None),
        ),
        out_specs=P(("key", "hid"), None),
        check_vma=False,
    )
```

```python
import functools
import math

import jax
import jax.numpy as jnp
from jax import lax
from jax.experimental import pallas as pl
from jax.experimental.pallas import tpu as pltpu
from jax.sharding import PartitionSpec as P

HEADS = 48
KV_HEADS = 8
HEAD = 128
GROUP = 6
D = 6144
MESH = pl.DeviceIdType.MESH
BF = jnp.bfloat16
F32 = jnp.float32

ZI = {0: 0, 1: 1, -1: 2, 2: 3, -2: 4, 3: 5, -3: 6, 4: 7}
YI = {0: 0, 1: 1, -1: 2, 2: 3}
ZGROUPS = (pl.ds(0, 1), pl.ds(1, 2), pl.ds(3, 2), pl.ds(5, 2), pl.ds(7, 1))

A_COLS = 2304
B_COLS = D - A_COLS
CA, A0, A1 = pl.ds(0, A_COLS), pl.ds(0, A_COLS // 2), pl.ds(A_COLS // 2, A_COLS // 2)
CB = pl.ds(A_COLS, B_COLS)
B0, B1 = pl.ds(A_COLS, B_COLS // 2), pl.ds(A_COLS + B_COLS // 2, B_COLS // 2)
LB, L0, L1 = pl.ds(0, B_COLS), pl.ds(0, B_COLS // 2), pl.ds(B_COLS // 2, B_COLS // 2)
N_GATHER = 56
N_REDUCE = 56


class Copies:
    def __init__(self, send_sems, recv_sems):
        self.sems = send_sems, recv_sems
        self.made = []
        self.finished = 0

    def send(self, src, dst, device):
        i = len(self.made)
        copy = pltpu.make_async_remote_copy(
            src_ref=src,
            dst_ref=dst,
            send_sem=self.sems[0].at[i],
            recv_sem=self.sems[1].at[i],
            device_id=device,
            device_id_type=MESH,
        )
        copy.start()
        self.made.append(copy)
        return copy

    def finish(self, but=0):
        last = len(self.made) - but
        for copy in self.made[self.finished : last]:
            copy.wait_send()
        self.finished = max(self.finished, last)


def where_am_i():
    key = lax.axis_index("key")
    hid = lax.axis_index("hid")
    return key // 2, key % 2, hid // 4, hid % 4


def device(x, core, z, y):
    return (lax.rem(x, 4) * 2 + core, lax.rem(z, 8) * 4 + lax.rem(y, 4))


def greet(devices):
    barrier = pltpu.get_barrier_semaphore()
    for one in devices:
        pl.semaphore_signal(barrier, inc=1, device_id=one, device_id_type=MESH)
    return lambda: pl.semaphore_wait(barrier, len(devices))


def add_into(dst, *srcs):
    total = dst[...].astype(F32)
    for src in srcs:
        total = total + src[...].astype(F32)
    dst[...] = total.astype(BF)


GATHER_ORDER = (
    "ay1", "bz1", "by10", "ay2", "bz2", "az10", "az11", "by11", "az12", "by20", "bz3", "by12",
    "bz4", "az20", "by21", "az21", "az22", "by13", "az30", "by22", "az31", "by14", "az32", "up",
    "az40", "by23", "az41", "by24", "az42",
)
REDUCE_ORDER = (
    "az42", "by04", "az41", "az40", "by03", "by02", "az32", "by01", "az31", "by00", "az30", "by14",
    "az22", "by13", "az21", "az20", "by12", "bz4", "az12", "bz3", "by11", "az11", "by10", "az10",
    "ay0", "bz2", "ay1", "bz1",
)
BZ_NEEDS = {4: ("by14",), 3: ("by13",), 2: ("by12", "bz3", "bz4"), 1: ("by11",)}
PIECES = (pl.ds(0, 1), pl.ds(1, 2), pl.ds(3, 1))


def ffn_phase(
    where, before, mid_ref, gain_ref, load_up, load_down, out_ref,
    up_w, down_w, rows, part, acc, act,
    a_zp, a_zm, a_yp, a_ym, b_yp, b_ym, b_zp, b_zm,
    g_send, g_recv, r_send, r_recv,
):
    x, core, z, y = where
    zp, zm = device(x, core, z + 1, y), device(x, core, z + 7, y)
    yp, ym = device(x, core, z, y + 1), device(x, core, z, y + 3)
    zp2, zm2 = device(x, core, z + 2, y), device(x, core, z + 6, y)

    wide = mid_ref[...].astype(F32)
    mean = jnp.mean(wide, axis=-1, keepdims=True)
    centred = wide - mean
    var = jnp.mean(centred * centred, axis=-1, keepdims=True)
    rows[0, 0] = (centred * lax.rsqrt(var + 1e-05) * gain_ref[...]).astype(BF)

    net = Copies(g_send, g_recv)
    flying = {}

    def z_hop(hop, ys, cols, half0, half1):
        if hop == 4:
            return (
                net.send(rows.at[ZI[-3], ys, :, half0], rows.at[ZI[4], ys, :, half0], zp),
                net.send(rows.at[ZI[3], ys, :, half1], rows.at[ZI[4], ys, :, half1], zm),
            )
        return (
            net.send(rows.at[ZI[1 - hop], ys, :, cols], rows.at[ZI[-hop], ys, :, cols], zp),
            net.send(rows.at[ZI[hop - 1], ys, :, cols], rows.at[ZI[hop], ys, :, cols], zm),
        )

    def y_first(zs, cols):
        return (
            net.send(rows.at[zs, 0, :, cols], rows.at[zs, YI[-1], :, cols], yp),
            net.send(rows.at[zs, 0, :, cols], rows.at[zs, YI[1], :, cols], ym),
        )

    def y_second(zs, half0, half1):
        return (
            net.send(rows.at[zs, YI[-1], :, half0], rows.at[zs, YI[2], :, half0], yp),
            net.send(rows.at[zs, YI[1], :, half1], rows.at[zs, YI[2], :, half1], ym),
        )

    def az_hop(hop, piece):
        flying["az%d%d" % (hop, piece)] = z_hop(hop, PIECES[piece], CA, A0, A1)

    def bz_hop(hop):
        if hop == 1:
            pair = z_hop(1, 0, CB, B0, B1)
        elif hop == 2:
            pair = (
                net.send(rows.at[0, 0, :, CB], rows.at[ZI[-2], 0, :, CB], zp2),
                net.send(rows.at[0, 0, :, CB], rows.at[ZI[2], 0, :, CB], zm2),
            )
        elif hop == 3:
            pair = z_hop(3, 0, CB, B0, B1)
        else:
            pair = (
                net.send(rows.at[ZI[-2], 0, :, B0], rows.at[ZI[4], 0, :, B0], zp2),
                net.send(rows.at[ZI[2], 0, :, B1], rows.at[ZI[4], 0, :, B1], zm2),
            )
        flying["bz%d" % hop] = pair

    def up_cols(first, size, fresh, low, high):
        cols = pl.ds(first, size)
        count = (high - low) * 32
        block = rows[low:high, :, :, cols].astype(F32).reshape(count, size).astype(BF)
        product = jnp.dot(block, up_w[cols, :], preferred_element_type=F32)
        if fresh:
            acc[low * 32 : high * 32] = product
        else:
            acc[low * 32 : high * 32] += product

    def up_rows(low, high):
        for i in range(2):
            up_cols(i * (A_COLS // 2), A_COLS // 2, i == 0, low, high)
        for i in range(2):
            up_cols(A_COLS + i * (B_COLS // 2), B_COLS // 2, False, low, high)

    own = pl.ds(0, 1)
    flying["ay1"] = y_first(own, CA)
    bz_hop(1)
    bz_hop(2)
    flying["by10"] = y_first(ZGROUPS[0], CB)
    az_hop(1, 0)
    before.finish()
    for name in GATHER_ORDER:
        if name == "up":
            load_up.wait()
            up_rows(0, 5)
            continue
        for copy in flying[name]:
            copy.wait_recv()
        kind, step = name[:2], int(name[2])
        if kind == "ay" and step == 1:
            flying["ay2"] = y_second(own, A0, A1)
            az_hop(1, 1)
        elif kind == "ay":
            az_hop(1, 2)
        elif kind == "az" and step < 4:
            az_hop(step + 1, int(name[3]))
        elif kind == "bz":
            if step == 2:
                bz_hop(3)
                bz_hop(4)
            flying["by1%d" % step] = y_first(ZGROUPS[step], CB)
        elif kind == "by" and step == 1:
            flying["by2" + name[3]] = y_second(ZGROUPS[int(name[3])], B0, B1)

    up_rows(5, 8)
    up = jnp.maximum(acc[...], 0.0)
    act[...] = (up * up).astype(BF)
    load_down.wait()

    def down_cols(first, size):
        cols = pl.ds(first, size)
        block = jnp.dot(act[...], down_w[:, cols], preferred_element_type=F32)
        part[:, :, :, cols] = block.reshape(8, 4, 8, size).astype(BF)

    gather = net
    net = Copies(r_send, r_recv)
    flying = {}
    done = set()

    def z_send(d, ys, cols, half0, half1, lcols, lh0, lh1, got_p, got_m, lys):
        if d == 4:
            return (
                net.send(part.at[ZI[4], ys, :, half1], got_p.at[3, lys, :, lh1], zp),
                net.send(part.at[ZI[4], ys, :, half0], got_m.at[3, lys, :, lh0], zm),
            )
        return (
            net.send(part.at[ZI[d], ys, :, cols], got_p.at[d - 1, lys, :, lcols], zp),
            net.send(part.at[ZI[-d], ys, :, cols], got_m.at[d - 1, lys, :, lcols], zm),
        )

    def z_add(d, ys, cols, half0, half1, lcols, lh0, lh1, got_p, got_m, lys):
        if d == 3:
            add_into(part.at[ZI[3], ys, :, half1], got_p.at[3, lys, :, lh1])
            add_into(part.at[ZI[-3], ys, :, half0], got_m.at[3, lys, :, lh0])
        elif d > 0:
            add_into(part.at[ZI[d], ys, :, cols], got_p.at[d, lys, :, lcols])
            add_into(part.at[ZI[-d], ys, :, cols], got_m.at[d, lys, :, lcols])
        else:
            add_into(
                part.at[0, ys, :, cols], got_p.at[0, lys, :, lcols], got_m.at[0, lys, :, lcols]
            )

    def y_send(step, zs, cols, half0, half1, lcols, lh0, lh1, got_p, got_m):
        if step == 0:
            return (
                net.send(part.at[zs, YI[2], :, half1], got_p.at[1, zs, :, lh1], yp),
                net.send(part.at[zs, YI[2], :, half0], got_m.at[1, zs, :, lh0], ym),
            )
        return (
            net.send(part.at[zs, YI[1], :, cols], got_p.at[0, zs, :, lcols], yp),
            net.send(part.at[zs, YI[-1], :, cols], got_m.at[0, zs, :, lcols], ym),
        )

    def y_add(step, zs, cols, half0, half1, lcols, lh0, lh1, got_p, got_m):
        if step == 0:
            add_into(part.at[zs, YI[1], :, half1], got_p.at[1, zs, :, lh1])
            add_into(part.at[zs, YI[-1], :, half0], got_m.at[1, zs, :, lh0])
        else:
            add_into(part.at[zs, 0, :, cols], got_p.at[0, zs, :, lcols], got_m.at[0, zs, :, lcols])

    za = [(p, CA, A0, A1, CA, A0, A1, a_zp, a_zm, p) for p in PIECES]

    def bz_send(d):
        slot, ahead, behind = {1: (0, zp, zm), 2: (2, zp2, zm2), 3: (1, zp, zm), 4: (3, zp2, zm2)}[d]
        if d == 4:
            return (
                net.send(part.at[ZI[4], 0, :, B1], b_zp.at[slot, 0, :, L1], ahead),
                net.send(part.at[ZI[4], 0, :, B0], b_zm.at[slot, 0, :, L0], behind),
            )
        return (
            net.send(part.at[ZI[d], 0, :, CB], b_zp.at[slot, 0], ahead),
            net.send(part.at[ZI[-d], 0, :, CB], b_zm.at[slot, 0], behind),
        )

    def bz_add(d):
        if d == 4:
            add_into(part.at[ZI[2], 0, :, B1], b_zp.at[3, 0, :, L1])
            add_into(part.at[ZI[-2], 0, :, B0], b_zm.at[3, 0, :, L0])
        elif d == 3:
            add_into(part.at[ZI[2], 0, :, CB], b_zp.at[1, 0])
            add_into(part.at[ZI[-2], 0, :, CB], b_zm.at[1, 0])

    yb = (CB, B0, B1, LB, L0, L1, b_yp, b_ym)
    ya = (CA, A0, A1, CA, A0, A1, a_yp, a_ym)

    down_cols(0, A_COLS // 2)
    behind = {
        p: net.send(part.at[ZI[4], PIECES[p], :, A0], a_zm.at[3, PIECES[p], :, A0], zm)
        for p in (2, 1, 0)
    }
    down_cols(A_COLS // 2, A_COLS // 2)
    for p in (2, 1, 0):
        ahead = net.send(part.at[ZI[4], PIECES[p], :, A1], a_zp.at[3, PIECES[p], :, A1], zp)
        flying["az4%d" % p] = ahead, behind[p]
    down_cols(A_COLS, B_COLS // 2)
    behind = {
        g: net.send(part.at[ZGROUPS[g], YI[2], :, B0], b_ym.at[1, ZGROUPS[g], :, L0], ym)
        for g in (4, 3, 2, 1, 0)
    }
    down_cols(A_COLS + B_COLS // 2, B_COLS // 2)
    for g in (4, 3, 2, 1, 0):
        ahead = net.send(part.at[ZGROUPS[g], YI[2], :, B1], b_yp.at[1, ZGROUPS[g], :, L1], yp)
        flying["by0%d" % g] = ahead, behind[g]
    gather.finish()
    for name in REDUCE_ORDER:
        for copy in flying[name]:
            copy.wait_recv()
        done.add(name)
        kind, step = name[:2], int(name[2])
        if kind == "az":
            p = int(name[3])
            z_add(step - 1, *za[p])
            if step > 1:
                flying["az%d%d" % (step - 1, p)] = z_send(step - 1, *za[p])
            elif p == 2:
                flying["ay0"] = y_send(0, own, *ya)
        elif kind == "by" and step == 0:
            y_add(0, ZGROUPS[int(name[3])], *yb)
            flying["by1" + name[3]] = y_send(1, ZGROUPS[int(name[3])], *yb)
        elif kind == "by":
            y_add(1, ZGROUPS[int(name[3])], *yb)
        elif kind == "bz":
            bz_add(step)
        elif kind == "ay" and step == 0:
            y_add(0, own, *ya)
        for d, needs in BZ_NEEDS.items():
            if "bz%d" % d not in flying and done.issuperset(needs):
                flying["bz%d" % d] = bz_send(d)
        if name in ("by14", "by12", "az10"):
            net.finish(16)
        if "ay1" not in flying and "ay0" in done and "az11" in done:
            flying["ay1"] = y_send(1, own, *ya)
        if name == "ay1":
            out_ref[:, CA] = (
                mid_ref[:, CA].astype(F32)
                + part[0, 0, :, CA].astype(F32)
                + a_yp[0, 0].astype(F32)
                + a_ym[0, 0].astype(F32)
            ).astype(BF)
        if name == "bz1":
            out_ref[:, CB] = (
                mid_ref[:, CB].astype(F32)
                + part[0, 0, :, CB].astype(F32)
                + b_zp[0, 0].astype(F32)
                + b_zm[0, 0].astype(F32)
                + b_zp[2, 0].astype(F32)
                + b_zm[2, 0].astype(F32)
            ).astype(BF)
    net.finish()


LOG2_SCALE = math.log2(math.e) / math.sqrt(HEAD)
Q_COLS = GROUP * HEAD
KEYS_OWN = 768
KEYS_CHIP = 2 * KEYS_OWN
RESP = 512
N_CHIP = 1536


def layer_kernel(
    q_hbm, ck_hbm, cv_hbm, rkv_hbm, seg_hbm, res_hbm, wo_hbm, gain_hbm, up_hbm, down_hbm, out_ref,
    q_ref, rkv_ref, seg_ref, res_ref, gain_ref, mid_ref, up_w, down_w,
    packed, got, qcat, osum, qall, rkv, kbuf, vbuf, wo, obuf, stat, robuf, rstat, attn, part, zp_buf, zm_buf,
    px, local_sem, s_sem, r_sem, *ffn_refs,
):
    x, core, z, y = where_am_i()
    sib = device(x, 1 - core, z, y)
    zdev = [device(x, core, z + d, y) for d in range(8)]
    xdev = [device(x + d, core, z, y) for d in range(4)]
    ydev = [device(x, core, z, y + d) for d in range(4)]
    ysib = [device(x, 1 - core, z, y + d) for d in range(4)]
    all_here = greet([*zdev[1:], *xdev[1:], *ydev[1:], *ysib])
    head = pl.ds(pl.multiple_of(z * HEAD, HEAD), HEAD)
    wo_rows = pl.ds(pl.multiple_of(y * 192, 64), 192)
    wo_own = pl.ds(pl.multiple_of(core * 768, 128), 768)

    loads = [
        pltpu.make_async_copy(src, dst, local_sem.at[3 + i])
        for i, (src, dst) in enumerate(
            (
                (q_hbm, q_ref),
                (rkv_hbm, rkv_ref),
                (seg_hbm, seg_ref),
                (res_hbm, res_ref),
                (gain_hbm, gain_ref),
                (up_hbm, up_w),
                (down_hbm, down_w),
            )
        )
    ]
    load_q, load_rkv, load_seg, load_res, load_gain, load_up, load_down = loads
    load_q.start()
    load_rkv.start()
    load_k = pltpu.make_async_copy(ck_hbm.at[:, head], kbuf.at[pl.ds(0, KEYS_OWN)], local_sem.at[0])
    load_v = pltpu.make_async_copy(
        cv_hbm.at[:, head], vbuf.at[pl.ds(0, KEYS_OWN), pl.ds(0, HEAD)], local_sem.at[1]
    )
    load_wo = pltpu.make_async_copy(wo_hbm, wo.at[wo_rows, wo_own], local_sem.at[2])
    load_k.start()
    load_v.start()
    load_wo.start()
    for load in (load_seg, load_res, load_gain):
        load.start()
    load_q.wait()
    load_rkv.wait()
    for i in range(8):
        packed[i, :, 0:Q_COLS] = q_ref[:, i * Q_COLS : (i + 1) * Q_COLS]
        packed[i, :, Q_COLS : Q_COLS + HEAD] = rkv_ref[:, i * HEAD : (i + 1) * HEAD]
        packed[i, :, Q_COLS + HEAD :] = rkv_ref[:, 1024 + i * HEAD : 1024 + (i + 1) * HEAD]
    all_here()
    net = Copies(s_sem, r_sem)

    def arrived(copies):
        for copy in copies:
            copy.wait_recv()

    moves = [
        net.send(packed.at[lax.rem(z + d, 8)], got.at[8 - d], zdev[d]) for d in (4, 3, 5, 2, 6, 1, 7)
    ]
    caches = [
        net.send(ck_hbm.at[:, head], kbuf.at[pl.ds(KEYS_OWN, KEYS_OWN)], sib),
        net.send(cv_hbm.at[:, head], vbuf.at[pl.ds(KEYS_OWN, KEYS_OWN), pl.ds(0, HEAD)], sib),
    ]
    got[0] = packed[z]
    vbuf[:, HEAD:] = jnp.ones((KEYS_CHIP + RESP, HEAD), BF)
    arrived(moves)
    rkv[0, 0] = got[:, :, Q_COLS:]
    kv_moves = [net.send(rkv.at[0, 0], rkv.at[0, 4 - d], ydev[d]) for d in (2, 1, 3)]
    kv_moves += [net.send(rkv.at[0, 0], rkv.at[1, (4 - d) % 4], ysib[d]) for d in (2, 1, 3, 0)]
    qall[0] = got[:, :, 0:Q_COLS]
    q_moves = [net.send(qall.at[0], qall.at[4 - d], xdev[d]) for d in (1, 3, 2)]

    load_seg.wait()
    seg = seg_ref[...]
    bounds = [
        jnp.sum(jnp.where(seg < s, 1, 0), keepdims=True) for s in (1, 2, 3)
    ]
    lanes = lax.broadcasted_iota(jnp.int32, (1, RESP), 1)
    key_row = (
        (2 * x + ((core + lanes // 256) & 1)) * 32
        + ((z + (lanes // 8)) & 7) * 4
        + ((y + (lanes // 64)) & 3)
    ) * 8 + (lanes & 7)
    slots = lax.broadcasted_iota(jnp.int32, (64, 1), 0)

    load_up.start()
    load_down.start()
    nt = (((1,), (1,)), ((), ()))
    lane = lax.broadcasted_iota(jnp.int32, (64, HEAD), 1)
    wide_lane = lax.broadcasted_iota(jnp.int32, (GROUP * 64, HEAD), 1)

    def attend_cache(i):
        wide = qall[i].astype(F32)
        q = jnp.concatenate(
            [wide[:, :, j * HEAD : (j + 1) * HEAD].reshape(64, HEAD) for j in range(GROUP)], 0
        ).astype(BF)
        qcat[i] = q
        score = lax.dot_general(q, kbuf[0:KEYS_CHIP, :], nt, preferred_element_type=F32)
        top = jnp.max(score, axis=-1, keepdims=True)
        weight = jnp.exp2((score - top) * LOG2_SCALE).astype(BF)
        mixed = jnp.dot(weight, vbuf[0:KEYS_CHIP, :], preferred_element_type=F32)
        osum[i, :, 0:HEAD] = mixed[:, 0:HEAD]
        osum[i, :, HEAD:] = jnp.where(wide_lane < 64, mixed[:, HEAD:], top)

    def attend_response(i):
        q_row = ((2 * ((x + i) & 3) + core) * 32 + ((z + slots // 8) & 7) * 4 + y) * 8 + (slots & 7)
        start = jnp.zeros_like(q_row)
        for bound in bounds:
            start = jnp.maximum(start, jnp.where(q_row >= bound, bound, 0))
        seen = (key_row <= q_row) & (key_row >= start)
        seen = jnp.concatenate([jnp.where(seen, 0.0, -jnp.inf)] * GROUP, 0)
        score = lax.dot_general(qcat[i], kbuf[KEYS_CHIP:, :], nt, preferred_element_type=F32) + seen
        first_top = osum[i, :, 2 * HEAD - 1 : 2 * HEAD]
        top = jnp.maximum(first_top, jnp.max(score, axis=-1, keepdims=True))
        weight = jnp.exp2((score - top) * LOG2_SCALE).astype(BF)
        mixed = osum[i] * jnp.exp2((first_top - top) * LOG2_SCALE) + jnp.dot(
            weight, vbuf[KEYS_CHIP:, :], preferred_element_type=F32
        )
        both = jnp.ones((64, HEAD), F32)
        for j in range(GROUP):
            rows = slice(j * 64, (j + 1) * 64)
            obuf[i, :, :, j * HEAD : (j + 1) * HEAD] = mixed[rows, 0:HEAD].reshape(8, 8, HEAD).astype(BF)
            both = jnp.where((lane & 31) == j, top[rows], both)
            both = jnp.where((lane & 31) == 8 + j, mixed[rows, HEAD : HEAD + 1], both)
        for g in range(4):
            quarter = both[g * 16 : (g + 1) * 16]
            packed_stat = quarter if g == 0 else jnp.where(lane[0:16] >= 32 * g, quarter, packed_stat)
        stat[i] = packed_stat

    o_moves = []

    def give(d):
        attend_response(d)
        o_moves.append(net.send(obuf.at[d], robuf.at[4 - d], xdev[d]))
        o_moves.append(net.send(stat.at[d], rstat.at[4 - d], xdev[d]))

    load_k.wait()
    load_v.wait()
    arrived(caches)
    attend_cache(0)
    load_wo.wait()
    own_wo = wo.at[wo_rows, wo_own]
    wo_moves = [net.send(own_wo, own_wo, ydev[d]) for d in (1, 3)]
    arrived([q_moves[2]])
    attend_cache(2)
    arrived(kv_moves)
    kbuf[pl.ds(KEYS_CHIP, RESP), :] = rkv[:, :, :, :, 0:HEAD].astype(F32).reshape(RESP, HEAD).astype(BF)
    vbuf[pl.ds(KEYS_CHIP, RESP), 0:HEAD] = (
        rkv[:, :, :, :, HEAD:].astype(F32).reshape(RESP, HEAD).astype(BF)
    )
    give(2)
    arrived([q_moves[0]])
    attend_cache(3)
    give(3)
    arrived([q_moves[1]])
    attend_cache(1)
    give(1)
    arrived(wo_moves)
    back, ahead = lax.rem(y + 3, 4), lax.rem(y + 1, 4)
    low = wo.at[pl.ds(pl.multiple_of(back * 192, 64), 96), wo_own]
    high = wo.at[pl.ds(pl.multiple_of(ahead * 192 + 96, 32), 96), wo_own]
    wo_moves = [net.send(low, low, ydev[1]), net.send(high, high, ydev[3])]
    attend_response(0)
    arrived(wo_moves)
    wo_cols = wo.at[:, wo_own]
    wo_sib = net.send(wo_cols, wo_cols, sib)
    arrived(o_moves)

    def unpacked(tile, shift):
        parts = [(tile, (HEAD - 32 * g - shift) % HEAD) for g in range(4)]
        return jnp.concatenate([pltpu.roll(t, by, 1) if by else t for t, by in parts], 0)

    tiles = [stat[0]] + [rstat[i] for i in range(1, 4)]
    tops = [unpacked(t, 0) for t in tiles]
    totals = [unpacked(t, 8) for t in tiles]
    top = functools.reduce(jnp.maximum, tops)
    scales = [jnp.exp2((t - top) * LOG2_SCALE) for t in tops]
    total = functools.reduce(jnp.add, [a * b for a, b in zip(scales, totals)])
    scales = [a / total for a in scales]
    for j in range(GROUP):
        cols = slice(j * HEAD, (j + 1) * HEAD)
        mixed = obuf[0, :, :, cols].astype(F32).reshape(64, HEAD) * scales[0][:, j : j + 1]
        for i in range(1, 4):
            mixed = mixed + robuf[i, :, :, cols].astype(F32).reshape(64, HEAD) * scales[i][:, j : j + 1]
        attn[0, :, :, cols] = mixed.reshape(8, 8, HEAD).astype(BF)
    a_moves = [net.send(attn.at[0], attn.at[4 - d], xdev[d]) for d in (2, 1, 3)]
    arrived([wo_sib])
    ring = {}

    far0, far1 = slice(0, 768), slice(768, N_CHIP)

    def project(*slots):
        count = 64 * len(slots)
        lhs = jnp.concatenate([attn[i].astype(F32).reshape(64, Q_COLS) for i in slots], 0).astype(BF)
        for p in range(2):
            cols = slice(p * 768, (p + 1) * 768)
            block = jnp.dot(lhs, wo[:, cols], preferred_element_type=F32)
            for k, i in enumerate(slots):
                part[:, i, :, cols] = block[k * 64 : (k + 1) * 64].reshape(8, 8, 768).astype(BF)
        for i in slots:
            ring[i] = [
                net.send(part.at[4, i, :, far1], zp_buf.at[3, i, :, far1], zdev[2]),
                net.send(part.at[4, i, :, far0], zm_buf.at[3, i, :, far0], zdev[6]),
                net.send(part.at[3, i], zp_buf.at[1, i], zdev[1]),
                net.send(part.at[5, i], zm_buf.at[1, i], zdev[7]),
            ]

    def relay(i):
        arrived(ring[i])
        add_into(part.at[2, i], zp_buf.at[1, i])
        add_into(part.at[2, i, :, far1], zp_buf.at[3, i, :, far1])
        add_into(part.at[6, i], zm_buf.at[1, i])
        add_into(part.at[6, i, :, far0], zm_buf.at[3, i, :, far0])
        ring[i] = [
            net.send(part.at[2, i], zp_buf.at[2, i], zdev[2]),
            net.send(part.at[6, i], zm_buf.at[2, i], zdev[6]),
            net.send(part.at[1, i], zp_buf.at[0, i], zdev[1]),
            net.send(part.at[7, i], zm_buf.at[0, i], zdev[7]),
        ]

    p_moves = []

    def settle(i):
        arrived(ring[i])
        add_into(
            part.at[0, i], zp_buf.at[0, i], zm_buf.at[0, i], zp_buf.at[2, i], zm_buf.at[2, i]
        )
        if i > 0:
            p_moves.append(net.send(part.at[0, i], px.at[4 - i], xdev[i]))

    project(0)
    arrived([a_moves[1], a_moves[2]])
    project(1, 3)
    relay(0)
    arrived([a_moves[0]])
    project(2)
    relay(1)
    relay(3)
    relay(2)
    settle(0)
    settle(1)
    settle(3)
    settle(2)
    px[0] = part[0, 0]
    load_res.wait()
    load_gain.wait()
    arrived(p_moves)
    for i in range(4):
        cols = pl.ds(pl.multiple_of(((x + i) & 3) * N_CHIP, HEAD), N_CHIP)
        mid_ref[:, cols] = (res_ref[:, cols].astype(F32) + px[i].astype(F32)).astype(BF)
    ffn_phase(
        (x, core, z, y), net, mid_ref, gain_ref, load_up, load_down, out_ref, up_w, down_w, *ffn_refs
    )


def on_device(
    queries,
    cache_keys,
    cache_values,
    response_kv,
    segments,
    residual,
    out_weight,
    norm_gain,
    up_weight,
    down_weight,
):
    hbm = pl.BlockSpec(memory_space=pl.ANY)
    hidden = up_weight.shape[1]
    return pl.pallas_call(
        layer_kernel,
        name="layer",
        out_shape=jax.ShapeDtypeStruct(residual.shape, BF),
        in_specs=[hbm] * 10,
        out_specs=pl.BlockSpec(memory_space=pltpu.VMEM),
        scratch_shapes=[
            pltpu.VMEM(queries.shape, BF),
            pltpu.VMEM(response_kv.shape, BF),
            pltpu.VMEM((16, 128), jnp.int32),
            pltpu.VMEM(residual.shape, BF),
            pltpu.VMEM((1, D), F32),
            pltpu.VMEM(residual.shape, BF),
            pltpu.VMEM((D, hidden), BF),
            pltpu.VMEM((hidden, D), BF),
            pltpu.VMEM((8, 8, 1024), BF),
            pltpu.VMEM((8, 8, 1024), BF),
            pltpu.VMEM((4, GROUP * 64, HEAD), BF),
            pltpu.VMEM((4, GROUP * 64, 2 * HEAD), F32),
            pltpu.VMEM((4, 8, 8, Q_COLS), BF),
            pltpu.VMEM((2, 4, 8, 8, 2 * HEAD), BF),
            pltpu.VMEM((KEYS_CHIP + RESP, HEAD), BF),
            pltpu.VMEM((KEYS_CHIP + RESP, 2 * HEAD), BF),
            pltpu.VMEM((Q_COLS, N_CHIP), BF),
            pltpu.VMEM((4, 8, 8, Q_COLS), BF),
            pltpu.VMEM((4, 16, HEAD), F32),
            pltpu.VMEM((4, 8, 8, Q_COLS), BF),
            pltpu.VMEM((4, 16, HEAD), F32),
            pltpu.VMEM((4, 8, 8, Q_COLS), BF),
            pltpu.VMEM((8, 4, 8, N_CHIP), BF),
            pltpu.VMEM((4, 4, 8, N_CHIP), BF),
            pltpu.VMEM((4, 4, 8, N_CHIP), BF),
            pltpu.VMEM((4, 8, N_CHIP), BF),
            pltpu.SemaphoreType.DMA((10,)),
            pltpu.SemaphoreType.DMA((72,)),
            pltpu.SemaphoreType.DMA((72,)),
            pltpu.VMEM((8, 4, 8, D), BF),
            pltpu.VMEM((8, 4, 8, D), BF),
            pltpu.VMEM((256, hidden), F32),
            pltpu.VMEM((256, hidden), BF),
            pltpu.VMEM((4, 4, 8, A_COLS), BF),
            pltpu.VMEM((4, 4, 8, A_COLS), BF),
            pltpu.VMEM((2, 1, 8, A_COLS), BF),
            pltpu.VMEM((2, 1, 8, A_COLS), BF),
            pltpu.VMEM((2, 8, 8, B_COLS), BF),
            pltpu.VMEM((2, 8, 8, B_COLS), BF),
            pltpu.VMEM((4, 1, 8, B_COLS), BF),
            pltpu.VMEM((4, 1, 8, B_COLS), BF),
            pltpu.SemaphoreType.DMA((N_GATHER,)),
            pltpu.SemaphoreType.DMA((N_GATHER,)),
            pltpu.SemaphoreType.DMA((N_REDUCE,)),
            pltpu.SemaphoreType.DMA((N_REDUCE,)),
        ],
        compiler_params=pltpu.CompilerParams(
            collective_id=0, has_side_effects=True, vmem_limit_bytes=60 * 1024 * 1024
        ),
    )(
        queries, cache_keys, cache_values, response_kv, segments.reshape(16, 128), residual,
        out_weight, norm_gain.reshape(1, D), up_weight, down_weight,
    )


def solution(mesh):
    return jax.shard_map(
        on_device,
        mesh=mesh,
        in_specs=(
            P(("key", "hid"), None),
            P("key", None),
            P("key", None),
            P(("key", "hid"), None),
            P(),
            P(("key", "hid"), None),
            P("hid", "key"),
            P(),
            P(None, "hid"),
            P("hid", None),
        ),
        out_specs=P(("key", "hid"), None),
        check_vma=False,
    )
```
